32 devices in a mesh: seq: 32 (over z, y, x, core).
Axes of the slice: x: 2, y: 2, z: 4, core: 2. Of those that a mesh axis runs over, the one named last changes fastest.
Arguments:
- hidden: bfloat16 [16384, 1472], P('seq'), may hold values from -6 to 6
- segments: int32 [16384], P('seq'), may hold values from 0 to 63, never falling along the last dimension, each value on 1 to 1024 neighbouring positions
- delete_mask: bfloat16 [16384], P('seq'), may hold values from -4 to 0
- bucket_table: int32 [2047], replicated, may hold values from 0 to 31
- attn_weight: bfloat16 [1472, 1536], P(None, 'seq'), may hold values from -1.1 to 1.1
- gate_weight: bfloat16 [1472, 3584], P(None, 'seq'), may hold values from -0.15625 to 0.15625
- up_weight: bfloat16 [1472, 3584], P(None, 'seq'), may hold values from -0.15625 to 0.15625
- down_weight: bfloat16 [3584, 1472], P('seq'), may hold values from -0.09375 to 0.09375
- norm_attn: float32 [1472], replicated, may hold values from 0.5 to 1.5
- norm_ffn: float32 [1472], replicated, may hold values from 0.5 to 1.5
- rel_bias: float32 [32, 6], replicated, may hold values from -4 to 4
- out_grad: bfloat16 [16384, 1472], P('seq'), may hold values from -6 to 6
Outputs:
- output: bfloat16 [16384, 1472], P('seq')
- d_hidden: float32 [16384, 1472], P('seq')
- d_attn_weight: float32 [1472, 1536], P(None, 'seq')
- d_gate_weight: float32 [1472, 3584], P(None, 'seq')
- d_up_weight: float32 [1472, 3584], P(None, 'seq')
- d_down_weight: float32 [3584, 1472], P('seq')
- d_norm_attn: float32 [1472], replicated
- d_norm_ffn: float32 [1472], replicated
- d_rel_bias: float32 [32, 6], replicated
The draws below stay inside these ranges and needn't reach their ends.
Inputs may be any that keep to these rules, and one draw needn't show every extreme that they name: `segments`: tokens of one sequence are contiguous; sequence numbers never fall; each sequence holds 1 to 1024 tokens and one holds exactly 1024.
All inputs are finite; a program needn't handle non-finite values.
Results may differ from the reference program's by a relative error of at most 0.014.
The reference program's roundings to bfloat16 on the way count: a program that leaves them out, or rounds other values in their place, can miss the bound.
Values may be sent and summed in bfloat16 or wider, within the bound.
A program may use at most 320 MiB of HBM per device.

```python
import math
import jax
import jax.numpy as jnp
import numpy as np
from jax import lax

D = 1472
HEADS = 6
HEAD_DIM = 64
FF = 3584
BUCKETS = 32
MAXLEN = 1024
TOK_DEV = 512
INNER = 384
TOKENS = 16384
SEGS = 64
N_SEQ = 32


def draw_attn_weight(key, part):
    key = jax.random.fold_in(key, 11)
    base = jnp.clip(jax.random.normal(key, (D, 4 * INNER), jnp.float32), -5.0, 5.0)
    column = jnp.arange(4 * INNER)
    factor = jnp.where(column < 2 * INNER, 0.5 * D ** (-0.5), jnp.where(column < 3 * INNER, D ** (-0.5), 4.0 * INNER ** (-0.5)))
    return jnp.clip(base * factor, -1.09, 1.09).astype(jnp.bfloat16)


def place_ends(drawn, stream_key, least, high):
    longest = drawn.shape.index(max(drawn.shape))
    spots = []
    for shift in (0, 1):
        where = [jax.random.randint(jax.random.fold_in(stream_key, axis), (), 0, length) for axis, length in enumerate(drawn.shape)]
        where[longest] = (where[longest] + shift) % drawn.shape[longest]
        spots.append(tuple(where))
    return drawn.at[spots[0]].set(least).at[spots[1]].set(high)


def steps_of(stream_key, dims, cuts, least, top_value):
    factor_of = 1.0
    for axis_at, parts in cuts:
        heights = jax.random.uniform(jax.random.fold_in(jax.random.fold_in(stream_key, 6), axis_at), (parts,), jnp.float32, least / len(cuts), top_value / len(cuts))
        factor_of = factor_of * jnp.repeat(jnp.exp(heights), dims[axis_at] // parts).reshape((-1,) + (1,) * (len(dims) - 1 - axis_at))
    return factor_of


def length_profile(number_of, total, bound, skew):
    loads = [(1 << 20) // math.isqrt(standing ** skew) + 1 for standing in range(2, number_of + 1)]
    spare, given = total - bound - (number_of - 1), [1] * (number_of - 1)
    while spare > 0:
        candidates = [i for i in range(number_of - 1) if given[i] < bound]
        pool, left = sum([loads[i] for i in candidates]), spare
        for i in candidates:
            extra = min(bound - given[i], max(1, left * loads[i] // pool), spare)
            given[i] = given[i] + extra
            spare = spare - extra
    return np.array([bound] + given)


def uneven(key, amount, total, limit, skew):
    if amount == 2:
        one = jax.random.randint(key, (), max(1, total - limit), min(limit, total - 1) + 1)
        return jnp.stack([one, total - one])
    lengths = jnp.asarray(length_profile(amount, total, limit, skew), jnp.int32)
    couples = (amount - 1) // 2
    giver, taker = lengths[1:1 + 2 * couples:2], lengths[2:2 + 2 * couples:2]
    slack = jnp.minimum(giver - 1, limit - taker)
    passed = jax.random.randint(jax.random.fold_in(key, 1), (couples,), 0, 1 << 20) % (slack + 1)
    lengths = lengths.at[1:1 + 2 * couples:2].set(giver - passed).at[2:2 + 2 * couples:2].set(taker + passed)
    return lengths[jax.random.permutation(jax.random.fold_in(key, 2), amount)]


def scatter_about(stream_key, dims, spread, most, pieces=(), kind=jnp.bfloat16):
    result = spread * jax.random.normal(stream_key, dims, jnp.float32)
    if pieces:
        result = result * steps_of(stream_key, dims, pieces, -0.22, 0.18)
    return jnp.clip(result, -most, most).astype(kind)


def setup_inputs(seed: int = 0) -> dict:
    arg_keys = jax.random.split(jax.random.key(seed), 13)
    hidden = scatter_about(arg_keys[0], (TOKENS, D), 1.0, 6.0, ((0, 32),))
    segments = jnp.searchsorted(jnp.cumsum(uneven(arg_keys[1], SEGS, TOKENS, MAXLEN, 2)), jnp.arange(TOKENS), side="right").astype(jnp.int32)
    delete_mask = jnp.clip(-4.0 + 4.0 * jax.random.uniform(arg_keys[2], (TOKENS,), jnp.float32) ** steps_of(arg_keys[2], (TOKENS,), ((0, 32),), -0.2, 0.2), -4.0, 0.0).astype(jnp.bfloat16)
    bucket_table = place_ends(jax.random.randint(arg_keys[3], (2 * MAXLEN - 1,), 0, BUCKETS), jax.random.fold_in(arg_keys[3], 1), 0, BUCKETS - 1).astype(jnp.int32)
    attn_weight = draw_attn_weight(jax.random.fold_in(arg_keys[12], 71), 0)
    gate_weight = scatter_about(arg_keys[5], (D, FF), D ** -0.5, 0.15625, ((1, 32),))
    up_weight = scatter_about(arg_keys[6], (D, FF), D ** -0.5, 0.15625, ((1, 32),))
    down_weight = scatter_about(arg_keys[7], (FF, D), FF ** -0.5, 0.09375, ((0, 32),))
    norm_attn = jnp.clip(1.0 + 0.1 * jax.random.normal(arg_keys[8], (D,), jnp.float32), 0.5, 1.5)
    norm_ffn = jnp.clip(1.0 + 0.1 * jax.random.normal(arg_keys[9], (D,), jnp.float32), 0.5, 1.5)
    rel_bias = scatter_about(arg_keys[10], (BUCKETS, HEADS), 1.0, 4.0, (), jnp.float32)
    out_grad = scatter_about(arg_keys[11], (TOKENS, D), 1.0, 6.0, ((0, 32),))
    return dict(hidden=hidden, segments=segments, delete_mask=delete_mask, bucket_table=bucket_table, attn_weight=attn_weight, gate_weight=gate_weight, up_weight=up_weight, down_weight=down_weight, norm_attn=norm_attn, norm_ffn=norm_ffn, rel_bias=rel_bias, out_grad=out_grad)


@jax.custom_vjp
def low(v):
    return lax.optimization_barrier(v.astype(jnp.bfloat16)).astype(jnp.float32)

@jax.custom_vjp
def low_back(v):
    return v

def low_keep(v):
    return (low(v), None)

def low_pass(kept, grad):
    return (grad,)

def back_keep(v):
    return (v, None)

def back_low(kept, grad):
    return (low(grad),)
low.defvjp(low_keep, low_pass)
low_back.defvjp(back_keep, back_low)

def rms_norm(value, gain):
    return value * lax.rsqrt(lax.optimization_barrier(jnp.mean(value * value, axis=-1, keepdims=True)) + 1e-06) * gain

def exact_product(left, right):
    return jnp.dot(left, right, precision=lax.Precision.HIGHEST)

def layer(hidden, attn_weight, gate_weight, up_weight, down_weight, norm_attn, norm_ffn, rel_bias, segments, delete_mask, bucket_table):
    inner_width = HEADS * HEAD_DIM
    reach_blocks = (MAXLEN + TOK_DEV - 2) // TOK_DEV
    margin = reach_blocks * TOK_DEV
    window = (2 * reach_blocks + 1) * TOK_DEV
    normed = low(rms_norm(hidden, norm_attn))
    projected = exact_product(normed, attn_weight[:, :3 * inner_width])
    queries = low(low_back(projected[:, :inner_width]))
    key_rows = low(low_back(projected[:, inner_width:2 * inner_width]))
    value_rows = low(low_back(projected[:, 2 * inner_width:3 * inner_width]))
    keys_padded = jnp.pad(key_rows, ((margin, margin), (0, 0)))
    values_padded = jnp.pad(value_rows, ((margin, margin), (0, 0)))
    seg_padded = jnp.pad(segments, (margin, margin), constant_values=-1)
    mask_padded = jnp.pad(delete_mask, (margin, margin))
    by_offset = jnp.take(rel_bias, bucket_table, axis=0).T
    offset = jnp.arange(window, dtype=jnp.int32)[None, :] - margin - jnp.arange(TOK_DEV, dtype=jnp.int32)[:, None]
    offset_index = jnp.clip(offset, 1 - MAXLEN, MAXLEN - 1) + MAXLEN - 1
    pos_bias = jnp.take(by_offset, offset_index, axis=1)

    def attend(block_num):
        start = block_num * TOK_DEV
        q_rows = lax.dynamic_slice_in_dim(queries, start, TOK_DEV, 0).reshape(TOK_DEV, HEADS, HEAD_DIM)
        k_win = lax.dynamic_slice_in_dim(keys_padded, start, window, 0).reshape(window, HEADS, HEAD_DIM)
        v_win = lax.dynamic_slice_in_dim(values_padded, start, window, 0).reshape(window, HEADS, HEAD_DIM)
        seg_query = lax.dynamic_slice_in_dim(segments, start, TOK_DEV, 0)
        seg_key = lax.dynamic_slice_in_dim(seg_padded, start, window, 0)
        mask_key = lax.dynamic_slice_in_dim(mask_padded, start, window, 0)
        raw = low_back(jnp.einsum('qhd,khd->hqk', q_rows, k_win, precision=lax.Precision.HIGHEST))
        scores = raw + pos_bias + mask_key[None, None, :]
        same_doc = seg_query[:, None] == seg_key[None, :]
        scores = jnp.where(same_doc[None], scores, -1e+30)
        row_max = lax.optimization_barrier(jnp.max(scores, axis=-1, keepdims=True))
        exp_scores = jnp.exp(scores - row_max)
        softmax_weights = low(exp_scores / lax.optimization_barrier(jnp.sum(exp_scores, axis=-1, keepdims=True)))
        mixed = jnp.einsum('hqk,khd->qhd', softmax_weights, v_win, precision=lax.Precision.HIGHEST)
        return mixed.reshape(TOK_DEV, inner_width)
    mixed_all = lax.map(jax.checkpoint(attend), jnp.arange(N_SEQ, dtype=jnp.int32))
    attended = low(low_back(mixed_all.reshape(N_SEQ * TOK_DEV, inner_width)))
    branch = low_back(lax.dot_general(attended, attn_weight[:, 3 * inner_width:], (((1,), (1,)), ((), ())), precision=lax.Precision.HIGHEST))
    after = hidden + branch
    normed_ffn = low(rms_norm(after, norm_ffn))
    ffn_rows = 8 * TOK_DEV

    def feed_block(block_num):
        row_block = lax.dynamic_slice_in_dim(normed_ffn, block_num * ffn_rows, ffn_rows, 0)
        gate_act = low_back(exact_product(row_block, gate_weight))
        up_act = low_back(exact_product(row_block, up_weight))
        return exact_product(low(jax.nn.gelu(gate_act) * up_act), down_weight)
    ffn_out = lax.map(jax.checkpoint(feed_block), jnp.arange(N_SEQ // 8, dtype=jnp.int32))
    return after + ffn_out.reshape(N_SEQ * TOK_DEV, D)

def reference(hidden, segments, delete_mask, bucket_table, attn_weight, gate_weight, up_weight, down_weight, norm_attn, norm_ffn, rel_bias, out_grad):
    mask_float = delete_mask.astype(jnp.float32)

    def closed(h_in, a_in, g_in, u_in, d_in, na_in, nf_in, rb_in):
        return layer(h_in, a_in, g_in, u_in, d_in, na_in, nf_in, rb_in, segments, mask_float, bucket_table)
    output, pull = jax.vjp(closed, hidden.astype(jnp.float32), attn_weight.astype(jnp.float32), gate_weight.astype(jnp.float32), up_weight.astype(jnp.float32), down_weight.astype(jnp.float32), norm_attn.astype(jnp.float32), norm_ffn.astype(jnp.float32), rel_bias.astype(jnp.float32))
    grads = pull(out_grad.astype(jnp.float32))
    return (output.astype(jnp.bfloat16), grads[0], grads[1], grads[2], grads[3], grads[4], grads[5], grads[6], grads[7])
```

```python
import functools
import math
import jax
import jax.numpy as jnp
from jax import lax
from jax.experimental import pallas as pl
from jax.experimental.pallas import tpu as pltpu
from jax.sharding import PartitionSpec as P

MESH = pl.DeviceIdType.MESH
BF = jnp.bfloat16
F32 = jnp.float32
BIG = 1e30
GRIDS = {32: (4, 2, 2)}
ORDERS = ("xyz", "zxy", "zyx")
GROUPS = 8
STAGES = 5
PIECE = 48
EPS = 1e-06


def nt(a, b):
    return lax.dot_general(a, b, (((1,), (1,)), ((), ())), preferred_element_type=F32)


def nn(a, b):
    return jnp.dot(a, b, preferred_element_type=F32)


def column_parts(width):
    return ((0, 256), (256, 640), (896, width - 896))


def when(cond, body):
    if cond is None:
        body()
    else:
        pl.when(cond)(body)


def inside(value, count):
    return (value >= 0) & (value < count)


class Place:
    def __init__(self, n):
        self.n = n
        self.grid = GRIDS[n]
        zs, ys, xs = self.grid
        self.me = lax.axis_index("seq")
        self.c = self.me % 2
        chip = self.me // 2
        self.x = chip % xs
        self.y = (chip // xs) % ys
        self.z = chip // (xs * ys)

    def dev(self, z, y, x):
        _, ys, xs = self.grid
        return ((z * ys + y) * xs + x) * 2 + self.c

    def around(self):
        zs = self.grid[0]
        z, y, x = self.z, self.y, self.x
        out = [
            (None, self.me + 1 - 2 * self.c),
            (None, self.dev(z, y, 1 - x)),
            (None, self.dev(z, 1 - y, x)),
            (z < zs - 1, self.dev(jnp.minimum(z + 1, zs - 1), y, x)),
            (z > 0, self.dev(jnp.maximum(z - 1, 0), y, x)),
        ]
        return out

    def barrier(self, reach, far=False):
        sem = pltpu.get_barrier_semaphore()
        pairs = self.around()
        if far:
            zs = self.grid[0]
            pairs = pairs[:3] + [(None, self.dev((self.z + i) % zs, self.y, self.x)) for i in range(1, zs)]
        for by in reach:
            target = self.me + by
            pairs.append((inside(target, self.n), jnp.clip(target, 0, self.n - 1)))
        count = 0
        for cond, device in pairs:
            when(
                cond,
                lambda device=device: pl.semaphore_signal(
                    sem, inc=1, device_id=(device,), device_id_type=MESH
                ),
            )
            count = count + (1 if cond is None else cond.astype(jnp.int32))
        pl.semaphore_wait(sem, count)


def gather_stages(here, blocks, send, recv, width):
    zs, ys, xs = here.grid
    z, y, x = here.z, here.y, here.x
    parts = []
    slot = 0
    for order, (first, wide) in zip(ORDERS, column_parts(width)):
        cols = pl.ds(first, wide)
        have = set()
        stages = []
        for dim in order:
            in_y = pl.ds(0, ys) if "y" in have else pl.ds(y, 1)
            in_x = pl.ds(0, xs) if "x" in have else pl.ds(x, 1)
            if dim == "z":
                for step in range(zs - 1):
                    moves = []
                    for way in (1, -1):
                        source = z - way * step
                        sends = inside(source, zs) & inside(z + way, zs)
                        gets = inside(z - way - way * step, zs) & inside(z - way, zs)
                        in_z = pl.ds(jnp.clip(source, 0, zs - 1), 1)
                        device = here.dev(jnp.clip(z + way, 0, zs - 1), y, x)
                        moves.append((sends, gets, in_z, in_y, in_x, cols, device, slot))
                        slot += 1
                    stages.append(moves)
            else:
                in_z = pl.ds(0, zs) if "z" in have else pl.ds(z, 1)
                device = here.dev(z, y, 1 - x) if dim == "x" else here.dev(z, 1 - y, x)
                stages.append([(None, None, in_z, in_y, in_x, cols, device, slot)])
                slot += 1
            have.add(dim)
        parts.append(stages)

    def copy(move, g):
        _, _, in_z, in_y, in_x, cols, device, at = move
        ref = blocks.at[g, in_z, in_y, in_x, :, cols]
        return pltpu.make_async_remote_copy(
            ref, ref, send.at[g, at], recv.at[g, at], device_id=(device,), device_id_type=MESH
        )

    return parts, copy, slot


def gather_round(parts, copy, r, ready):
    for k in range(STAGES, -1, -1):
        g = r - k

        def step(g=g, k=k):
            if k == 0:
                ready(g)
            for stages in parts:
                if k > 0:
                    for move in stages[k - 1]:
                        when(move[1], lambda move=move: copy(move, g).wait_recv())
                if k < STAGES:
                    for move in stages[k]:
                        when(move[0], lambda move=move: copy(move, g).start())

        if isinstance(r, int):
            if 0 <= g < GROUPS:
                step()
        else:
            pl.when(inside(g, GROUPS))(step)


def gather_drain(parts, copy):
    def body(g, _):
        for stages in parts:
            for moves in stages:
                for move in moves:
                    when(move[0], lambda move=move: copy(move, g).wait_send())
        return 0

    lax.fori_loop(0, GROUPS, body, 0)


def shift_line(table, rel, head):
    line = jnp.zeros(table.shape, F32)
    for bucket in range(rel.shape[0]):
        line = jnp.where(table == bucket, rel[bucket, head], line)
    return line


def gelu_parts(v):
    root = math.sqrt(2.0 / math.pi)
    sq = v * v
    t = jnp.tanh(root * (v + 0.044715 * (sq * v)))
    half = 0.5 * (1.0 + t)
    value = v * half
    slope = half + 0.5 * v * (1.0 - t * t) * (root * (1.0 + 3 * 0.044715 * sq))
    return value, slope


def row_norm(v):
    return lax.rsqrt(jnp.mean(v * v, axis=-1, keepdims=True) + EPS)


REACH = (1, -1, 2, -2)


def forward_kernel(
    n, heads,
    slab, hid, dy, kx_own, qx, table, rel, na, nf,
    o_grads, o_outp, o_dn2p, o_x1, o_at, o_q, o_kv, o_kx, o_lse, o_ga,
    G, ga, n2f, dyf, kv, kx, qv, x1, at, lse,
    gs, gr, lsem, hs, hr, ks, kr, cs, cr, osem, stsem,
):
    here = Place(n)
    c = here.c
    rows, D = hid.shape
    inner = qv.shape[1]
    nz = here.grid[0]
    partner = here.me + 1 - 2 * c
    window = kv.shape[0]
    tiles = rows // 256
    span = (window - rows) + 256
    mine = pl.ds(pl.multiple_of(c * rows, rows), rows)
    centre = pl.ds(2 * rows, rows)

    def to_partner(src, dst, i):
        return pltpu.make_async_remote_copy(
            src, dst, cs.at[i], cr.at[i], device_id=(partner,), device_id_type=MESH
        )

    def halo(ref, by, i, send, recv):
        return pltpu.make_async_remote_copy(
            ref.at[centre],
            ref.at[pl.ds((2 - by) * rows, rows)],
            send.at[i],
            recv.at[i],
            device_id=(jnp.clip(here.me + by, 0, n - 1),),
            device_id_type=MESH,
        )

    def halo_each(ref, send, recv, what):
        for i, by in enumerate(REACH):
            to, frm = inside(here.me + by, n), inside(here.me - by, n)
            if what == "start":
                when(to, lambda i=i, by=by: halo(ref, by, i, send, recv).start())
            elif what == "recv":
                when(frm, lambda i=i, by=by: halo(ref, by, i, send, recv).wait_recv())
            else:
                when(to, lambda i=i, by=by: halo(ref, by, i, send, recv).wait_send())

    own = [
        pltpu.make_async_copy(slab.at[g], G.at[g, here.z, here.y, here.x], lsem.at[g])
        for g in range(GROUPS)
    ]
    for copy in own:
        copy.start()
    kx_in = pltpu.make_async_copy(kx_own, kx.at[centre], lsem.at[GROUPS])
    kx_in.start()
    dy_in = pltpu.make_async_copy(dy, dyf.at[mine], lsem.at[GROUPS + 1])
    dy_in.start()
    here.barrier(REACH)
    for copy in own:
        copy.wait()
    parts, copy, _ = gather_stages(here, G, gs, gr, D)
    ag = lambda r: gather_round(parts, copy, r, lambda g: None)
    ag(0)
    kx_in.wait()
    halo_each(kx, ks, kr, "start")
    dy_in.wait()
    dy_out = to_partner(dyf.at[mine], dyf.at[mine], 0)
    dy_out.start()
    edge = jnp.where(lax.broadcasted_iota(jnp.int32, (rows, 128), 1) == 25, -BIG, 0.0).astype(BF)
    for by in REACH:
        def absent(by=by):
            at_rows = pl.ds((2 - by) * rows, rows)
            kv[at_rows, :] = jnp.zeros((rows, kv.shape[1]), BF)
            kx[at_rows, :] = edge
        pl.when(jnp.logical_not(inside(here.me - by, n)))(absent)

    def attention(n1, bias, vt, S, Pm):
        ag(1)

        def norm_rows(i, _):
            at_rows = pl.ds(i * 64, 64)
            v = hid[at_rows, :].astype(F32)
            n1[at_rows, :] = (v * row_norm(v) * na[...]).astype(BF)
            return 0

        lax.fori_loop(0, rows // 64, norm_rows, 0)
        ag(2)
        lines = table.shape[0]
        for head in range(heads):
            line = shift_line(table[...], rel, head)
            for b in range(bias.shape[1] // 128):
                lo = line[19 - b : 20 - b, :]
                hi = line[18 - b : 19 - b, :]
                both = jnp.broadcast_to(jnp.concatenate([lo, hi], 1), (128, 256))
                bias[head, 128 * b : 128 * b + 128, :] = pltpu.roll(both, 0, 1, stride=1, stride_axis=0)[:, :128]
            if head == 1:
                ag(3)
            if head == 3:
                ag(4)
        ag(5)
        keep = pltpu.make_async_copy(G.at[0], ga.at[:, :, :, c], lsem.at[GROUPS + 2])
        keep.start()
        give = to_partner(G.at[0], ga.at[:, :, :, c], 1)
        give.start()
        keep.wait()
        give.wait_recv()
        ga_out = pltpu.make_async_copy(ga, o_ga, osem.at[1])
        ga_out.start()

        for part in (1, 2, 0):
            weight = ga[part].reshape(inner, D)
            for half in range(rows // 256):
                at_rows = pl.ds(256 * half, 256)
                got = nt(n1[at_rows, :], weight).astype(BF)
                if part == 0:
                    qv[at_rows, :] = got
                else:
                    kv[pl.ds(2 * rows + 256 * half, 256), (part - 1) * inner : part * inner] = got
        halo_each(kv, hs, hr, "start")
        ag(6)
        halo_each(kx, ks, kr, "recv")
        halo_each(kv, hs, hr, "recv")
        kv_out = pltpu.make_async_copy(kv, o_kv, osem.at[2])
        kv_out.start()
        kx_out = pltpu.make_async_copy(kx, o_kx, osem.at[3])
        kx_out.start()
        q_out = pltpu.make_async_copy(qv, o_q, osem.at[4])
        q_out.start()

        def turn(i, _):
            at_rows = pl.ds(pl.multiple_of(i * 256, 256), 256)
            vt[:, at_rows] = kv[at_rows, inner:].T
            return 0

        lax.fori_loop(0, window // 256, turn, 0)
        lane = lax.broadcasted_iota(jnp.int32, (256, 128), 1) // 64

        def pair(hp, _):
            @pl.when(hp > 0)
            def _():
                ag(hp + 6)

            cols = pl.ds(pl.multiple_of(hp * 128, 128), 128)

            def one(k, _):
                t, e = k // 2, k % 2
                base = pl.multiple_of(t * 256, 256)
                head = hp * 2 + e
                q = qv[pl.ds(base, 256), cols]
                q = jnp.where(lane == e, q, jnp.zeros_like(q))
                qa = jnp.concatenate([q, qx[pl.ds(base, 256), :]], 1)

                def score(b, m):
                    at_rows = pl.ds(pl.multiple_of(base + b * 256, 256), 256)
                    ka = jnp.concatenate([kv[at_rows, cols], kx[at_rows, :]], 1)
                    s = nt(ka, qa)
                    low = pl.multiple_of(b * 256, 256)
                    plane = jnp.concatenate(
                        [bias[head, pl.ds(low + 128, 256), :], bias[head, pl.ds(low, 256), :]], 1
                    )
                    s = s + plane
                    S[pl.ds(low, 256), :] = s
                    return jnp.maximum(m, jnp.max(s.reshape(32, 8, 256), axis=0))

                m = lax.fori_loop(0, span // 256, score, jnp.full((8, 256), -3e38, F32))
                m = jnp.max(m, axis=0, keepdims=True)

                def weigh(b, total):
                    at_rows = pl.ds(pl.multiple_of(b * 256, 256), 256)
                    p = jnp.exp(S[at_rows, :] - m)
                    Pm[at_rows, :] = p.astype(BF)
                    return total + jnp.sum(p.reshape(32, 8, 256), axis=0)

                total = lax.fori_loop(0, span // 256, weigh, jnp.zeros((8, 256), F32))
                total = jnp.sum(total, axis=0, keepdims=True)
                out_rows = pl.ds(pl.multiple_of(head * 64, 64), 64)
                mixed = nn(vt[out_rows, pl.ds(base, span)], Pm[...])
                at[out_rows, pl.ds(base, 256)] = mixed / total
                lse[pl.ds(head, 1), pl.ds(base, 256)] = m + jnp.log(total)
                return 0

            lax.fori_loop(0, 2 * tiles, one, 0)
            return 0

        lax.fori_loop(0, heads // 2, pair, 0)
        outs = [
            pltpu.make_async_copy(at, o_at, osem.at[5]),
            pltpu.make_async_copy(lse, o_lse, osem.at[6]),
        ]
        for o in outs:
            o.start()
        w_out = ga[3].reshape(inner, D)

        def after(i, _):
            at_rows = pl.ds(pl.multiple_of(i * 128, 128), 128)
            a = at[:, at_rows].T.astype(BF)
            v = hid[at_rows, :].astype(F32) + nn(a, w_out)
            x1[at_rows, :] = v
            n2f[pl.ds(pl.multiple_of(c * rows + i * 128, 128), 128), :] = (v * row_norm(v) * nf[...]).astype(BF)
            return 0

        lax.fori_loop(0, rows // 128, after, 0)
        n2_out = to_partner(n2f.at[mine], n2f.at[mine], 2)
        n2_out.start()
        x1_out = pltpu.make_async_copy(x1, o_x1, osem.at[7])
        x1_out.start()
        give.wait_send()
        n2_out.wait()
        dy_out.wait()
        halo_each(kx, ks, kr, "send")
        halo_each(kv, hs, hr, "send")
        for o in outs + [ga_out, kv_out, kx_out, q_out, x1_out]:
            o.wait()

    pl.run_scoped(
        attention,
        pltpu.VMEM((rows, D), BF),
        pltpu.VMEM((heads, span + 128, 128), F32),
        pltpu.VMEM((inner, window), BF),
        pltpu.VMEM((span, 256), F32),
        pltpu.VMEM((span, 256), BF),
    )

    def feed(acc_o, acc_n, ft, gt, ut, stage):
        acc_o[...] = jnp.zeros_like(acc_o)
        acc_n[...] = jnp.zeros_like(acc_n)

        def stage_out(j):
            return pltpu.make_async_copy(stage.at[j % 2], o_grads.at[j + 1], stsem.at[j % 2])

        def chunk(j, _):
            ag(j + 9)
            g = j + 1
            wg = G.at[g, :, :, :, pl.ds(0, 16), :]
            wu = G.at[g, :, :, :, pl.ds(16, 16), :]
            wd = G.at[g, :, :, :, pl.ds(32, 16), :]
            whole = lambda ref: ref[...].reshape(256, D)

            def tokens(i, _):
                at_rows = pl.ds(pl.multiple_of(i * 256, 256), 256)
                n2 = n2f[at_rows, :]
                gate = nt(whole(wg), n2)
                up = nt(whole(wu), n2)
                df = nt(whole(wd), dyf[at_rows, :])
                value, slope = gelu_parts(gate)
                f = (value * up).astype(BF)
                dg = (df * up * slope).astype(BF)
                du = (df * value).astype(BF)
                ft[:, at_rows] = f
                gt[:, at_rows] = dg
                ut[:, at_rows] = du
                acc_o[at_rows, :] += nn(f.T, whole(wd))
                acc_n[at_rows, :] += nn(dg.T, whole(wg)) + nn(du.T, whole(wu))
                return 0

            lax.fori_loop(0, 2 * rows // 256, tokens, 0)

            @pl.when(j >= 2)
            def _():
                stage_out(j - 2).wait()

            s = j % 2
            stage[s, :, :, :, 0:16, :] = nn(gt[...], n2f[...]).astype(BF).reshape(here.grid + (16, D))
            stage[s, :, :, :, 16:32, :] = nn(ut[...], n2f[...]).astype(BF).reshape(here.grid + (16, D))
            stage[s, :, :, :, 32:48, :] = nn(ft[...], dyf[...]).astype(BF).reshape(here.grid + (16, D))
            stage_out(j).start()
            return 0

        lax.fori_loop(0, GROUPS - 1, chunk, 0)
        outs = [
            pltpu.make_async_copy(acc_o, o_outp, osem.at[0]),
            pltpu.make_async_copy(acc_n, o_dn2p, osem.at[1]),
        ]
        for o in outs:
            o.start()
        gather_drain(parts, copy)
        for o in outs:
            o.wait()
        stage_out(GROUPS - 3).wait()
        stage_out(GROUPS - 2).wait()

    pl.run_scoped(
        feed,
        pltpu.VMEM((2 * rows, D), F32),
        pltpu.VMEM((2 * rows, D), F32),
        pltpu.VMEM((256, 2 * rows), BF),
        pltpu.VMEM((256, 2 * rows), BF),
        pltpu.VMEM((256, 2 * rows), BF),
        pltpu.VMEM((2,) + here.grid + (PIECE, D), BF),
    )


def forward_call(n, heads, slab, hid, dy, kx_own, qx, table, rel, na, nf):
    rows, D = hid.shape
    inner = heads * 64
    zs, ys, xs = GRIDS[n]
    window = 5 * rows
    span = window - rows + 256
    shape = jax.ShapeDtypeStruct
    any_, vm = pl.BlockSpec(memory_space=pl.ANY), pl.BlockSpec(memory_space=pltpu.VMEM)
    sm = pl.BlockSpec(memory_space=pltpu.SMEM)
    slots = 3 * 8
    dma = pltpu.SemaphoreType.DMA
    return pl.pallas_call(
        functools.partial(forward_kernel, n, heads),
        out_shape=(
            shape((GROUPS, zs, ys, xs, PIECE, D), BF),
            shape((2 * rows, D), F32),
            shape((2 * rows, D), F32),
            shape((rows, D), F32),
            shape((inner, rows), F32),
            shape((rows, inner), BF),
            shape((window, 2 * inner), BF),
            shape((window, 128), BF),
            shape((8, rows), F32),
            shape((zs, ys, xs, 2, PIECE, D), BF),
        ),
        in_specs=[any_, vm, any_, any_, vm, vm, sm, vm, vm],
        out_specs=(any_,) * 10,
        scratch_shapes=[
            pltpu.VMEM((GROUPS, zs, ys, xs, PIECE, D), BF),
            pltpu.VMEM((zs, ys, xs, 2, PIECE, D), BF),
            pltpu.VMEM((2 * rows, D), BF),
            pltpu.VMEM((2 * rows, D), BF),
            pltpu.VMEM((window, 2 * inner), BF),
            pltpu.VMEM((window, 128), BF),
            pltpu.VMEM((rows, inner), BF),
            pltpu.VMEM((rows, D), F32),
            pltpu.VMEM((inner, rows), F32),
            pltpu.VMEM((8, rows), F32),
            dma((GROUPS, slots)), dma((GROUPS, slots)),
            dma((GROUPS + 3,)),
            dma((4,)), dma((4,)), dma((4,)), dma((4,)),
            dma((3,)), dma((3,)),
            dma((8,)), dma((2,)),
        ],
        compiler_params=pltpu.CompilerParams(
            collective_id=1, has_side_effects=True, vmem_limit_bytes=63 * 2**20
        ),
        cost_estimate=pl.CostEstimate(flops=55 * 10**9, bytes_accessed=80 * 10**6, transcendentals=10**7),
        name="forward",
    )(slab, hid, dy, kx_own, qx, table, rel, na, nf)


def prepare(hidden, segments, delete_mask, bucket_table, attn_weight, gate_weight, up_weight, down_weight):
    D = hidden.shape[1]
    rows = hidden.shape[0]
    groups = GROUPS - 1
    ffn = jnp.stack([gate_weight.T, up_weight.T, down_weight]).reshape(3, groups, 16, D)
    ffn = jnp.transpose(ffn, (1, 0, 2, 3)).reshape(groups, PIECE, D)
    slab = jnp.concatenate([attn_weight.T[None], ffn], 0)
    lane = jnp.arange(128, dtype=jnp.int32)[None, :]
    seg = segments[:, None]
    digit = jnp.where(lane < 9, seg % 8, jnp.where(lane < 17, (seg // 8) % 8, seg // 64))
    hit = digit == (lane - 1) % 8
    coded = (lane >= 1) & (lane < 25)
    kx = jnp.where(lane == 0, delete_mask.astype(F32)[:, None], jnp.where(coded & ~hit, -BIG, 0.0)).astype(BF)
    qx = jnp.where((lane == 0) | (lane == 25) | (coded & hit), 1.0, 0.0).astype(BF)
    reach = bucket_table.shape[0]
    table = jnp.pad(jnp.flip(bucket_table), (257, 20 * 128 - 257 - reach), constant_values=-1).reshape(20, 128)
    table = jnp.pad(table, ((0, 4), (0, 0)), constant_values=-1)
    return slab, kx, qx, table


FIRST = (1, 2, 3, 4, 5, 0, 6, 7)
AT = 5
SLOTS = 3
WORK = 6
LINES = 56


def group_of(pos):
    if isinstance(pos, int):
        return FIRST[pos]
    return jnp.where(pos < AT, pos + 1, jnp.where(pos == AT, 0, pos))


def add_into(dst, src):
    dst[...] = (dst[...].astype(F32) + src[...].astype(F32)).astype(BF)


class Scatter:
    def __init__(self, here, source, work, land, landa, landz, result, send, recv, load, width):
        self.here, self.source, self.work, self.result = here, source, work, result
        self.land, self.landa, self.landz = land, landa, landz
        self.send, self.recv, self.load = send, recv, load
        self.parts = column_parts(width)

    def loading(self, part, pos):
        here = self.here
        zs, ys, xs = here.grid
        in_y = pl.ds(here.y, 1) if part == 1 else pl.ds(0, ys)
        in_x = pl.ds(here.x, 1) if part == 2 else pl.ds(0, xs)
        cols = pl.ds(*self.parts[part])
        return pltpu.make_async_copy(
            self.source.at[group_of(pos), :, in_y, in_x, :, cols],
            self.work.at[pos % WORK, :, in_y, in_x, :, cols],
            self.load.at[pos, part],
        )

    def start_load(self, pos):
        for part in range(3):
            self.loading(part, pos).start()

    def moves(self, part, k, pos):
        here = self.here
        zs, ys, xs = here.grid
        z, y, x = here.z, here.y, here.x
        cols = pl.ds(*self.parts[part])
        dim = (("z0", "z1", "z2", "y", "x"), ("y", "x", "z0", "z1", "z2"), ("x", "y", "z0", "z1", "z2"))[part][k]
        work, source, g = self.work, self.source, group_of(pos)
        w, slot = pos % WORK, pos % SLOTS
        base = 8 * part

        def remote(src, dst, at, device):
            return pltpu.make_async_remote_copy(
                src, dst, self.send.at[pos, at], self.recv.at[pos, at], device_id=(device,), device_id_type=MESH
            )

        if dim[0] == "z":
            step = int(dim[1])
            out = []
            for turn, way in enumerate((1, -1)):
                target = z + way * (zs - 1 - step)
                got = z + way * (zs - 2 - step)
                sends = inside(z + way, zs) & inside(target, zs)
                gets = inside(z - way, zs) & inside(got, zs)
                spot = step if turn == 0 or step == 0 else step + 2
                device = here.dev(jnp.clip(z + way, 0, zs - 1), y, x)
                block, mine = jnp.clip(target, 0, zs - 1), jnp.clip(got, 0, zs - 1)
                if part == 0:
                    src, dst = work.at[w, block, :, :, :, cols], self.landa.at[slot, spot]
                else:
                    src, dst = work.at[w, block, y, x, :, cols], self.landz.at[slot, spot, :, cols]

                def consume(mine=mine, dst=dst):
                    if part == 0:
                        for b in range(ys):
                            add_into(work.at[w, mine, b, :, :, cols], dst.at[b])
                    elif step < zs - 2:
                        add_into(work.at[w, mine, y, x, :, cols], dst)

                out.append((sends, gets, remote(src, dst, base + 2 + 2 * step + turn, device), consume))
            return out
        at = base + (0 if dim == "y" else 1)
        device = here.dev(z, 1 - y, x) if dim == "y" else here.dev(z, y, 1 - x)
        if k == 0 and dim == "y":
            src = source.at[g, :, pl.ds(1 - y, 1), :, :, cols]
            dst = work.at[w, :, pl.ds(y, 1), :, :, cols]
            pairs = [(work.at[w, b, y, :, :, cols], work.at[w, b, 1 - y, :, :, cols]) for b in range(zs)]
        elif k == 0:
            src = source.at[g, :, :, pl.ds(1 - x, 1), :, cols]
            dst = work.at[w, :, :, pl.ds(x, 1), :, cols]
            pairs = [(work.at[w, b, :, x, :, cols], work.at[w, b, :, 1 - x, :, cols]) for b in range(zs)]
        elif part != 0:
            src = work.at[w, :, y, 1 - x, :, cols] if dim == "x" else work.at[w, :, 1 - y, x, :, cols]
            dst = self.land.at[slot, :, :, cols]
            pairs = [(work.at[w, b, y, x, :, cols], self.land.at[slot, b, :, cols]) for b in range(zs)]
        elif dim == "y":
            src = work.at[w, z, 1 - y, :, :, cols]
            dst = self.land.at[slot, pl.ds(0, xs), :, cols]
            pairs = [(work.at[w, z, y, b, :, cols], self.land.at[slot, b, :, cols]) for b in range(xs)]
        else:
            src = work.at[w, z, y, 1 - x, :, cols]
            dst = self.land.at[slot, xs, :, cols]
            pairs = []

        def consume():
            for to, frm in pairs:
                add_into(to, frm)

        return [(None, None, remote(src, dst, at, device), consume)]

    def finish(self, part, pos):
        here = self.here
        zs, ys, xs = here.grid
        z, y, x = here.z, here.y, here.x
        slot, g = pos % SLOTS, group_of(pos)
        first, wide = self.parts[part]
        cols = pl.ds(first, wide)
        own = self.work[pos % WORK, z, y, x, :, cols].astype(F32)
        if part == 0:
            self.result[g, :, cols] = own + self.land[slot, xs, :, cols].astype(F32)
            return
        up = self.landz[slot, zs - 2, :, cols].astype(F32)
        down = self.landz[slot, zs, :, cols].astype(F32)
        self.result[g, :, cols] = own + jnp.where(z > 0, up, 0.0) + jnp.where(z < zs - 1, down, 0.0)

    def round(self, r):
        for k in range(STAGES, -1, -1):
            pos = r - k

            def step(pos=pos, k=k):
                for part in range(3):
                    if k == (0 if part == 0 else 1):
                        self.loading(part, pos).wait()
                    if k > 0:
                        for _, gets, copy, consume in self.moves(part, k - 1, pos):
                            def take(copy=copy, consume=consume):
                                copy.wait_recv()
                                consume()

                            when(gets, take)
                    if k < STAGES:
                        for sends, _, copy, _ in self.moves(part, k, pos):
                            when(sends, lambda copy=copy: copy.start())
                        continue
                    self.finish(part, pos)
                    for stage in range(STAGES):
                        for sends, _, copy, _ in self.moves(part, stage, pos):
                            when(sends, lambda copy=copy: copy.wait_send())
                if k == STAGES:
                    when(pos + WORK < GROUPS, lambda: self.start_load(pos + WORK))

            if isinstance(pos, int):
                if 0 <= pos < GROUPS:
                    step()
            else:
                pl.when(inside(pos, GROUPS))(step)


def norm_back(v, gain, d):
    r = row_norm(v)
    vr = v * r
    dg = d * gain
    return r * (dg - vr * jnp.mean(vr * dg, axis=-1, keepdims=True)), d * vr


def put_line(small, first, line):
    width = line.shape[1]
    for i in range(-(-width // 128)):
        wide = min(128, width - 128 * i)
        small[first + i : first + i + 1, 0:wide] = line[:, 128 * i : 128 * i + wide]


def backward_kernel(
    n, heads,
    grads, outp, dn2p, x1_in, at_in, q_in, kv_in, kx_in, lse, ga_in,
    hid, dy, qx, table, rel, na, nf,
    gr, o_out, o_dh, o_res, o_small, dn_land, op_land,
    work, land, landa, landz, res, dx1, kv, kx, qv, at, ga, dat, das, back, fold, small, sland,
    ss, rs, lds, cs, cr, hs, hr, ls, ps, pr, osem,
):
    here = Place(n)
    c = here.c
    rows, D = dx1.shape
    inner = qv.shape[1]
    window = kv.shape[0]
    zs, ys, xs = here.grid
    z, y, x = here.z, here.y, here.x
    span = window - rows + 256
    partner = here.me + 1 - 2 * c
    mine = pl.ds(pl.multiple_of(c * rows, rows), rows)
    theirs = pl.ds(pl.multiple_of((1 - c) * rows, rows), rows)

    def to_partner(src, dst, i):
        return pltpu.make_async_remote_copy(
            src, dst, cs.at[i], cr.at[i], device_id=(partner,), device_id_type=MESH
        )

    def local(src, dst, i):
        return pltpu.make_async_copy(src, dst, ls.at[i])

    sc = Scatter(here, gr, work, land, landa, landz, res, ss, rs, lds, D)
    for pos in range(WORK):
        if pos != AT:
            sc.start_load(pos)
    loads = [
        local(dn2p.at[mine], dx1, 0), local(kv_in, kv, 1), local(kx_in, kx, 2),
        local(q_in, qv, 3), local(at_in, at, 4), local(ga_in, ga, 5),
    ]
    for load in loads:
        load.start()
    here.barrier(REACH, True)
    dn_out = to_partner(dn2p.at[theirs], dn_land, 0)
    dn_out.start()
    sc.round(0)
    op_out = to_partner(outp.at[theirs], op_land, 1)
    op_out.start()
    small[...] = jnp.zeros_like(small)

    def after_ffn(x1, other, grad, low):
        first = [local(x1_in, x1, 6), local(dy, grad, 7)]
        for load in first:
            load.start()
        dn_out.wait_recv()
        second = local(dn_land, other, 8)
        second.start()
        for load in loads + first + [second]:
            load.wait()
        w_out = ga[zs - 1].reshape(inner, D)

        def through(i, total):
            at_rows = pl.ds(pl.multiple_of(i * 128, 128), 128)
            d = dx1[at_rows, :] + other[at_rows, :]
            back_v, gain_d = norm_back(x1[at_rows, :], nf[...], d)
            v = grad[at_rows, :].astype(F32) + back_v
            dx1[at_rows, :] = v
            v = v.astype(BF)
            low[at_rows, :] = v
            da = nt(v, w_out).astype(BF)
            das[at_rows, :] = da
            dat[:, at_rows] = da.T
            return total + jnp.sum(gain_d.reshape(16, 8, D), axis=0)

        total = lax.fori_loop(0, rows // 128, through, jnp.zeros((8, D), F32))
        put_line(small, 44, jnp.sum(total, axis=0, keepdims=True))
        third = local(outp.at[mine], other, 9)
        third.start()
        sc.round(1)
        for h in range(2):
            part = nn(at[pl.ds(h * (inner // 2), inner // 2), :].astype(BF), low[...])
            ga[zs - 1, h] = part.astype(BF).reshape(xs, 2, PIECE, D)
        third.wait()
        op_out.wait_recv()

        def add(i, _):
            at_rows = pl.ds(pl.multiple_of(i * 64, 64), 64)
            x1[at_rows, :] = x1[at_rows, :] + other[at_rows, :]
            return 0

        lax.fori_loop(0, rows // 64, add, 0)
        fourth = local(op_land, other, 10)
        fourth.start()
        fourth.wait()

        def put(i, _):
            at_rows = pl.ds(pl.multiple_of(i * 64, 64), 64)
            low[at_rows, :] = (x1[at_rows, :] + other[at_rows, :]).astype(BF)
            return 0

        lax.fori_loop(0, rows // 64, put, 0)
        out = pltpu.make_async_copy(low, o_out, osem.at[0])
        out.start()
        out.wait()
        dn_out.wait_send()
        op_out.wait_send()

    pl.run_scoped(
        after_ffn, pltpu.VMEM((rows, D), F32), pltpu.VMEM((rows, D), F32), pltpu.VMEM((rows, D), BF),
        pltpu.VMEM((rows, D), BF),
    )

    def home(dkv, hp, by, i):
        return pltpu.make_async_remote_copy(
            dkv.at[hp, pl.ds((2 + by) * rows, rows)],
            back.at[hp, i],
            hs.at[hp, i],
            hr.at[hp, i],
            device_id=(jnp.clip(here.me + by, 0, n - 1),),
            device_id_type=MESH,
        )

    def attention(acc_k, acc_v, skew, kt, bias, dkv, dqt, n1, proj, proj_t, hid_v):
        hid_in = local(hid, hid_v, 11)
        hid_in.start()

        def turn(i, _):
            at_rows = pl.ds(pl.multiple_of(i * 256, 256), 256)
            kt[:, at_rows] = kv[at_rows, 0:inner].T
            return 0

        lax.fori_loop(0, window // 256, turn, 0)
        dqt[...] = jnp.zeros_like(dqt)
        lane = lax.broadcasted_iota(jnp.int32, (256, 128), 1) // 64
        lane_of = lax.broadcasted_iota(jnp.int32, (32, 128), 1)
        blocks = skew.shape[0] // 128

        def one_head(hp, e):
            head = hp * 2 + e
            cols = pl.ds(pl.multiple_of(hp * 128, 128), 128)
            vcols = pl.ds(pl.multiple_of(inner + hp * 128, 128), 128)
            out_rows = pl.ds(pl.multiple_of(head * 64, 64), 64)
            line = shift_line(table[...], rel, head)
            for b in range(blocks):
                both = jnp.concatenate([line[19 - b : 20 - b, :], line[18 - b : 19 - b, :]], 1)
                both = jnp.broadcast_to(both, (128, 256))
                bias[128 * b : 128 * b + 128, :] = pltpu.roll(both, 0, 1, stride=1, stride_axis=0)[:, :128]
            skew[...] = jnp.zeros_like(skew)

            def tile(t, _):
                base = pl.multiple_of(t * 256, 256)
                here_q = pl.ds(base, 256)
                q = qv[here_q, cols]
                q = jnp.where(lane == e, q, jnp.zeros_like(q))
                qa = jnp.concatenate([q, qx[here_q, :]], 1)
                da = das[here_q, cols]
                da = jnp.where(lane == e, da, jnp.zeros_like(da))
                logs = lse[pl.ds(head, 1), here_q]
                delta = jnp.sum(dat[out_rows, here_q].astype(F32) * at[out_rows, here_q], axis=0, keepdims=True)

                def block(b, dq):
                    low = pl.multiple_of(b * 256, 256)
                    at_rows = pl.ds(pl.multiple_of(base + b * 256, 256), 256)
                    ka = jnp.concatenate([kv[at_rows, cols], kx[at_rows, :]], 1)
                    plane = jnp.concatenate([bias[pl.ds(low + 128, 256), :], bias[pl.ds(low, 256), :]], 1)
                    p = jnp.exp(nt(ka, qa) + plane - logs)
                    ds = p * (nt(kv[at_rows, vcols], da) - delta)
                    skew[pl.ds(low + 128, 256), :] += ds[:, 0:128]
                    skew[pl.ds(low, 256), :] += ds[:, 128:256]
                    dsr = ds.astype(BF)
                    acc_v[at_rows, :] += nn(p.astype(BF), da)
                    acc_k[at_rows, :] += nn(dsr, q)
                    return dq + nn(kt[out_rows, at_rows], dsr)

                dqt[out_rows, here_q] = lax.fori_loop(0, span // 256, block, jnp.zeros((64, 256), F32))
                return 0

            lax.fori_loop(0, rows // 256, tile, 0)
            tail = [None] * (blocks + 1)
            for b in range(blocks):
                a = jnp.concatenate([skew[128 * b : 128 * b + 128, :], jnp.zeros((128, 128), F32)], 1)
                half = 64
                while half >= 1:
                    a = a[0:half] + pltpu.roll(a[half : 2 * half], 256 - half, 1)
                    half //= 2
                for at_line, part in ((19 - b, a[:, 0:128]), (18 - b, a[:, 128:256])):
                    tail[at_line] = part if tail[at_line] is None else tail[at_line] + part
            line_d = jnp.concatenate(tail + [jnp.zeros((4, 128), F32)], 0)
            sums = [
                jnp.sum(jnp.where(table[...] == b, line_d, 0.0), axis=0, keepdims=True) for b in range(rel.shape[0])
            ]
            sums = jnp.sum(jnp.concatenate(sums, 0), axis=1, keepdims=True)
            small[0:32, :] = jnp.where(lane_of == head, sums, small[0:32, :])

        def pair(hp, _):
            sc.round(hp + 2)
            acc_k[...] = jnp.zeros_like(acc_k)
            acc_v[...] = jnp.zeros_like(acc_v)
            lax.fori_loop(0, 2, lambda e, _: (one_head(hp, e), 0)[1], 0)

            def pack(i, _):
                at_rows = pl.ds(pl.multiple_of(i * 128, 128), 128)
                dkv[hp, at_rows, 0:128] = acc_k[at_rows, :].astype(BF)
                dkv[hp, at_rows, 128:256] = acc_v[at_rows, :].astype(BF)
                return 0

            lax.fori_loop(0, window // 128, pack, 0)
            for i, by in enumerate(REACH):
                when(inside(here.me + by, n), lambda i=i, by=by: home(dkv, hp, by, i).start())
            return 0

        lax.fori_loop(0, heads // 2, pair, 0)
        hid_in.wait()

        def norm_rows(i, _):
            at_rows = pl.ds(pl.multiple_of(i * 64, 64), 64)
            v = hid_v[at_rows, :].astype(F32)
            n1[at_rows, :] = (v * row_norm(v) * na[...]).astype(BF)
            return 0

        lax.fori_loop(0, rows // 64, norm_rows, 0)

        def gather_pair(hp, _):
            for i, by in enumerate(REACH):
                frm = inside(here.me - by, n)
                when(frm, lambda i=i, by=by: home(dkv, hp, by, i).wait_recv())

                def absent(i=i):
                    back[hp, i] = jnp.zeros((rows, 256), BF)

                when(jnp.logical_not(frm), absent)

            def sum_rows(j, _):
                at_rows = pl.ds(pl.multiple_of(j * 128, 128), 128)
                total = dkv[hp, pl.ds(pl.multiple_of(2 * rows + j * 128, 128), 128), :].astype(F32)
                for i in range(4):
                    total = total + back[hp, i, at_rows, :].astype(F32)
                total = total.astype(BF)
                for part in range(2):
                    piece = total[:, 128 * part : 128 * part + 128]
                    to = pl.ds(pl.multiple_of((1 + part) * inner + hp * 128, 128), 128)
                    proj[at_rows, to] = piece
                    proj_t[to, at_rows] = piece.T
                to = pl.ds(pl.multiple_of(hp * 128, 128), 128)
                piece = dqt[to, at_rows].astype(BF)
                proj_t[to, at_rows] = piece
                proj[at_rows, to] = piece.T
                return 0

            lax.fori_loop(0, rows // 128, sum_rows, 0)
            return 0

        lax.fori_loop(0, heads // 2, gather_pair, 0)

        def to_hidden(i, total):
            at_rows = pl.ds(pl.multiple_of(i * 128, 128), 128)
            d = nn(proj[at_rows, 0:inner], ga[0].reshape(inner, D))
            d = d + nn(proj[at_rows, inner : 2 * inner], ga[1].reshape(inner, D))
            d = d + nn(proj[at_rows, 2 * inner : 3 * inner], ga[2].reshape(inner, D))
            back_v, gain_d = norm_back(hid_v[at_rows, :].astype(F32), na[...], d)
            dx1[at_rows, :] = dx1[at_rows, :] + back_v
            return total + jnp.sum(gain_d.reshape(16, 8, D), axis=0)

        total = lax.fori_loop(0, rows // 128, to_hidden, jnp.zeros((8, D), F32))
        put_line(small, 32, jnp.sum(total, axis=0, keepdims=True))
        dh_out = pltpu.make_async_copy(dx1, o_dh, osem.at[1])
        dh_out.start()

        for part in range(3):
            for h in range(2):
                take = pl.ds(part * inner + h * (inner // 2), inner // 2)
                ga[part, h] = nn(proj_t[take, :], n1[...]).astype(BF).reshape(xs, 2, PIECE, D)
        for i, by in enumerate(REACH):
            def sent(i=i, by=by):
                for hp in range(heads // 2):
                    home(dkv, hp, by, i).wait_send()

            when(inside(here.me + by, n), sent)
        dh_out.wait()

    inner_f = heads * 64
    pl.run_scoped(
        attention,
        pltpu.VMEM((window, 128), F32), pltpu.VMEM((window, 128), F32), pltpu.VMEM((span + 128, 128), F32),
        pltpu.VMEM((inner_f, window), BF), pltpu.VMEM((span + 128, 128), F32), pltpu.VMEM((heads // 2, window, 256), BF),
        pltpu.VMEM((inner_f, rows), F32), pltpu.VMEM((rows, D), BF), pltpu.VMEM((rows, 3 * inner_f), BF),
        pltpu.VMEM((3 * inner_f, rows), BF), pltpu.VMEM((rows, D), BF),
    )

    fold_out = to_partner(ga.at[:, :, :, 1 - c], fold, 2)
    fold_out.start()
    def small_to(src, slot, device, i):
        return pltpu.make_async_remote_copy(
            src, sland.at[slot], ps.at[i], pr.at[i], device_id=(device,), device_id_type=MESH
        )

    swap = small_to(small, 0, partner, 0)
    swap.start()
    fold_out.wait()
    for a in range(zs):
        for b in range(ys):
            add_into(fold.at[a, b], ga.at[a, b, :, c])
    fold_in = pltpu.make_async_copy(fold, gr.at[0], osem.at[2])
    fold_in.start()
    fold_in.wait()
    sc.start_load(AT)
    sc.round(5)
    swap.wait()
    small[...] = small[...] + sland[0]
    swap = small_to(small, 1, here.dev(z, y, 1 - x), 1)
    swap.start()
    sc.round(6)
    swap.wait()
    small[...] = small[...] + sland[1]
    swap = small_to(small, 2, here.dev(z, 1 - y, x), 2)
    swap.start()
    sc.round(7)
    swap.wait()
    small[...] = small[...] + sland[2]
    swaps = []
    for far in range(1, zs):
        swaps.append(small_to(small, 3 + far, here.dev((z + far) % zs, y, x), 2 + far))
        swaps[-1].start()
    sc.round(8)
    for swap in swaps:
        swap.wait()
    sland[3] = small[...]
    ordered = jnp.zeros(small.shape, F32)
    for plane in range(zs):
        ordered = ordered + sland[3 + (z - plane + zs) % zs]
    small[...] = ordered
    small_out = pltpu.make_async_copy(small, o_small, osem.at[3])
    small_out.start()
    for r in range(9, GROUPS + STAGES):
        sc.round(r)
    res_out = pltpu.make_async_copy(res, o_res, osem.at[4])
    res_out.start()
    res_out.wait()
    small_out.wait()


def backward_call(n, heads, kept, hid, dy, qx, table, rel, na, nf):
    grads, outp, dn2p, x1, at, q, kv, kx, lse, ga = kept
    rows, D = hid.shape
    inner = heads * 64
    zs, ys, xs = GRIDS[n]
    window = 5 * rows
    shape = jax.ShapeDtypeStruct
    any_, vm = pl.BlockSpec(memory_space=pl.ANY), pl.BlockSpec(memory_space=pltpu.VMEM)
    sm = pl.BlockSpec(memory_space=pltpu.SMEM)
    dma = pltpu.SemaphoreType.DMA
    return pl.pallas_call(
        functools.partial(backward_kernel, n, heads),
        out_shape=(
            shape(grads.shape, BF),
            shape((rows, D), BF),
            shape((rows, D), F32),
            shape((GROUPS, PIECE, D), F32),
            shape((LINES, 128), F32),
            shape((rows, D), F32),
            shape((rows, D), F32),
        ),
        in_specs=[any_] * 8 + [vm] + [any_] * 3 + [vm, vm, sm, vm, vm],
        out_specs=(any_,) * 7,
        input_output_aliases={0: 0},
        scratch_shapes=[
            pltpu.VMEM((WORK, zs, ys, xs, PIECE, D), BF),
            pltpu.VMEM((SLOTS, zs, PIECE, D), BF),
            pltpu.VMEM((SLOTS, 5, ys, xs, PIECE, 256), BF),
            pltpu.VMEM((SLOTS, 5, PIECE, D), BF),
            pltpu.VMEM((GROUPS, PIECE, D), F32),
            pltpu.VMEM((rows, D), F32),
            pltpu.VMEM((window, 2 * inner), BF),
            pltpu.VMEM((window, 128), BF),
            pltpu.VMEM((rows, inner), BF),
            pltpu.VMEM((inner, rows), F32),
            pltpu.VMEM((zs, ys, xs, 2, PIECE, D), BF),
            pltpu.VMEM((inner, rows), BF),
            pltpu.VMEM((rows, inner), BF),
            pltpu.VMEM((heads // 2, 4, rows, 256), BF),
            pltpu.VMEM((zs, ys, xs, PIECE, D), BF),
            pltpu.VMEM((LINES, 128), F32),
            pltpu.VMEM((3 + zs, LINES, 128), F32),
            dma((GROUPS, 24)), dma((GROUPS, 24)), dma((GROUPS, 3)),
            dma((3,)), dma((3,)),
            dma((heads // 2, 4)), dma((heads // 2, 4)),
            dma((12,)),
            dma((3 + zs,)), dma((3 + zs,)),
            dma((5,)),
        ],
        compiler_params=pltpu.CompilerParams(
            collective_id=2, has_side_effects=True, vmem_limit_bytes=63 * 2**20
        ),
        cost_estimate=pl.CostEstimate(flops=12 * 10**9, bytes_accessed=60 * 10**6, transcendentals=10**7),
        name="backward",
    )(grads, outp, dn2p, x1, at, q, kv, kx, lse, ga, hid, dy, qx, table, rel, na, nf)


def shards(
    n, hidden, segments, delete_mask, bucket_table, attn_weight, gate_weight, up_weight, down_weight,
    norm_attn, norm_ffn, rel_bias, out_grad,
):
    heads = rel_bias.shape[1]
    D = hidden.shape[1]
    slab, kx, qx, table = prepare(
        hidden, segments, delete_mask, bucket_table, attn_weight, gate_weight, up_weight, down_weight
    )
    na, nf = norm_attn[None], norm_ffn[None]
    kept = forward_call(n, heads, slab, hidden, out_grad, kx, qx, table, rel_bias, na, nf)
    _, output, d_hidden, res, small, _, _ = backward_call(
        n, heads, kept, hidden, out_grad, qx, table, rel_bias, na, nf
    )
    ffn = res[1:].reshape(GROUPS - 1, 3, 16, D)
    mats = [ffn[:, i].reshape(-1, D) for i in range(3)]
    line = lambda first: small[first : first + 12].reshape(-1)[:D]
    return (
        output, d_hidden, res[0].T, mats[0].T, mats[1].T, mats[2], line(32), line(44), small[:32, :heads],
    )


def shifted(x, axis, by):
    count = lax.axis_size(axis)
    pairs = [(i, i + by) for i in range(count) if 0 <= i + by < count]
    return lax.ppermute(x, axis, pairs)


def shortened(x):

    def short(part):
        return part.astype(jnp.bfloat16) if part.dtype == jnp.float32 else part

    return jax.tree.map(short, x)


def rms_norm(value, gain):
    return value * lax.rsqrt(jnp.mean(value * value, axis=-1, keepdims=True) + 1e-06) * gain


def matmul(left, right):
    return jnp.dot(left, right, preferred_element_type=jnp.float32)


def matmul_tn(left, right):
    return lax.dot_general(
        left, right, (((0,), (0,)), ((), ())), preferred_element_type=jnp.float32
    )


def matmul_nt(left, right):
    return lax.dot_general(
        left, right, (((1,), (1,)), ((), ())), preferred_element_type=jnp.float32
    )


def gated_unit(gate_in, up_in):
    return jax.nn.gelu(gate_in) * up_in


def toeplitz(line, row_count, window):
    span_len = line.shape[0]
    tiled = jnp.tile(line, row_count)[: row_count * (span_len - 1)].reshape(row_count, span_len - 1)
    return tiled[:, :window]


def diagonal_sums(plane, span_len):
    row_count, window = plane.shape
    padded = jnp.pad(plane, ((0, 0), (0, span_len - 1 - window))).reshape(-1)
    padded = jnp.pad(padded, (0, row_count)).reshape(row_count, span_len)
    return jnp.sum(padded, axis=0)


def head_scores(q_head, k_head, mask_win, same_doc, bias_plane):
    raw = matmul_nt(q_head, k_head)
    scores = raw + bias_plane + mask_win[None, :]
    return jnp.where(same_doc, scores, -1e30)


def plain_shards(
    hidden,
    segments,
    delete_mask,
    bucket_table,
    attn_weight,
    gate_weight,
    up_weight,
    down_weight,
    norm_attn,
    norm_ffn,
    rel_bias,
    out_grad,
):
    row_count = hidden.shape[0]
    head_count = rel_bias.shape[1]
    bucket_count = rel_bias.shape[0]
    inner_width = attn_weight.shape[1] * lax.axis_size("seq") // 4
    head_width = inner_width // head_count
    table_len = bucket_table.shape[0]
    longest = (table_len + 1) // 2
    reach_blocks = (longest + row_count - 2) // row_count
    margin = reach_blocks * row_count
    window = (2 * reach_blocks + 1) * row_count
    span_len = row_count + window - 1
    w_attn, w_gate, w_up, w_down = (
        lax.all_gather(attn_weight, "seq", axis=1, tiled=True),
        lax.all_gather(gate_weight, "seq", axis=1, tiled=True),
        lax.all_gather(up_weight, "seq", axis=1, tiled=True),
        lax.all_gather(down_weight, "seq", axis=0, tiled=True),
    )
    residual = hidden.astype(jnp.float32)
    normed = rms_norm(residual, norm_attn).astype(jnp.bfloat16)
    projected = matmul(normed, w_attn[:, : 3 * inner_width]).astype(jnp.bfloat16)
    queries = projected[:, :inner_width]
    key_rows = projected[:, inner_width : 2 * inner_width]
    value_rows = projected[:, 2 * inner_width :]
    own_block = (key_rows, value_rows, segments + 1, delete_mask)
    both_sides = []
    for direction in (1, -1):
        current = own_block
        received = []
        for distance in range(reach_blocks):
            current = shifted((current[0], current[1], current[2], current[3]), "seq", direction)
            received.append(current)
        both_sides.append(received)
    ordered = both_sides[0][::-1] + [own_block] + both_sides[1]
    k_win = jnp.concatenate([portion[0] for portion in ordered], 0)
    v_win = jnp.concatenate([portion[1] for portion in ordered], 0)
    seg_win = jnp.concatenate([portion[2] for portion in ordered], 0)
    mask_win = jnp.concatenate([portion[3] for portion in ordered], 0).astype(jnp.float32)
    line_index = (jnp.arange(span_len, dtype=jnp.int32) + row_count - 1) % span_len
    line_offset = line_index - margin - (row_count - 1)
    line_bucket = jnp.take(
        bucket_table, jnp.clip(line_offset, 1 - longest, longest - 1) + longest - 1
    )
    line_onehot = (
        line_bucket[:, None] == jnp.arange(bucket_count, dtype=jnp.int32)[None, :]
    ).astype(jnp.float32)
    line_bias = jnp.dot(line_onehot, rel_bias, precision=lax.Precision.HIGHEST)
    same_doc = segments[:, None] + 1 == seg_win[None, :]
    mixed_parts = []
    log_parts = []
    for head in range(head_count):
        cols = slice(head * head_width, (head + 1) * head_width)
        bias_plane = toeplitz(line_bias[:, head], row_count, window)
        scores = head_scores(queries[:, cols], k_win[:, cols], mask_win, same_doc, bias_plane)
        row_max = jnp.max(scores, axis=-1, keepdims=True)
        exp_scores = jnp.exp(scores - row_max)
        row_total = jnp.sum(exp_scores, axis=-1, keepdims=True)
        log_parts.append(row_max + jnp.log(row_total))
        softmax_weights = (exp_scores / row_total).astype(jnp.bfloat16)
        mixed_parts.append(matmul(softmax_weights, v_win[:, cols]))
    attended = jnp.concatenate(mixed_parts, 1).astype(jnp.bfloat16)
    w_out = w_attn[:, 3 * inner_width :]
    after = residual + matmul_nt(attended, w_out)
    normed_ffn = rms_norm(after, norm_ffn).astype(jnp.bfloat16)
    gate_act = matmul(normed_ffn, w_gate)
    up_act = matmul(normed_ffn, w_up)
    activated = gated_unit(gate_act, up_act).astype(jnp.bfloat16)
    output = (after + matmul(activated, w_down)).astype(jnp.bfloat16)
    d_activated = matmul_nt(out_grad, w_down)
    d_down = matmul_tn(activated, out_grad)
    unit_out, unit_pull = jax.vjp(gated_unit, gate_act, up_act)
    d_gate_act, d_up_act = unit_pull(d_activated)
    d_gate_act = d_gate_act.astype(jnp.bfloat16)
    d_up_act = d_up_act.astype(jnp.bfloat16)
    d_normed_ffn = matmul_nt(d_gate_act, w_gate) + matmul_nt(d_up_act, w_up)
    d_w_gate = matmul_tn(normed_ffn, d_gate_act)
    d_w_up = matmul_tn(normed_ffn, d_up_act)
    norm_out, second_pull = jax.vjp(rms_norm, after, norm_ffn)
    d_after_part, d_norm_ffn = second_pull(d_normed_ffn)
    d_after = out_grad.astype(jnp.float32) + d_after_part
    d_after_low = d_after.astype(jnp.bfloat16)
    d_w_out = matmul_tn(d_after_low, attended)
    d_mixed = matmul(d_after_low, w_out).astype(jnp.bfloat16)
    dq_parts = []
    dk_parts = []
    dv_parts = []
    line_grads = []
    for head in range(head_count):
        cols = slice(head * head_width, (head + 1) * head_width)
        bias_plane = toeplitz(line_bias[:, head], row_count, window)
        scores = head_scores(queries[:, cols], k_win[:, cols], mask_win, same_doc, bias_plane)
        recomputed = jnp.exp(scores - log_parts[head])
        d_mix_head = d_mixed[:, cols]
        d_weights = matmul_nt(d_mix_head, v_win[:, cols])
        dv_parts.append(matmul_tn(recomputed.astype(jnp.bfloat16), d_mix_head))
        row_delta = jnp.sum(recomputed * d_weights, axis=-1, keepdims=True)
        d_scores = recomputed * (d_weights - row_delta)
        line_grads.append(diagonal_sums(d_scores, span_len))
        d_scores_low = d_scores.astype(jnp.bfloat16)
        dq_parts.append(matmul(d_scores_low, k_win[:, cols]))
        dk_parts.append(matmul_tn(d_scores_low, queries[:, cols]))
    d_queries = jnp.concatenate(dq_parts, 1)
    d_k_win = jnp.concatenate(dk_parts, 1)
    d_v_win = jnp.concatenate(dv_parts, 1)
    d_rel = lax.dot_general(
        line_onehot,
        jnp.stack(line_grads, 1),
        (((0,), (0,)), ((), ())),
        precision=lax.Precision.HIGHEST,
    )
    returned = [
        (
            d_k_win[slot * row_count : (slot + 1) * row_count],
            d_v_win[slot * row_count : (slot + 1) * row_count],
        )
        for slot in range(2 * reach_blocks + 1)
    ]
    d_keys = returned[reach_blocks][0]
    d_values = returned[reach_blocks][1]
    for direction in (1, -1):
        carried = (jnp.zeros_like(d_keys), jnp.zeros_like(d_values))
        for distance in range(reach_blocks, 0, -1):
            portion = returned[reach_blocks - direction * distance]
            carried = shifted(
                (shortened(carried[0] + portion[0]), shortened(carried[1] + portion[1])),
                "seq",
                -direction,
            )
        d_keys = d_keys + carried[0]
        d_values = d_values + carried[1]
    d_projected = jnp.concatenate([d_queries, d_keys, d_values], 1).astype(jnp.bfloat16)
    d_normed = matmul_nt(d_projected, w_attn[:, : 3 * inner_width])
    d_w_proj = matmul_tn(normed, d_projected)
    first_out, first_pull = jax.vjp(rms_norm, residual, norm_attn)
    d_resid_part, d_norm_attn = first_pull(d_normed)
    d_hidden = d_after + d_resid_part
    d_attn_full = jnp.concatenate([d_w_proj, d_w_out], 1)
    g_attn, g_gate, g_up, g_down = (
        lax.psum_scatter(d_attn_full, "seq", scatter_dimension=1, tiled=True),
        lax.psum_scatter(d_w_gate, "seq", scatter_dimension=1, tiled=True),
        lax.psum_scatter(d_w_up, "seq", scatter_dimension=1, tiled=True),
        lax.psum_scatter(d_down, "seq", scatter_dimension=0, tiled=True),
    )
    s_attn, s_ffn, s_rel = lax.psum((d_norm_attn, d_norm_ffn, d_rel), "seq")
    return (output, d_hidden, g_attn, g_gate, g_up, g_down, s_attn, s_ffn, s_rel)


def solution(mesh):
    placed = (
        P("seq", None), P("seq"), P("seq"), P(), P(None, "seq"), P(None, "seq"), P(None, "seq"), P("seq", None),
        P(), P(), P(), P("seq", None),
    )
    n = mesh.shape["seq"]
    body = functools.partial(shards, n) if n in GRIDS else plain_shards
    return jax.shard_map(
        body,
        mesh=mesh,
        in_specs=placed,
        out_specs=(
            P("seq", None), P("seq", None), P(None, "seq"), P(None, "seq"), P(None, "seq"), P("seq", None),
            P(), P(), P(),
        ),
        check_vma=False,
    )
```

```python
import functools
import math
import jax
import jax.numpy as jnp
from jax import lax
from jax.experimental import pallas as pl
from jax.experimental.pallas import tpu as pltpu
from jax.sharding import PartitionSpec as P

MESH = pl.DeviceIdType.MESH
BF = jnp.bfloat16
F32 = jnp.float32
BIG = 1e30
GRIDS = {32: (4, 2, 2)}
ORDERS = ("xyz", "zxy", "zyx")
GROUPS = 8
STAGES = 5
PIECE = 48
EPS = 1e-06


def nt(a, b):
    return lax.dot_general(a, b, (((1,), (1,)), ((), ())), preferred_element_type=F32)


def nn(a, b):
    return jnp.dot(a, b, preferred_element_type=F32)


def column_parts(width):
    return ((0, 384), (384, 512), (896, width - 896))


def when(cond, body):
    if cond is None:
        body()
    else:
        pl.when(cond)(body)


def inside(value, count):
    return (value >= 0) & (value < count)


class Place:
    def __init__(self, n):
        self.n = n
        self.grid = GRIDS[n]
        zs, ys, xs = self.grid
        self.me = lax.axis_index("seq")
        self.c = self.me % 2
        chip = self.me // 2
        self.x = chip % xs
        self.y = (chip // xs) % ys
        self.z = chip // (xs * ys)

    def dev(self, z, y, x):
        _, ys, xs = self.grid
        return ((z * ys + y) * xs + x) * 2 + self.c

    def around(self):
        zs = self.grid[0]
        z, y, x = self.z, self.y, self.x
        out = [
            (None, self.me + 1 - 2 * self.c),
            (None, self.dev(z, y, 1 - x)),
            (None, self.dev(z, 1 - y, x)),
            (z < zs - 1, self.dev(jnp.minimum(z + 1, zs - 1), y, x)),
            (z > 0, self.dev(jnp.maximum(z - 1, 0), y, x)),
        ]
        return out

    def barrier(self, reach, far=False):
        sem = pltpu.get_barrier_semaphore()
        pairs = self.around()
        if far:
            zs = self.grid[0]
            pairs = pairs[:3] + [(None, self.dev((self.z + i) % zs, self.y, self.x)) for i in range(1, zs)]
        for by in reach:
            target = self.me + by
            pairs.append((inside(target, self.n), jnp.clip(target, 0, self.n - 1)))
        count = 0
        for cond, device in pairs:
            when(
                cond,
                lambda device=device: pl.semaphore_signal(
                    sem, inc=1, device_id=(device,), device_id_type=MESH
                ),
            )
            count = count + (1 if cond is None else cond.astype(jnp.int32))
        pl.semaphore_wait(sem, count)


def gather_stages(here, blocks, send, recv, width):
    zs, ys, xs = here.grid
    z, y, x = here.z, here.y, here.x
    parts = []
    slot = 0
    for order, (first, wide) in zip(ORDERS, column_parts(width)):
        cols = pl.ds(first, wide)
        have = set()
        stages = []
        for dim in order:
            in_y = pl.ds(0, ys) if "y" in have else pl.ds(y, 1)
            in_x = pl.ds(0, xs) if "x" in have else pl.ds(x, 1)
            if dim == "z":
                for step in range(zs - 1):
                    moves = []
                    for way in (1, -1):
                        source = z - way * step
                        sends = inside(source, zs) & inside(z + way, zs)
                        gets = inside(z - way - way * step, zs) & inside(z - way, zs)
                        in_z = pl.ds(jnp.clip(source, 0, zs - 1), 1)
                        device = here.dev(jnp.clip(z + way, 0, zs - 1), y, x)
                        moves.append((sends, gets, in_z, in_y, in_x, cols, device, slot))
                        slot += 1
                    stages.append(moves)
            else:
                in_z = pl.ds(0, zs) if "z" in have else pl.ds(z, 1)
                device = here.dev(z, y, 1 - x) if dim == "x" else here.dev(z, 1 - y, x)
                stages.append([(None, None, in_z, in_y, in_x, cols, device, slot)])
                slot += 1
            have.add(dim)
        parts.append(stages)

    def copy(move, g):
        _, _, in_z, in_y, in_x, cols, device, at = move
        ref = blocks.at[g, in_z, in_y, in_x, :, cols]
        return pltpu.make_async_remote_copy(
            ref, ref, send.at[g, at], recv.at[g, at], device_id=(device,), device_id_type=MESH
        )

    return parts, copy, slot


def gather_visit(parts, copy, v):
    for k in range(STAGES, -1, -1):
        fast = isinstance(v, int) and v == k
        g = 0 if fast else v - 2 * k

        def step(g=g, k=k):
            for stages in parts:
                if k > 0:
                    for move in stages[k - 1]:
                        when(move[1], lambda move=move: copy(move, g).wait_recv())
                if k < STAGES:
                    for move in stages[k]:
                        when(move[0], lambda move=move: copy(move, g).start())

        if isinstance(v, int):
            if fast or 0 < g < GROUPS:
                step()
            if fast and 0 < v - 2 * k < GROUPS:
                step(v - 2 * k)
        else:
            pl.when((g > 0) & (g < GROUPS))(step)


def gather_drain(parts, copy):
    def body(g, _):
        for stages in parts:
            for moves in stages:
                for move in moves:
                    when(move[0], lambda move=move: copy(move, g).wait_send())
        return 0

    lax.fori_loop(0, GROUPS, body, 0)


def shift_line(table, rel, head):
    line = jnp.zeros(table.shape, F32)
    for bucket in range(rel.shape[0]):
        line = jnp.where(table == bucket, rel[bucket, head], line)
    return line


def gelu_parts(v):
    root = math.sqrt(2.0 / math.pi)
    sq = v * v
    t = jnp.tanh(root * (v + 0.044715 * (sq * v)))
    half = 0.5 * (1.0 + t)
    value = v * half
    slope = half + 0.5 * v * (1.0 - t * t) * (root * (1.0 + 3 * 0.044715 * sq))
    return value, slope


def row_norm(v):
    return lax.rsqrt(jnp.mean(v * v, axis=-1, keepdims=True) + EPS)


REACH = (4, -4)


class Halo:
    def __init__(self, here, ref, send, recv):
        self.here, self.ref, self.send, self.recv = here, ref, send, recv
        self.rows = ref.shape[-2] // 5
        even = here.x == 0
        self.even = even
        self.partner = here.me + 1 - 2 * here.c
        self.across = here.me + jnp.where(even, 2, -2)
        self.near = jnp.where(even, 4, 0)
        self.far = 4 - self.near
        step = jnp.where(even, 4, -4)
        self.to_far = inside(here.me + step, here.n)
        self.from_far = inside(here.me - step, here.n)
        self.far_device = jnp.clip(here.me + step, 0, here.n - 1)
        core0 = here.c == 0
        self.has_prev, self.has_next = here.me >= 2, here.me < here.n - 2
        self.over = jnp.where(core0, self.has_next, self.has_prev)
        self.under = jnp.where(core0, self.has_prev, self.has_next)

    def part(self, slot, piece):
        at = pl.ds(pl.multiple_of(slot * self.rows, self.rows), self.rows)
        return self.ref.at[at] if piece is None else self.ref.at[piece, at]

    def move(self, kind, piece):
        c, j = self.here.c, 0 if piece is None else piece
        src, dst, device = (
            (2, self.far, self.across),
            (self.near, self.far, self.far_device),
            (2, jnp.where(c == 0, 1, 3), self.partner),
            (jnp.where(c == 0, 4, 0), jnp.where(c == 0, 3, 1), self.partner),
        )[kind]
        return pltpu.make_async_remote_copy(
            self.part(src, piece), self.part(dst, piece), self.send.at[j, kind], self.recv.at[j, kind],
            device_id=(device,), device_id_type=MESH,
        )

    def begin(self, piece=None):
        self.move(0, piece).start()
        self.move(2, piece).start()

    def forward(self, piece=None):
        self.move(0, piece).wait_recv()
        when(self.to_far, lambda: self.move(1, piece).start())

    def spread(self, piece=None):
        when(self.from_far, lambda: self.move(1, piece).wait_recv())
        when(self.over, lambda: self.move(3, piece).start())

    def settle(self, piece=None):
        self.move(2, piece).wait_recv()
        when(self.under, lambda: self.move(3, piece).wait_recv())

    def close(self, piece=None):
        self.move(0, piece).wait_send()
        self.move(2, piece).wait_send()
        when(self.to_far, lambda: self.move(1, piece).wait_send())
        when(self.over, lambda: self.move(3, piece).wait_send())

    def absent(self):
        core0 = self.here.c == 0
        no_prev, no_next = jnp.logical_not(self.has_prev), jnp.logical_not(self.has_next)
        return ((no_prev, 0), (no_next, 4), (no_prev & core0, 1), (no_next & jnp.logical_not(core0), 3))


def forward_kernel(
    n, heads,
    slab, hid, dy, kx_own, qx, table, rel, na, nf,
    o_grads, o_outp, o_dn2p, o_x1, o_at, o_q, o_kv, o_kx, o_lse, o_ga,
    G, ga, n2f, dyf, kv, kx, qv, x1, at, lse,
    gs, gr, lsem, hs, hr, ks, kr, cs, cr, osem, stsem,
):
    here = Place(n)
    c = here.c
    rows, D = hid.shape
    inner = qv.shape[1]
    nz = here.grid[0]
    partner = here.me + 1 - 2 * c
    window = kx.shape[0]
    tiles = rows // 256
    span = (window - rows) + 256
    mine = pl.ds(pl.multiple_of(c * rows, rows), rows)
    centre = pl.ds(2 * rows, rows)

    def to_partner(src, dst, i):
        return pltpu.make_async_remote_copy(
            src, dst, cs.at[i], cr.at[i], device_id=(partner,), device_id_type=MESH
        )

    kv_halo, kx_halo = Halo(here, kv, hs, hr), Halo(here, kx, ks, kr)

    own = [
        pltpu.make_async_copy(slab.at[g], G.at[g, here.z, here.y, here.x], lsem.at[g])
        for g in range(GROUPS)
    ]
    for copy in own:
        copy.start()
    kx_in = pltpu.make_async_copy(kx_own, kx.at[centre], lsem.at[GROUPS])
    kx_in.start()
    dy_in = pltpu.make_async_copy(dy, dyf.at[mine], lsem.at[GROUPS + 1])
    dy_in.start()
    here.barrier(REACH)
    for copy in own:
        copy.wait()
    parts, copy, _ = gather_stages(here, G, gs, gr, D)
    ag = lambda v: gather_visit(parts, copy, v)
    ag(0)
    kx_in.wait()
    kx_halo.begin()
    dy_in.wait()
    dy_out = to_partner(dyf.at[mine], dyf.at[mine], 0)
    dy_out.start()
    edge = jnp.where(lax.broadcasted_iota(jnp.int32, (rows, 128), 1) == 25, -BIG, 0.0).astype(BF)
    for cond, slot in kv_halo.absent():
        def absent(slot=slot):
            at_rows = pl.ds(slot * rows, rows)
            kx[at_rows, :] = edge
            for hp in range(heads // 2):
                kv[hp, at_rows, :] = jnp.zeros((rows, 256), BF)

        pl.when(cond)(absent)

    def attention(n1, bias, vt, S, Pm):
        ag(1)

        def norm_rows(i, _):
            at_rows = pl.ds(i * 64, 64)
            v = hid[at_rows, :].astype(F32)
            n1[at_rows, :] = (v * row_norm(v) * na[...]).astype(BF)
            return 0

        lax.fori_loop(0, rows // 64, norm_rows, 0)
        ag(2)
        kx_halo.forward()
        for head in range(heads):
            line = shift_line(table[...], rel, head)
            for b in range(bias.shape[1] // 128):
                lo = line[19 - b : 20 - b, :]
                hi = line[18 - b : 19 - b, :]
                both = jnp.broadcast_to(jnp.concatenate([lo, hi], 1), (128, 256))
                bias[head, 128 * b : 128 * b + 128, :] = pltpu.roll(both, 0, 1, stride=1, stride_axis=0)[:, :128]
            if head == 1:
                ag(3)
                kx_halo.spread()
            if head == 3:
                ag(4)
                kx_halo.settle()
        ag(5)
        keep = pltpu.make_async_copy(G.at[0], ga.at[:, :, :, c], lsem.at[GROUPS + 2])
        keep.start()
        give = to_partner(G.at[0], ga.at[:, :, :, c], 1)
        give.start()
        keep.wait()
        give.wait_recv()
        ga_out = pltpu.make_async_copy(ga, o_ga, osem.at[1])
        ga_out.start()

        for part in (1, 2, 0):
            weight = ga[part].reshape(inner, D)
            for half in range(rows // 256):
                at_rows = pl.ds(256 * half, 256)
                got = nt(n1[at_rows, :], weight).astype(BF)
                if part == 0:
                    qv[at_rows, :] = got
                    continue
                for hp in range(heads // 2):
                    kv[hp, pl.ds(2 * rows + 256 * half, 256), 128 * (part - 1) : 128 * part] = got[
                        :, 128 * hp : 128 * hp + 128
                    ]
            if part == 2:
                for hp in range(heads // 2):
                    kv_halo.begin(hp)
        kx_out = pltpu.make_async_copy(kx, o_kx, osem.at[3])
        kx_out.start()
        q_out = pltpu.make_async_copy(qv, o_q, osem.at[4])
        q_out.start()
        ag(6)
        kv_halo.forward(0)
        ag(7)
        kv_halo.forward(1)
        kv_halo.spread(0)
        kv_halo.forward(2)
        kv_halo.settle(0)
        lane = lax.broadcasted_iota(jnp.int32, (256, 128), 1) // 64

        def pair(hp, _):
            @pl.when(hp > 0)
            def _():
                kv_halo.settle(hp)

            cols = pl.ds(pl.multiple_of(hp * 128, 128), 128)

            def turn(i, _):
                at_rows = pl.ds(pl.multiple_of(i * 256, 256), 256)
                vt[:, at_rows] = kv[hp, at_rows, 128:256].T
                return 0

            lax.fori_loop(0, window // 256, turn, 0)

            def one(k, _):
                @pl.when(k == 1)
                def _():
                    ag(8 + hp)

                t, e = k // 2, k % 2
                base = pl.multiple_of(t * 256, 256)
                head = hp * 2 + e
                q = qv[pl.ds(base, 256), cols]
                q = jnp.where(lane == e, q, jnp.zeros_like(q))
                qa = jnp.concatenate([q, qx[pl.ds(base, 256), :]], 1)

                def score(b, m):
                    at_rows = pl.ds(pl.multiple_of(base + b * 256, 256), 256)
                    ka = jnp.concatenate([kv[hp, at_rows, 0:128], kx[at_rows, :]], 1)
                    s = nt(ka, qa)
                    low = pl.multiple_of(b * 256, 256)
                    plane = jnp.concatenate(
                        [bias[head, pl.ds(low + 128, 256), :], bias[head, pl.ds(low, 256), :]], 1
                    )
                    s = s + plane
                    S[pl.ds(low, 256), :] = s
                    return jnp.maximum(m, jnp.max(s.reshape(32, 8, 256), axis=0))

                m = lax.fori_loop(0, span // 256, score, jnp.full((8, 256), -3e38, F32), unroll=True)
                m = jnp.max(m, axis=0, keepdims=True)

                def weigh(b, total):
                    at_rows = pl.ds(pl.multiple_of(b * 256, 256), 256)
                    p = jnp.exp(S[at_rows, :] - m)
                    Pm[at_rows, :] = p.astype(BF)
                    return total + jnp.sum(p.reshape(32, 8, 256), axis=0)

                total = lax.fori_loop(0, span // 256, weigh, jnp.zeros((8, 256), F32), unroll=True)
                total = jnp.sum(total, axis=0, keepdims=True)
                out_rows = pl.ds(pl.multiple_of(head * 64, 64), 64)
                mixed = nn(vt[pl.ds(pl.multiple_of(e * 64, 64), 64), pl.ds(base, span)], Pm[...])
                at[out_rows, pl.ds(base, 256)] = mixed / total
                lse[pl.ds(head, 1), pl.ds(base, 256)] = m + jnp.log(total)
                return 0

            lax.fori_loop(0, 2 * tiles, one, 0)

            @pl.when(hp < heads // 2 - 1)
            def _():
                kv_halo.spread(hp + 1)

            return 0

        lax.fori_loop(0, heads // 2, pair, 0)
        kv_out = pltpu.make_async_copy(kv, o_kv, osem.at[2])
        kv_out.start()
        outs = [
            pltpu.make_async_copy(at, o_at, osem.at[5]),
            pltpu.make_async_copy(lse, o_lse, osem.at[6]),
        ]
        for o in outs:
            o.start()
        w_out = ga[3].reshape(inner, D)

        def after(i, _):
            at_rows = pl.ds(pl.multiple_of(i * 128, 128), 128)
            a = at[:, at_rows].T.astype(BF)
            v = hid[at_rows, :].astype(F32) + nn(a, w_out)
            x1[at_rows, :] = v
            n2f[pl.ds(pl.multiple_of(c * rows + i * 128, 128), 128), :] = (v * row_norm(v) * nf[...]).astype(BF)
            return 0

        lax.fori_loop(0, rows // 128, after, 0)
        n2_out = to_partner(n2f.at[mine], n2f.at[mine], 2)
        n2_out.start()
        x1_out = pltpu.make_async_copy(x1, o_x1, osem.at[7])
        x1_out.start()
        give.wait_send()
        n2_out.wait()
        dy_out.wait()
        kx_halo.close()
        for hp in range(heads // 2):
            kv_halo.close(hp)
        for o in outs + [ga_out, kv_out, kx_out, q_out, x1_out]:
            o.wait()

    pl.run_scoped(
        attention,
        pltpu.VMEM((rows, D), BF),
        pltpu.VMEM((heads, span + 128, 128), F32),
        pltpu.VMEM((128, window), BF),
        pltpu.VMEM((span, 256), F32),
        pltpu.VMEM((span, 256), BF),
    )

    def feed(acc_o, acc_n, ft, gt, ut, stage):
        acc_o[...] = jnp.zeros_like(acc_o)
        acc_n[...] = jnp.zeros_like(acc_n)

        def stage_out(j):
            return pltpu.make_async_copy(stage.at[j % 2], o_grads.at[j + 1], stsem.at[j % 2])

        def chunk(j, _):
            ag(j + 11)
            g = j + 1
            wg = G.at[g, :, :, :, pl.ds(0, 16), :]
            wu = G.at[g, :, :, :, pl.ds(16, 16), :]
            wd = G.at[g, :, :, :, pl.ds(32, 16), :]
            whole = lambda ref: ref[...].reshape(256, D)

            def tokens(i, _):
                at_rows = pl.ds(pl.multiple_of(i * 256, 256), 256)
                n2 = n2f[at_rows, :]
                gate = nt(whole(wg), n2)
                up = nt(whole(wu), n2)
                df = nt(whole(wd), dyf[at_rows, :])
                value, slope = gelu_parts(gate)
                f = (value * up).astype(BF)
                dg = (df * up * slope).astype(BF)
                du = (df * value).astype(BF)
                ft[:, at_rows] = f
                gt[:, at_rows] = dg
                ut[:, at_rows] = du
                acc_o[at_rows, :] += nn(f.T, whole(wd))
                acc_n[at_rows, :] += nn(dg.T, whole(wg)) + nn(du.T, whole(wu))
                return 0

            lax.fori_loop(0, 2 * rows // 256, tokens, 0, unroll=2)

            @pl.when(j >= 2)
            def _():
                stage_out(j - 2).wait()

            s = j % 2
            stage[s, :, :, :, 0:16, :] = nn(gt[...], n2f[...]).astype(BF).reshape(here.grid + (16, D))
            stage[s, :, :, :, 16:32, :] = nn(ut[...], n2f[...]).astype(BF).reshape(here.grid + (16, D))
            stage[s, :, :, :, 32:48, :] = nn(ft[...], dyf[...]).astype(BF).reshape(here.grid + (16, D))
            stage_out(j).start()
            return 0

        lax.fori_loop(0, GROUPS - 1, chunk, 0)
        outs = [
            pltpu.make_async_copy(acc_o, o_outp, osem.at[0]),
            pltpu.make_async_copy(acc_n, o_dn2p, osem.at[1]),
        ]
        for o in outs:
            o.start()
        gather_drain(parts, copy)
        for o in outs:
            o.wait()
        stage_out(GROUPS - 3).wait()
        stage_out(GROUPS - 2).wait()

    pl.run_scoped(
        feed,
        pltpu.VMEM((2 * rows, D), F32),
        pltpu.VMEM((2 * rows, D), F32),
        pltpu.VMEM((256, 2 * rows), BF),
        pltpu.VMEM((256, 2 * rows), BF),
        pltpu.VMEM((256, 2 * rows), BF),
        pltpu.VMEM((2,) + here.grid + (PIECE, D), BF),
    )


def forward_call(n, heads, slab, hid, dy, kx_own, qx, table, rel, na, nf):
    rows, D = hid.shape
    inner = heads * 64
    zs, ys, xs = GRIDS[n]
    window = 5 * rows
    span = window - rows + 256
    shape = jax.ShapeDtypeStruct
    any_, vm = pl.BlockSpec(memory_space=pl.ANY), pl.BlockSpec(memory_space=pltpu.VMEM)
    sm = pl.BlockSpec(memory_space=pltpu.SMEM)
    slots = 3 * 8
    dma = pltpu.SemaphoreType.DMA
    return pl.pallas_call(
        functools.partial(forward_kernel, n, heads),
        out_shape=(
            shape((GROUPS, zs, ys, xs, PIECE, D), BF),
            shape((2 * rows, D), F32),
            shape((2 * rows, D), F32),
            shape((rows, D), F32),
            shape((inner, rows), F32),
            shape((rows, inner), BF),
            shape((heads // 2, window, 256), BF),
            shape((window, 128), BF),
            shape((8, rows), F32),
            shape((zs, ys, xs, 2, PIECE, D), BF),
        ),
        in_specs=[any_, vm, any_, any_, vm, vm, sm, vm, vm],
        out_specs=(any_,) * 10,
        scratch_shapes=[
            pltpu.VMEM((GROUPS, zs, ys, xs, PIECE, D), BF),
            pltpu.VMEM((zs, ys, xs, 2, PIECE, D), BF),
            pltpu.VMEM((2 * rows, D), BF),
            pltpu.VMEM((2 * rows, D), BF),
            pltpu.VMEM((heads // 2, window, 256), BF),
            pltpu.VMEM((window, 128), BF),
            pltpu.VMEM((rows, inner), BF),
            pltpu.VMEM((rows, D), F32),
            pltpu.VMEM((inner, rows), F32),
            pltpu.VMEM((8, rows), F32),
            dma((GROUPS, slots)), dma((GROUPS, slots)),
            dma((GROUPS + 3,)),
            dma((heads // 2, 4)), dma((heads // 2, 4)), dma((1, 4)), dma((1, 4)),
            dma((3,)), dma((3,)),
            dma((8,)), dma((2,)),
        ],
        compiler_params=pltpu.CompilerParams(
            collective_id=1, has_side_effects=True, vmem_limit_bytes=63 * 2**20
        ),
        cost_estimate=pl.CostEstimate(flops=55 * 10**9, bytes_accessed=80 * 10**6, transcendentals=10**7),
        name="forward",
    )(slab, hid, dy, kx_own, qx, table, rel, na, nf)


def prepare(hidden, segments, delete_mask, bucket_table, attn_weight, gate_weight, up_weight, down_weight):
    D = hidden.shape[1]
    rows = hidden.shape[0]
    groups = GROUPS - 1
    ffn = jnp.stack([gate_weight.T, up_weight.T, down_weight]).reshape(3, groups, 16, D)
    ffn = jnp.transpose(ffn, (1, 0, 2, 3)).reshape(groups, PIECE, D)
    slab = jnp.concatenate([attn_weight.T[None], ffn], 0)
    lane = jnp.arange(128, dtype=jnp.int32)[None, :]
    seg = segments[:, None]
    digit = jnp.where(lane < 9, seg % 8, jnp.where(lane < 17, (seg // 8) % 8, seg // 64))
    hit = digit == (lane - 1) % 8
    coded = (lane >= 1) & (lane < 25)
    kx = jnp.where(lane == 0, delete_mask.astype(F32)[:, None], jnp.where(coded & ~hit, -BIG, 0.0)).astype(BF)
    qx = jnp.where((lane == 0) | (lane == 25) | (coded & hit), 1.0, 0.0).astype(BF)
    reach = bucket_table.shape[0]
    table = jnp.pad(jnp.flip(bucket_table), (257, 20 * 128 - 257 - reach), constant_values=-1).reshape(20, 128)
    table = jnp.pad(table, ((0, 4), (0, 0)), constant_values=-1)
    return slab, kx, qx, table


FIRST = (1, 2, 3, 4, 5, 6, 7, 0)
AT = 7
AFTER = 11
SLOTS = 4
ZSLOTS = 6
WORK = 8
LINES = 56


def group_of(pos):
    if isinstance(pos, int):
        return FIRST[pos]
    return (pos + 1) % GROUPS


def add_into(dst, src):
    dst[...] = (dst[...].astype(F32) + src[...].astype(F32)).astype(BF)


class Scatter:
    def __init__(self, here, source, work, land, landa, landz, result, send, recv, load, width):
        self.here, self.source, self.work, self.result = here, source, work, result
        self.land, self.landa, self.landz = land, landa, landz
        self.send, self.recv, self.load = send, recv, load
        self.parts = column_parts(width)

    def loading(self, part, pos):
        here = self.here
        zs, ys, xs = here.grid
        in_y = pl.ds(here.y, 1) if part == 1 else pl.ds(0, ys)
        in_x = pl.ds(here.x, 1) if part == 2 else pl.ds(0, xs)
        cols = pl.ds(*self.parts[part])
        return pltpu.make_async_copy(
            self.source.at[group_of(pos), :, in_y, in_x, :, cols],
            self.work.at[pos % WORK, :, in_y, in_x, :, cols],
            self.load.at[pos, part],
        )

    def start_load(self, pos):
        for part in range(3):
            self.loading(part, pos).start()

    def moves(self, part, k, pos):
        here = self.here
        zs, ys, xs = here.grid
        z, y, x = here.z, here.y, here.x
        cols = pl.ds(*self.parts[part])
        dim = (("z0", "z1", "z2", "y", "x"), ("y", "x", "z0", "z1", "z2"), ("x", "y", "z0", "z1", "z2"))[part][k]
        work, source, g = self.work, self.source, group_of(pos)
        w, slot, zslot = pos % WORK, pos % SLOTS, pos % ZSLOTS
        base = 8 * part

        def remote(src, dst, at, device):
            return pltpu.make_async_remote_copy(
                src, dst, self.send.at[pos, at], self.recv.at[pos, at], device_id=(device,), device_id_type=MESH
            )

        if dim[0] == "z":
            step = int(dim[1])
            out = []
            for turn, way in enumerate((1, -1)):
                target = z + way * (zs - 1 - step)
                got = z + way * (zs - 2 - step)
                sends = inside(z + way, zs) & inside(target, zs)
                gets = inside(z - way, zs) & inside(got, zs)
                spot = step if turn == 0 or step == 0 else step + 2
                device = here.dev(jnp.clip(z + way, 0, zs - 1), y, x)
                block, mine = jnp.clip(target, 0, zs - 1), jnp.clip(got, 0, zs - 1)
                if part == 0:
                    src, dst = work.at[w, block, :, :, :, cols], self.landa.at[zslot, spot]
                else:
                    src, dst = work.at[w, block, y, x, :, cols], self.landz.at[zslot, spot, :, cols]

                def consume(mine=mine, dst=dst):
                    if part == 0:
                        for b in range(ys):
                            add_into(work.at[w, mine, b, :, :, cols], dst.at[b])
                    elif step < zs - 2:
                        add_into(work.at[w, mine, y, x, :, cols], dst)

                out.append((sends, gets, remote(src, dst, base + 2 + 2 * step + turn, device), consume))
            return out
        at = base + (0 if dim == "y" else 1)
        device = here.dev(z, 1 - y, x) if dim == "y" else here.dev(z, y, 1 - x)
        if k == 0 and dim == "y":
            src = source.at[g, :, pl.ds(1 - y, 1), :, :, cols]
            dst = work.at[w, :, pl.ds(y, 1), :, :, cols]
            pairs = [(work.at[w, b, y, :, :, cols], work.at[w, b, 1 - y, :, :, cols]) for b in range(zs)]
        elif k == 0:
            src = source.at[g, :, :, pl.ds(1 - x, 1), :, cols]
            dst = work.at[w, :, :, pl.ds(x, 1), :, cols]
            pairs = [(work.at[w, b, :, x, :, cols], work.at[w, b, :, 1 - x, :, cols]) for b in range(zs)]
        elif part != 0:
            src = work.at[w, :, y, 1 - x, :, cols] if dim == "x" else work.at[w, :, 1 - y, x, :, cols]
            dst = self.land.at[slot, :, :, cols]
            pairs = [(work.at[w, b, y, x, :, cols], self.land.at[slot, b, :, cols]) for b in range(zs)]
        elif dim == "y":
            src = work.at[w, z, 1 - y, :, :, cols]
            dst = self.land.at[slot, pl.ds(0, xs), :, cols]
            pairs = [(work.at[w, z, y, b, :, cols], self.land.at[slot, b, :, cols]) for b in range(xs)]
        else:
            src = work.at[w, z, y, 1 - x, :, cols]
            dst = self.land.at[slot, xs, :, cols]
            pairs = []

        def consume():
            for to, frm in pairs:
                add_into(to, frm)

        return [(None, None, remote(src, dst, at, device), consume)]

    def finish(self, part, pos):
        here = self.here
        zs, ys, xs = here.grid
        z, y, x = here.z, here.y, here.x
        slot, g = pos % SLOTS, group_of(pos)
        first, wide = self.parts[part]
        cols = pl.ds(first, wide)
        own = self.work[pos % WORK, z, y, x, :, cols].astype(F32)
        if part == 0:
            self.result[g, :, cols] = own + self.land[slot, xs, :, cols].astype(F32)
            return
        up = self.landz[pos % ZSLOTS, zs - 2, :, cols].astype(F32)
        down = self.landz[pos % ZSLOTS, zs, :, cols].astype(F32)
        self.result[g, :, cols] = own + jnp.where(z > 0, up, 0.0) + jnp.where(z < zs - 1, down, 0.0)

    def round(self, r):
        for k in range(STAGES, -1, -1):
            pos = r - 2 * k

            def step(pos=pos, k=k):
                for part in range(3):
                    if k == (0 if part == 0 else 1):
                        self.loading(part, pos).wait()
                    if k > 0:
                        for _, gets, copy, consume in self.moves(part, k - 1, pos):
                            def take(copy=copy, consume=consume):
                                copy.wait_recv()
                                consume()

                            when(gets, take)
                    if k < STAGES:
                        for sends, _, copy, _ in self.moves(part, k, pos):
                            when(sends, lambda copy=copy: copy.start())
                        continue
                    self.finish(part, pos)
                    for stage in range(STAGES):
                        for sends, _, copy, _ in self.moves(part, stage, pos):
                            when(sends, lambda copy=copy: copy.wait_send())

            if isinstance(pos, int):
                if 0 <= pos < GROUPS - 1:
                    step()
            else:
                pl.when(inside(pos, GROUPS - 1))(step)
            if isinstance(r, int) and r - AFTER == k:
                step(AT, k)


def norm_back(v, gain, d):
    r = row_norm(v)
    vr = v * r
    dg = d * gain
    return r * (dg - vr * jnp.mean(vr * dg, axis=-1, keepdims=True)), d * vr


def put_line(small, first, line):
    width = line.shape[1]
    for i in range(-(-width // 128)):
        wide = min(128, width - 128 * i)
        small[first + i : first + i + 1, 0:wide] = line[:, 128 * i : 128 * i + wide]


def backward_kernel(
    n, heads,
    grads, outp, dn2p, x1_in, at_in, q_in, kv_in, kx_in, lse, ga_in,
    hid, dy, qx, table, rel, na, nf,
    gr, o_out, o_dh, o_res, o_small, dn_land, op_land,
    work, land, landa, landz, res, dx1, kv, kx, qv, at, ga, dat, das, back, fold, small, sland,
    ss, rs, lds, cs, cr, hs, hr, ls, ps, pr, osem,
):
    here = Place(n)
    c = here.c
    rows, D = dx1.shape
    inner = qv.shape[1]
    window = kx.shape[0]
    zs, ys, xs = here.grid
    z, y, x = here.z, here.y, here.x
    span = window - rows + 256
    partner = here.me + 1 - 2 * c
    mine = pl.ds(pl.multiple_of(c * rows, rows), rows)
    theirs = pl.ds(pl.multiple_of((1 - c) * rows, rows), rows)

    def to_partner(src, dst, i):
        return pltpu.make_async_remote_copy(
            src, dst, cs.at[i], cr.at[i], device_id=(partner,), device_id_type=MESH
        )

    def local(src, dst, i):
        return pltpu.make_async_copy(src, dst, ls.at[i])

    sc = Scatter(here, gr, work, land, landa, landz, res, ss, rs, lds, D)
    for pos in range(WORK):
        if pos != AT:
            sc.start_load(pos)
    loads = [
        local(dn2p.at[mine], dx1, 0), local(kv_in, kv, 1), local(kx_in, kx, 2),
        local(q_in, qv, 3), local(at_in, at, 4), local(ga_in, ga, 5),
    ]
    for load in loads:
        load.start()
    here.barrier(REACH, True)
    dn_out = to_partner(dn2p.at[theirs], dn_land, 0)
    dn_out.start()
    sc.round(0)
    op_out = to_partner(outp.at[theirs], op_land, 1)
    op_out.start()
    small[...] = jnp.zeros_like(small)

    def after_ffn(x1, other, grad, low):
        first = [local(x1_in, x1, 6), local(dy, grad, 7)]
        for load in first:
            load.start()
        dn_out.wait_recv()
        second = local(dn_land, other, 8)
        second.start()
        sc.round(1)
        for load in loads + first + [second]:
            load.wait()
        w_out = ga[zs - 1].reshape(inner, D)

        def through(i, total):
            at_rows = pl.ds(pl.multiple_of(i * 128, 128), 128)
            d = dx1[at_rows, :] + other[at_rows, :]
            back_v, gain_d = norm_back(x1[at_rows, :], nf[...], d)
            v = grad[at_rows, :].astype(F32) + back_v
            dx1[at_rows, :] = v
            v = v.astype(BF)
            low[at_rows, :] = v
            da = nt(v, w_out).astype(BF)
            das[at_rows, :] = da
            dat[:, at_rows] = da.T
            return total + jnp.sum(gain_d.reshape(16, 8, D), axis=0)

        total = lax.fori_loop(0, rows // 128, through, jnp.zeros((8, D), F32))
        put_line(small, 44, jnp.sum(total, axis=0, keepdims=True))
        third = local(outp.at[mine], other, 9)
        third.start()
        sc.round(2)
        for h in range(2):
            part = nn(at[pl.ds(h * (inner // 2), inner // 2), :].astype(BF), low[...])
            ga[zs - 1, h] = part.astype(BF).reshape(xs, 2, PIECE, D)
        third.wait()
        op_out.wait_recv()

        def add(i, _):
            at_rows = pl.ds(pl.multiple_of(i * 64, 64), 64)
            x1[at_rows, :] = x1[at_rows, :] + other[at_rows, :]
            return 0

        lax.fori_loop(0, rows // 64, add, 0)
        fourth = local(op_land, other, 10)
        fourth.start()
        fourth.wait()

        def put(i, _):
            at_rows = pl.ds(pl.multiple_of(i * 64, 64), 64)
            low[at_rows, :] = (x1[at_rows, :] + other[at_rows, :]).astype(BF)
            return 0

        lax.fori_loop(0, rows // 64, put, 0)
        out = pltpu.make_async_copy(low, o_out, osem.at[0])
        out.start()
        out.wait()
        dn_out.wait_send()
        op_out.wait_send()

    pl.run_scoped(
        after_ffn, pltpu.VMEM((rows, D), F32), pltpu.VMEM((rows, D), F32), pltpu.VMEM((rows, D), BF),
        pltpu.VMEM((rows, D), BF),
    )

    way = Halo(here, kx, hs, hr)

    def home(dkv, hp, kind):
        src, device = (
            (jnp.where(c == 0, 1, 3), partner),
            (jnp.where(c == 0, 3, 1), partner),
            (way.far, jnp.clip(here.me - jnp.where(way.even, 4, -4), 0, n - 1)),
            (way.near, way.across),
        )[kind]
        return pltpu.make_async_remote_copy(
            dkv.at[hp, pl.ds(pl.multiple_of(src * rows, rows), rows)],
            back.at[hp, kind],
            hs.at[hp, kind],
            hr.at[hp, kind],
            device_id=(device,),
            device_id_type=MESH,
        )

    def add_back(dkv, hp, kind, slot):
        at_rows = pl.ds(pl.multiple_of(slot * rows, rows), rows)
        add_into(dkv.at[hp, at_rows], back.at[hp, kind])

    def home_begin(dkv, hp):
        when(way.under, lambda: home(dkv, hp, 0).start())
        home(dkv, hp, 1).start()

    def home_merge(dkv, hp):
        def merge():
            home(dkv, hp, 0).wait_recv()
            add_back(dkv, hp, 0, jnp.where(c == 0, 4, 0))

        when(way.over, merge)
        when(way.from_far, lambda: home(dkv, hp, 2).start())

    def home_cross(dkv, hp):
        def merge():
            home(dkv, hp, 2).wait_recv()
            add_back(dkv, hp, 2, way.near)

        when(way.to_far, merge)
        home(dkv, hp, 3).start()

    def home_close(dkv, hp):
        when(way.under, lambda: home(dkv, hp, 0).wait_send())
        home(dkv, hp, 1).wait_send()
        when(way.from_far, lambda: home(dkv, hp, 2).wait_send())
        home(dkv, hp, 3).wait_send()

    def pairs(dkv, dqt, acc_k, acc_v, skew, kt, bias):
        dqt[...] = jnp.zeros_like(dqt)
        lane = lax.broadcasted_iota(jnp.int32, (256, 128), 1) // 64
        lane_of = lax.broadcasted_iota(jnp.int32, (32, 128), 1)
        blocks = skew.shape[0] // 128

        def one_head(hp, e):
            head = hp * 2 + e
            pl.when(e == 0)(lambda: sc.round(3 + hp))
            cols = pl.ds(pl.multiple_of(hp * 128, 128), 128)
            out_rows = pl.ds(pl.multiple_of(head * 64, 64), 64)
            line = shift_line(table[...], rel, head)
            for b in range(blocks):
                both = jnp.concatenate([line[19 - b : 20 - b, :], line[18 - b : 19 - b, :]], 1)
                both = jnp.broadcast_to(both, (128, 256))
                bias[128 * b : 128 * b + 128, :] = pltpu.roll(both, 0, 1, stride=1, stride_axis=0)[:, :128]
            skew[...] = jnp.zeros_like(skew)

            def tile(t, _):
                base = pl.multiple_of(t * 256, 256)
                here_q = pl.ds(base, 256)
                q = qv[here_q, cols]
                q = jnp.where(lane == e, q, jnp.zeros_like(q))
                qa = jnp.concatenate([q, qx[here_q, :]], 1)
                da = das[here_q, cols]
                da = jnp.where(lane == e, da, jnp.zeros_like(da))
                logs = lse[pl.ds(head, 1), here_q]
                delta = jnp.sum(dat[out_rows, here_q].astype(F32) * at[out_rows, here_q], axis=0, keepdims=True)

                def block(b, dq):
                    low = pl.multiple_of(b * 256, 256)
                    at_rows = pl.ds(pl.multiple_of(base + b * 256, 256), 256)
                    ka = jnp.concatenate([kv[hp, at_rows, 0:128], kx[at_rows, :]], 1)
                    plane = jnp.concatenate([bias[pl.ds(low + 128, 256), :], bias[pl.ds(low, 256), :]], 1)
                    p = jnp.exp(nt(ka, qa) + plane - logs)
                    ds = p * (nt(kv[hp, at_rows, 128:256], da) - delta)
                    skew[pl.ds(low + 128, 256), :] += ds[:, 0:128]
                    skew[pl.ds(low, 256), :] += ds[:, 128:256]
                    dsr = ds.astype(BF)
                    acc_v[at_rows, :] += nn(p.astype(BF), da)
                    acc_k[at_rows, :] += nn(dsr, q)
                    return dq + nn(kt[pl.ds(pl.multiple_of(e * 64, 64), 64), at_rows], dsr)

                dqt[out_rows, here_q] = lax.fori_loop(0, span // 256, block, jnp.zeros((64, 256), F32), unroll=True)
                return 0

            lax.fori_loop(0, rows // 256, tile, 0)
            tail = [None] * (blocks + 1)
            for b in range(blocks):
                a = jnp.concatenate([skew[128 * b : 128 * b + 128, :], jnp.zeros((128, 128), F32)], 1)
                half = 64
                while half >= 1:
                    a = a[0:half] + pltpu.roll(a[half : 2 * half], 256 - half, 1)
                    half //= 2
                for at_line, part in ((19 - b, a[:, 0:128]), (18 - b, a[:, 128:256])):
                    tail[at_line] = part if tail[at_line] is None else tail[at_line] + part
            line_d = jnp.concatenate(tail + [jnp.zeros((4, 128), F32)], 0)
            sums = [
                jnp.sum(jnp.where(table[...] == b, line_d, 0.0), axis=0, keepdims=True) for b in range(rel.shape[0])
            ]
            sums = jnp.sum(jnp.concatenate(sums, 0), axis=1, keepdims=True)
            small[0:32, :] = jnp.where(lane_of == head, sums, small[0:32, :])

        def pair(hp, _):
            acc_k[...] = jnp.zeros_like(acc_k)
            acc_v[...] = jnp.zeros_like(acc_v)

            def turn(i, _):
                at_rows = pl.ds(pl.multiple_of(i * 256, 256), 256)
                kt[:, at_rows] = kv[hp, at_rows, 0:128].T
                return 0

            lax.fori_loop(0, window // 256, turn, 0)
            lax.fori_loop(0, 2, lambda e, _: (one_head(hp, e), 0)[1], 0)

            def pack(i, _):
                at_rows = pl.ds(pl.multiple_of(i * 128, 128), 128)
                dkv[hp, at_rows, 0:128] = acc_k[at_rows, :].astype(BF)
                dkv[hp, at_rows, 128:256] = acc_v[at_rows, :].astype(BF)
                return 0

            lax.fori_loop(0, window // 128, pack, 0)
            home_begin(dkv, hp)
            pl.when(hp >= 1)(lambda: home_merge(dkv, hp - 1))
            pl.when(hp >= 2)(lambda: home_cross(dkv, hp - 2))
            return 0

        lax.fori_loop(0, heads // 2, pair, 0)
        last = heads // 2 - 1
        home_cross(dkv, last - 1)
        home_merge(dkv, last)
        sc.round(6)

    def to_weights(dkv, dqt, n1, proj, proj_t, hid_v):
        hid_in = local(hid, hid_v, 11)
        hid_in.start()
        hid_in.wait()

        def norm_rows(i, _):
            at_rows = pl.ds(pl.multiple_of(i * 64, 64), 64)
            v = hid_v[at_rows, :].astype(F32)
            n1[at_rows, :] = (v * row_norm(v) * na[...]).astype(BF)
            return 0

        lax.fori_loop(0, rows // 64, norm_rows, 0)

        def gather_pair(hp, _):
            home(dkv, hp, 1).wait_recv()
            home(dkv, hp, 3).wait_recv()

            def sum_rows(j, _):
                at_rows = pl.ds(pl.multiple_of(j * 128, 128), 128)
                total = dkv[hp, pl.ds(pl.multiple_of(2 * rows + j * 128, 128), 128), :].astype(F32)
                for i in (1, 3):
                    total = total + back[hp, i, at_rows, :].astype(F32)
                total = total.astype(BF)
                for part in range(2):
                    piece = total[:, 128 * part : 128 * part + 128]
                    to = pl.ds(pl.multiple_of((1 + part) * inner + hp * 128, 128), 128)
                    proj[at_rows, to] = piece
                    proj_t[to, at_rows] = piece.T
                to = pl.ds(pl.multiple_of(hp * 128, 128), 128)
                piece = dqt[to, at_rows].astype(BF)
                proj_t[to, at_rows] = piece
                proj[at_rows, to] = piece.T
                return 0

            lax.fori_loop(0, rows // 128, sum_rows, 0)
            return 0

        last = heads // 2 - 1
        sc.round(7)
        lax.fori_loop(0, last, gather_pair, 0)
        home_cross(dkv, last)
        sc.round(8)
        gather_pair(last, 0)

        def to_hidden(i, total):
            at_rows = pl.ds(pl.multiple_of(i * 128, 128), 128)
            d = nn(proj[at_rows, 0:inner], ga[0].reshape(inner, D))
            d = d + nn(proj[at_rows, inner : 2 * inner], ga[1].reshape(inner, D))
            d = d + nn(proj[at_rows, 2 * inner : 3 * inner], ga[2].reshape(inner, D))
            back_v, gain_d = norm_back(hid_v[at_rows, :].astype(F32), na[...], d)
            dx1[at_rows, :] = dx1[at_rows, :] + back_v
            return total + jnp.sum(gain_d.reshape(16, 8, D), axis=0)

        total = lax.fori_loop(0, rows // 128, to_hidden, jnp.zeros((8, D), F32))
        put_line(small, 32, jnp.sum(total, axis=0, keepdims=True))
        dh_out = pltpu.make_async_copy(dx1, o_dh, osem.at[1])
        dh_out.start()
        sc.round(9)

        for part in range(3):
            for h in range(2):
                take = pl.ds(part * inner + h * (inner // 2), inner // 2)
                ga[part, h] = nn(proj_t[take, :], n1[...]).astype(BF).reshape(xs, 2, PIECE, D)
        for hp in range(heads // 2):
            home_close(dkv, hp)
        dh_out.wait()

    def attention(dkv, dqt):
        pl.run_scoped(
            functools.partial(pairs, dkv, dqt),
            pltpu.VMEM((window, 128), F32), pltpu.VMEM((window, 128), F32), pltpu.VMEM((span + 128, 128), F32),
            pltpu.VMEM((128, window), BF), pltpu.VMEM((span + 128, 128), F32),
        )
        pl.run_scoped(
            functools.partial(to_weights, dkv, dqt),
            pltpu.VMEM((rows, D), BF), pltpu.VMEM((rows, 3 * inner), BF), pltpu.VMEM((3 * inner, rows), BF),
            pltpu.VMEM((rows, D), BF),
        )

    pl.run_scoped(attention, pltpu.VMEM((heads // 2, window, 256), BF), pltpu.VMEM((inner, rows), F32))

    fold_out = to_partner(ga.at[:, :, :, 1 - c], fold, 2)
    fold_out.start()
    def small_to(src, slot, device, i):
        return pltpu.make_async_remote_copy(
            src, sland.at[slot], ps.at[i], pr.at[i], device_id=(device,), device_id_type=MESH
        )

    swap = small_to(small, 0, partner, 0)
    swap.start()
    sc.round(10)
    fold_out.wait()
    for a in range(zs):
        for b in range(ys):
            add_into(fold.at[a, b], ga.at[a, b, :, c])
    fold_in = pltpu.make_async_copy(fold, gr.at[0], osem.at[2])
    fold_in.start()
    fold_in.wait()
    sc.start_load(AT)
    sc.round(11)
    swap.wait()
    small[...] = small[...] + sland[0]
    swap = small_to(small, 1, here.dev(z, y, 1 - x), 1)
    swap.start()
    sc.round(12)
    swap.wait()
    small[...] = small[...] + sland[1]
    swap = small_to(small, 2, here.dev(z, 1 - y, x), 2)
    swap.start()
    sc.round(13)
    swap.wait()
    small[...] = small[...] + sland[2]
    swaps = []
    for far in range(1, zs):
        swaps.append(small_to(small, 3 + far, here.dev((z + far) % zs, y, x), 2 + far))
        swaps[-1].start()
    sc.round(14)
    for swap in swaps:
        swap.wait()
    sland[3] = small[...]
    ordered = jnp.zeros(small.shape, F32)
    for plane in range(zs):
        ordered = ordered + sland[3 + (z - plane + zs) % zs]
    small[...] = ordered
    small_out = pltpu.make_async_copy(small, o_small, osem.at[3])
    small_out.start()
    for r in range(15, GROUPS - 1 + 2 * STAGES):
        sc.round(r)
    res_out = pltpu.make_async_copy(res, o_res, osem.at[4])
    res_out.start()
    res_out.wait()
    small_out.wait()


def backward_call(n, heads, kept, hid, dy, qx, table, rel, na, nf):
    grads, outp, dn2p, x1, at, q, kv, kx, lse, ga = kept
    rows, D = hid.shape
    inner = heads * 64
    zs, ys, xs = GRIDS[n]
    window = 5 * rows
    shape = jax.ShapeDtypeStruct
    any_, vm = pl.BlockSpec(memory_space=pl.ANY), pl.BlockSpec(memory_space=pltpu.VMEM)
    sm = pl.BlockSpec(memory_space=pltpu.SMEM)
    dma = pltpu.SemaphoreType.DMA
    return pl.pallas_call(
        functools.partial(backward_kernel, n, heads),
        out_shape=(
            shape(grads.shape, BF),
            shape((rows, D), BF),
            shape((rows, D), F32),
            shape((GROUPS, PIECE, D), F32),
            shape((LINES, 128), F32),
            shape((rows, D), F32),
            shape((rows, D), F32),
        ),
        in_specs=[any_] * 8 + [vm] + [any_] * 3 + [vm, vm, sm, vm, vm],
        out_specs=(any_,) * 7,
        input_output_aliases={0: 0},
        scratch_shapes=[
            pltpu.VMEM((WORK, zs, ys, xs, PIECE, D), BF),
            pltpu.VMEM((SLOTS, zs, PIECE, D), BF),
            pltpu.VMEM((ZSLOTS, 5, ys, xs, PIECE, 384), BF),
            pltpu.VMEM((ZSLOTS, 5, PIECE, D), BF),
            pltpu.VMEM((GROUPS, PIECE, D), F32),
            pltpu.VMEM((rows, D), F32),
            pltpu.VMEM((heads // 2, window, 256), BF),
            pltpu.VMEM((window, 128), BF),
            pltpu.VMEM((rows, inner), BF),
            pltpu.VMEM((inner, rows), F32),
            pltpu.VMEM((zs, ys, xs, 2, PIECE, D), BF),
            pltpu.VMEM((inner, rows), BF),
            pltpu.VMEM((rows, inner), BF),
            pltpu.VMEM((heads // 2, 4, rows, 256), BF),
            pltpu.VMEM((zs, ys, xs, PIECE, D), BF),
            pltpu.VMEM((LINES, 128), F32),
            pltpu.VMEM((3 + zs, LINES, 128), F32),
            dma((GROUPS, 24)), dma((GROUPS, 24)), dma((GROUPS, 3)),
            dma((3,)), dma((3,)),
            dma((heads // 2, 4)), dma((heads // 2, 4)),
            dma((12,)),
            dma((3 + zs,)), dma((3 + zs,)),
            dma((5,)),
        ],
        compiler_params=pltpu.CompilerParams(
            collective_id=2, has_side_effects=True, vmem_limit_bytes=63 * 2**20
        ),
        cost_estimate=pl.CostEstimate(flops=12 * 10**9, bytes_accessed=60 * 10**6, transcendentals=10**7),
        name="backward",
    )(grads, outp, dn2p, x1, at, q, kv, kx, lse, ga, hid, dy, qx, table, rel, na, nf)


def shards(
    n, hidden, segments, delete_mask, bucket_table, attn_weight, gate_weight, up_weight, down_weight,
    norm_attn, norm_ffn, rel_bias, out_grad,
):
    heads = rel_bias.shape[1]
    D = hidden.shape[1]
    slab, kx, qx, table = prepare(
        hidden, segments, delete_mask, bucket_table, attn_weight, gate_weight, up_weight, down_weight
    )
    na, nf = norm_attn[None], norm_ffn[None]
    kept = forward_call(n, heads, slab, hidden, out_grad, kx, qx, table, rel_bias, na, nf)
    _, output, d_hidden, res, small, _, _ = backward_call(
        n, heads, kept, hidden, out_grad, qx, table, rel_bias, na, nf
    )
    ffn = res[1:].reshape(GROUPS - 1, 3, 16, D)
    mats = [ffn[:, i].reshape(-1, D) for i in range(3)]
    line = lambda first: small[first : first + 12].reshape(-1)[:D]
    return (
        output, d_hidden, res[0].T, mats[0].T, mats[1].T, mats[2], line(32), line(44), small[:32, :heads],
    )


def shifted(x, axis, by):
    count = lax.axis_size(axis)
    pairs = [(i, i + by) for i in range(count) if 0 <= i + by < count]
    return lax.ppermute(x, axis, pairs)


def shortened(x):

    def short(part):
        return part.astype(jnp.bfloat16) if part.dtype == jnp.float32 else part

    return jax.tree.map(short, x)


def rms_norm(value, gain):
    return value * lax.rsqrt(jnp.mean(value * value, axis=-1, keepdims=True) + 1e-06) * gain


def matmul(left, right):
    return jnp.dot(left, right, preferred_element_type=jnp.float32)


def matmul_tn(left, right):
    return lax.dot_general(
        left, right, (((0,), (0,)), ((), ())), preferred_element_type=jnp.float32
    )


def matmul_nt(left, right):
    return lax.dot_general(
        left, right, (((1,), (1,)), ((), ())), preferred_element_type=jnp.float32
    )


def gated_unit(gate_in, up_in):
    return jax.nn.gelu(gate_in) * up_in


def toeplitz(line, row_count, window):
    span_len = line.shape[0]
    tiled = jnp.tile(line, row_count)[: row_count * (span_len - 1)].reshape(row_count, span_len - 1)
    return tiled[:, :window]


def diagonal_sums(plane, span_len):
    row_count, window = plane.shape
    padded = jnp.pad(plane, ((0, 0), (0, span_len - 1 - window))).reshape(-1)
    padded = jnp.pad(padded, (0, row_count)).reshape(row_count, span_len)
    return jnp.sum(padded, axis=0)


def head_scores(q_head, k_head, mask_win, same_doc, bias_plane):
    raw = matmul_nt(q_head, k_head)
    scores = raw + bias_plane + mask_win[None, :]
    return jnp.where(same_doc, scores, -1e30)


def plain_shards(
    hidden,
    segments,
    delete_mask,
    bucket_table,
    attn_weight,
    gate_weight,
    up_weight,
    down_weight,
    norm_attn,
    norm_ffn,
    rel_bias,
    out_grad,
):
    row_count = hidden.shape[0]
    head_count = rel_bias.shape[1]
    bucket_count = rel_bias.shape[0]
    inner_width = attn_weight.shape[1] * lax.axis_size("seq") // 4
    head_width = inner_width // head_count
    table_len = bucket_table.shape[0]
    longest = (table_len + 1) // 2
    reach_blocks = (longest + row_count - 2) // row_count
    margin = reach_blocks * row_count
    window = (2 * reach_blocks + 1) * row_count
    span_len = row_count + window - 1
    w_attn, w_gate, w_up, w_down = (
        lax.all_gather(attn_weight, "seq", axis=1, tiled=True),
        lax.all_gather(gate_weight, "seq", axis=1, tiled=True),
        lax.all_gather(up_weight, "seq", axis=1, tiled=True),
        lax.all_gather(down_weight, "seq", axis=0, tiled=True),
    )
    residual = hidden.astype(jnp.float32)
    normed = rms_norm(residual, norm_attn).astype(jnp.bfloat16)
    projected = matmul(normed, w_attn[:, : 3 * inner_width]).astype(jnp.bfloat16)
    queries = projected[:, :inner_width]
    key_rows = projected[:, inner_width : 2 * inner_width]
    value_rows = projected[:, 2 * inner_width :]
    own_block = (key_rows, value_rows, segments + 1, delete_mask)
    both_sides = []
    for direction in (1, -1):
        current = own_block
        received = []
        for distance in range(reach_blocks):
            current = shifted((current[0], current[1], current[2], current[3]), "seq", direction)
            received.append(current)
        both_sides.append(received)
    ordered = both_sides[0][::-1] + [own_block] + both_sides[1]
    k_win = jnp.concatenate([portion[0] for portion in ordered], 0)
    v_win = jnp.concatenate([portion[1] for portion in ordered], 0)
    seg_win = jnp.concatenate([portion[2] for portion in ordered], 0)
    mask_win = jnp.concatenate([portion[3] for portion in ordered], 0).astype(jnp.float32)
    line_index = (jnp.arange(span_len, dtype=jnp.int32) + row_count - 1) % span_len
    line_offset = line_index - margin - (row_count - 1)
    line_bucket = jnp.take(
        bucket_table, jnp.clip(line_offset, 1 - longest, longest - 1) + longest - 1
    )
    line_onehot = (
        line_bucket[:, None] == jnp.arange(bucket_count, dtype=jnp.int32)[None, :]
    ).astype(jnp.float32)
    line_bias = jnp.dot(line_onehot, rel_bias, precision=lax.Precision.HIGHEST)
    same_doc = segments[:, None] + 1 == seg_win[None, :]
    mixed_parts = []
    log_parts = []
    for head in range(head_count):
        cols = slice(head * head_width, (head + 1) * head_width)
        bias_plane = toeplitz(line_bias[:, head], row_count, window)
        scores = head_scores(queries[:, cols], k_win[:, cols], mask_win, same_doc, bias_plane)
        row_max = jnp.max(scores, axis=-1, keepdims=True)
        exp_scores = jnp.exp(scores - row_max)
        row_total = jnp.sum(exp_scores, axis=-1, keepdims=True)
        log_parts.append(row_max + jnp.log(row_total))
        softmax_weights = (exp_scores / row_total).astype(jnp.bfloat16)
        mixed_parts.append(matmul(softmax_weights, v_win[:, cols]))
    attended = jnp.concatenate(mixed_parts, 1).astype(jnp.bfloat16)
    w_out = w_attn[:, 3 * inner_width :]
    after = residual + matmul_nt(attended, w_out)
    normed_ffn = rms_norm(after, norm_ffn).astype(jnp.bfloat16)
    gate_act = matmul(normed_ffn, w_gate)
    up_act = matmul(normed_ffn, w_up)
    activated = gated_unit(gate_act, up_act).astype(jnp.bfloat16)
    output = (after + matmul(activated, w_down)).astype(jnp.bfloat16)
    d_activated = matmul_nt(out_grad, w_down)
    d_down = matmul_tn(activated, out_grad)
    unit_out, unit_pull = jax.vjp(gated_unit, gate_act, up_act)
    d_gate_act, d_up_act = unit_pull(d_activated)
    d_gate_act = d_gate_act.astype(jnp.bfloat16)
    d_up_act = d_up_act.astype(jnp.bfloat16)
    d_normed_ffn = matmul_nt(d_gate_act, w_gate) + matmul_nt(d_up_act, w_up)
    d_w_gate = matmul_tn(normed_ffn, d_gate_act)
    d_w_up = matmul_tn(normed_ffn, d_up_act)
    norm_out, second_pull = jax.vjp(rms_norm, after, norm_ffn)
    d_after_part, d_norm_ffn = second_pull(d_normed_ffn)
    d_after = out_grad.astype(jnp.float32) + d_after_part
    d_after_low = d_after.astype(jnp.bfloat16)
    d_w_out = matmul_tn(d_after_low, attended)
    d_mixed = matmul(d_after_low, w_out).astype(jnp.bfloat16)
    dq_parts = []
    dk_parts = []
    dv_parts = []
    line_grads = []
    for head in range(head_count):
        cols = slice(head * head_width, (head + 1) * head_width)
        bias_plane = toeplitz(line_bias[:, head], row_count, window)
        scores = head_scores(queries[:, cols], k_win[:, cols], mask_win, same_doc, bias_plane)
        recomputed = jnp.exp(scores - log_parts[head])
        d_mix_head = d_mixed[:, cols]
        d_weights = matmul_nt(d_mix_head, v_win[:, cols])
        dv_parts.append(matmul_tn(recomputed.astype(jnp.bfloat16), d_mix_head))
        row_delta = jnp.sum(recomputed * d_weights, axis=-1, keepdims=True)
        d_scores = recomputed * (d_weights - row_delta)
        line_grads.append(diagonal_sums(d_scores, span_len))
        d_scores_low = d_scores.astype(jnp.bfloat16)
        dq_parts.append(matmul(d_scores_low, k_win[:, cols]))
        dk_parts.append(matmul_tn(d_scores_low, queries[:, cols]))
    d_queries = jnp.concatenate(dq_parts, 1)
    d_k_win = jnp.concatenate(dk_parts, 1)
    d_v_win = jnp.concatenate(dv_parts, 1)
    d_rel = lax.dot_general(
        line_onehot,
        jnp.stack(line_grads, 1),
        (((0,), (0,)), ((), ())),
        precision=lax.Precision.HIGHEST,
    )
    returned = [
        (
            d_k_win[slot * row_count : (slot + 1) * row_count],
            d_v_win[slot * row_count : (slot + 1) * row_count],
        )
        for slot in range(2 * reach_blocks + 1)
    ]
    d_keys = returned[reach_blocks][0]
    d_values = returned[reach_blocks][1]
    for direction in (1, -1):
        carried = (jnp.zeros_like(d_keys), jnp.zeros_like(d_values))
        for distance in range(reach_blocks, 0, -1):
            portion = returned[reach_blocks - direction * distance]
            carried = shifted(
                (shortened(carried[0] + portion[0]), shortened(carried[1] + portion[1])),
                "seq",
                -direction,
            )
        d_keys = d_keys + carried[0]
        d_values = d_values + carried[1]
    d_projected = jnp.concatenate([d_queries, d_keys, d_values], 1).astype(jnp.bfloat16)
    d_normed = matmul_nt(d_projected, w_attn[:, : 3 * inner_width])
    d_w_proj = matmul_tn(normed, d_projected)
    first_out, first_pull = jax.vjp(rms_norm, residual, norm_attn)
    d_resid_part, d_norm_attn = first_pull(d_normed)
    d_hidden = d_after + d_resid_part
    d_attn_full = jnp.concatenate([d_w_proj, d_w_out], 1)
    g_attn, g_gate, g_up, g_down = (
        lax.psum_scatter(d_attn_full, "seq", scatter_dimension=1, tiled=True),
        lax.psum_scatter(d_w_gate, "seq", scatter_dimension=1, tiled=True),
        lax.psum_scatter(d_w_up, "seq", scatter_dimension=1, tiled=True),
        lax.psum_scatter(d_down, "seq", scatter_dimension=0, tiled=True),
    )
    s_attn, s_ffn, s_rel = lax.psum((d_norm_attn, d_norm_ffn, d_rel), "seq")
    return (output, d_hidden, g_attn, g_gate, g_up, g_down, s_attn, s_ffn, s_rel)


def solution(mesh):
    placed = (
        P("seq", None), P("seq"), P("seq"), P(), P(None, "seq"), P(None, "seq"), P(None, "seq"), P("seq", None),
        P(), P(), P(), P("seq", None),
    )
    n = mesh.shape["seq"]
    body = functools.partial(shards, n) if n in GRIDS else plain_shards
    return jax.shard_map(
        body,
        mesh=mesh,
        in_specs=placed,
        out_specs=(
            P("seq", None), P("seq", None), P(None, "seq"), P(None, "seq"), P(None, "seq"), P("seq", None),
            P(), P(), P(),
        ),
        check_vma=False,
    )
```

```python
import functools
import math
import jax
import jax.numpy as jnp
from jax import lax
from jax.experimental import pallas as pl
from jax.experimental.pallas import tpu as pltpu
from jax.sharding import PartitionSpec as P

MESH = pl.DeviceIdType.MESH
BF = jnp.bfloat16
F32 = jnp.float32
BIG = 1e30
GRIDS = {32: (4, 2, 2)}
ORDERS = ("xyz", "zxy", "zyx")
GROUPS = 8
STAGES = 5
GATHER_DELAY = ((0, 2, 4, 5, 6, 7), (0, 1, 2, 3, 5, 7), (0, 1, 2, 3, 5, 7))
SCATTER_DELAY = ((0, 1, 2, 3, 5, 7), (0, 2, 4, 5, 6, 7), (0, 2, 4, 5, 6, 7))
PIECE = 48
EPS = 1e-06


def nt(a, b):
    return lax.dot_general(a, b, (((1,), (1,)), ((), ())), preferred_element_type=F32)


def nn(a, b):
    return jnp.dot(a, b, preferred_element_type=F32)


def column_parts(width):
    return ((0, 384), (384, 512), (896, width - 896))


def when(cond, body):
    if cond is None:
        body()
    else:
        pl.when(cond)(body)


def inside(value, count):
    return (value >= 0) & (value < count)


class Place:
    def __init__(self, n):
        self.n = n
        self.grid = GRIDS[n]
        zs, ys, xs = self.grid
        self.me = lax.axis_index("seq")
        self.c = self.me % 2
        chip = self.me // 2
        self.x = chip % xs
        self.y = (chip // xs) % ys
        self.z = chip // (xs * ys)

    def dev(self, z, y, x):
        _, ys, xs = self.grid
        return ((z * ys + y) * xs + x) * 2 + self.c

    def around(self):
        zs = self.grid[0]
        z, y, x = self.z, self.y, self.x
        out = [
            (None, self.me + 1 - 2 * self.c),
            (None, self.dev(z, y, 1 - x)),
            (None, self.dev(z, 1 - y, x)),
            (z < zs - 1, self.dev(jnp.minimum(z + 1, zs - 1), y, x)),
            (z > 0, self.dev(jnp.maximum(z - 1, 0), y, x)),
        ]
        return out

    def barrier(self, reach, far=False):
        sem = pltpu.get_barrier_semaphore()
        pairs = self.around()
        if far:
            zs = self.grid[0]
            pairs = pairs[:3] + [(None, self.dev((self.z + i) % zs, self.y, self.x)) for i in range(1, zs)]
        for by in reach:
            target = self.me + by
            pairs.append((inside(target, self.n), jnp.clip(target, 0, self.n - 1)))
        count = 0
        for cond, device in pairs:
            when(
                cond,
                lambda device=device: pl.semaphore_signal(
                    sem, inc=1, device_id=(device,), device_id_type=MESH
                ),
            )
            count = count + (1 if cond is None else cond.astype(jnp.int32))
        pl.semaphore_wait(sem, count)


def gather_stages(here, blocks, send, recv, width):
    zs, ys, xs = here.grid
    z, y, x = here.z, here.y, here.x
    parts = []
    slot = 0
    for order, (first, wide) in zip(ORDERS, column_parts(width)):
        cols = pl.ds(first, wide)
        have = set()
        stages = []
        for dim in order:
            in_y = pl.ds(0, ys) if "y" in have else pl.ds(y, 1)
            in_x = pl.ds(0, xs) if "x" in have else pl.ds(x, 1)
            if dim == "z":
                for step in range(zs - 1):
                    moves = []
                    for way in (1, -1):
                        source = z - way * step
                        sends = inside(source, zs) & inside(z + way, zs)
                        gets = inside(z - way - way * step, zs) & inside(z - way, zs)
                        in_z = pl.ds(jnp.clip(source, 0, zs - 1), 1)
                        device = here.dev(jnp.clip(z + way, 0, zs - 1), y, x)
                        moves.append((sends, gets, in_z, in_y, in_x, cols, device, slot))
                        slot += 1
                    stages.append(moves)
            else:
                in_z = pl.ds(0, zs) if "z" in have else pl.ds(z, 1)
                device = here.dev(z, y, 1 - x) if dim == "x" else here.dev(z, 1 - y, x)
                stages.append([(None, None, in_z, in_y, in_x, cols, device, slot)])
                slot += 1
            have.add(dim)
        parts.append(stages)

    def copy(move, g):
        _, _, in_z, in_y, in_x, cols, device, at = move
        ref = blocks.at[g, in_z, in_y, in_x, :, cols]
        return pltpu.make_async_remote_copy(
            ref, ref, send.at[g, at], recv.at[g, at], device_id=(device,), device_id_type=MESH
        )

    return parts, copy, slot


def gather_visit(parts, copy, v):
    for k in range(STAGES, -1, -1):
        for part, stages in enumerate(parts):

            def step(g, k=k, stages=stages):
                if k > 0:
                    for move in stages[k - 1]:
                        when(move[1], lambda move=move: copy(move, g).wait_recv())
                if k < STAGES:
                    for move in stages[k]:
                        when(move[0], lambda move=move: copy(move, g).start())

            g = v - GATHER_DELAY[part][k]
            if not isinstance(v, int):
                pl.when((g > 0) & (g < GROUPS))(functools.partial(step, g))
                continue
            if v == k:
                step(0)
            if 0 < g < GROUPS:
                step(g)


def gather_drain(parts, copy):
    def body(g, _):
        for stages in parts:
            for moves in stages:
                for move in moves:
                    when(move[0], lambda move=move: copy(move, g).wait_send())
        return 0

    lax.fori_loop(0, GROUPS, body, 0)


def shift_line(table, rel, head):
    line = jnp.zeros(table.shape, F32)
    for bucket in range(rel.shape[0]):
        line = jnp.where(table == bucket, rel[bucket, head], line)
    return line


def gelu_parts(v):
    root = math.sqrt(2.0 / math.pi)
    sq = v * v
    t = jnp.tanh(root * (v + 0.044715 * (sq * v)))
    half = 0.5 * (1.0 + t)
    value = v * half
    slope = half + 0.5 * v * (1.0 - t * t) * (root * (1.0 + 3 * 0.044715 * sq))
    return value, slope


def row_norm(v):
    return lax.rsqrt(jnp.mean(v * v, axis=-1, keepdims=True) + EPS)


REACH = (4, -4)


class Halo:
    def __init__(self, here, ref, send, recv):
        self.here, self.ref, self.send, self.recv = here, ref, send, recv
        self.rows = ref.shape[-2] // 5
        even = here.x == 0
        self.even = even
        self.partner = here.me + 1 - 2 * here.c
        self.across = here.me + jnp.where(even, 2, -2)
        self.near = jnp.where(even, 4, 0)
        self.far = 4 - self.near
        step = jnp.where(even, 4, -4)
        self.to_far = inside(here.me + step, here.n)
        self.from_far = inside(here.me - step, here.n)
        self.far_device = jnp.clip(here.me + step, 0, here.n - 1)
        core0 = here.c == 0
        self.has_prev, self.has_next = here.me >= 2, here.me < here.n - 2
        self.over = jnp.where(core0, self.has_next, self.has_prev)
        self.under = jnp.where(core0, self.has_prev, self.has_next)

    def part(self, slot, piece):
        at = pl.ds(pl.multiple_of(slot * self.rows, self.rows), self.rows)
        return self.ref.at[at] if piece is None else self.ref.at[piece, at]

    def move(self, kind, piece):
        c, j = self.here.c, 0 if piece is None else piece
        src, dst, device = (
            (2, self.far, self.across),
            (self.near, self.far, self.far_device),
            (2, jnp.where(c == 0, 1, 3), self.partner),
            (jnp.where(c == 0, 4, 0), jnp.where(c == 0, 3, 1), self.partner),
        )[kind]
        return pltpu.make_async_remote_copy(
            self.part(src, piece), self.part(dst, piece), self.send.at[j, kind], self.recv.at[j, kind],
            device_id=(device,), device_id_type=MESH,
        )

    def begin(self, piece=None):
        self.move(0, piece).start()
        self.move(2, piece).start()

    def forward(self, piece=None):
        self.move(0, piece).wait_recv()
        when(self.to_far, lambda: self.move(1, piece).start())

    def spread(self, piece=None):
        when(self.from_far, lambda: self.move(1, piece).wait_recv())
        when(self.over, lambda: self.move(3, piece).start())

    def settle(self, piece=None):
        self.move(2, piece).wait_recv()
        when(self.under, lambda: self.move(3, piece).wait_recv())

    def close(self, piece=None):
        self.move(0, piece).wait_send()
        self.move(2, piece).wait_send()
        when(self.to_far, lambda: self.move(1, piece).wait_send())
        when(self.over, lambda: self.move(3, piece).wait_send())

    def absent(self):
        core0 = self.here.c == 0
        no_prev, no_next = jnp.logical_not(self.has_prev), jnp.logical_not(self.has_next)
        return ((no_prev, 0), (no_next, 4), (no_prev & core0, 1), (no_next & jnp.logical_not(core0), 3))


def forward_kernel(
    n, heads,
    slab, hid, dy, kx_own, qx, table, rel, na, nf,
    o_grads, o_outp, o_dn2p, o_x1, o_at, o_q, o_kv, o_kx, o_lse, o_ga,
    G, ga, n2f, dyf, kv, kx, qv, x1, at, lse,
    gs, gr, lsem, hs, hr, ks, kr, cs, cr, osem, stsem,
):
    here = Place(n)
    c = here.c
    rows, D = hid.shape
    inner = qv.shape[1]
    nz = here.grid[0]
    partner = here.me + 1 - 2 * c
    window = kx.shape[0]
    tiles = rows // 256
    span = (window - rows) + 256
    mine = pl.ds(pl.multiple_of(c * rows, rows), rows)
    centre = pl.ds(2 * rows, rows)

    def to_partner(src, dst, i):
        return pltpu.make_async_remote_copy(
            src, dst, cs.at[i], cr.at[i], device_id=(partner,), device_id_type=MESH
        )

    kv_halo, kx_halo = Halo(here, kv, hs, hr), Halo(here, kx, ks, kr)

    own = [
        pltpu.make_async_copy(slab.at[g], G.at[g, here.z, here.y, here.x], lsem.at[g])
        for g in range(GROUPS)
    ]
    for copy in own:
        copy.start()
    kx_in = pltpu.make_async_copy(kx_own, kx.at[centre], lsem.at[GROUPS])
    kx_in.start()
    dy_in = pltpu.make_async_copy(dy, dyf.at[mine], lsem.at[GROUPS + 1])
    dy_in.start()
    here.barrier(REACH)
    for copy in own:
        copy.wait()
    parts, copy, _ = gather_stages(here, G, gs, gr, D)
    ag = lambda v: gather_visit(parts, copy, v)
    ag(0)
    kx_in.wait()
    kx_halo.begin()
    dy_in.wait()
    dy_out = to_partner(dyf.at[mine], dyf.at[mine], 0)
    dy_out.start()
    edge = jnp.where(lax.broadcasted_iota(jnp.int32, (rows, 128), 1) == 25, -BIG, 0.0).astype(BF)
    for cond, slot in kv_halo.absent():
        def absent(slot=slot):
            at_rows = pl.ds(slot * rows, rows)
            kx[at_rows, :] = edge
            for hp in range(heads // 2):
                kv[hp, at_rows, :] = jnp.zeros((rows, 256), BF)

        pl.when(cond)(absent)

    def attention(n1, bias, vt, S, Pm):
        ag(1)

        def norm_rows(i, _):
            at_rows = pl.ds(i * 64, 64)
            v = hid[at_rows, :].astype(F32)
            n1[at_rows, :] = (v * row_norm(v) * na[...]).astype(BF)
            return 0

        lax.fori_loop(0, rows // 64, norm_rows, 0)
        ag(2)
        kx_halo.forward()
        for head in range(heads):
            line = shift_line(table[...], rel, head)
            for b in range(bias.shape[1] // 128):
                lo = line[19 - b : 20 - b, :]
                hi = line[18 - b : 19 - b, :]
                both = jnp.broadcast_to(jnp.concatenate([lo, hi], 1), (128, 256))
                bias[head, 128 * b : 128 * b + 128, :] = pltpu.roll(both, 0, 1, stride=1, stride_axis=0)[:, :128]
            if head == 1:
                ag(3)
                kx_halo.spread()
            if head == 3:
                ag(4)
                kx_halo.settle()
        ag(5)
        keep = pltpu.make_async_copy(G.at[0], ga.at[:, :, :, c], lsem.at[GROUPS + 2])
        keep.start()
        give = to_partner(G.at[0], ga.at[:, :, :, c], 1)
        give.start()
        keep.wait()
        give.wait_recv()
        ga_out = pltpu.make_async_copy(ga, o_ga, osem.at[1])
        ga_out.start()

        for part in (1, 2, 0):
            weight = ga[part].reshape(inner, D)
            for half in range(rows // 256):
                at_rows = pl.ds(256 * half, 256)
                got = nt(n1[at_rows, :], weight).astype(BF)
                if part == 0:
                    qv[at_rows, :] = got
                    continue
                for hp in range(heads // 2):
                    kv[hp, pl.ds(2 * rows + 256 * half, 256), 128 * (part - 1) : 128 * part] = got[
                        :, 128 * hp : 128 * hp + 128
                    ]
            if part == 2:
                for hp in range(heads // 2):
                    kv_halo.begin(hp)
        kx_out = pltpu.make_async_copy(kx, o_kx, osem.at[3])
        kx_out.start()
        q_out = pltpu.make_async_copy(qv, o_q, osem.at[4])
        q_out.start()
        ag(6)
        kv_halo.forward(0)
        kv_halo.forward(1)
        kv_halo.spread(0)
        kv_halo.forward(2)
        kv_halo.settle(0)
        lane = lax.broadcasted_iota(jnp.int32, (256, 128), 1) // 64

        def pair(hp, _):
            @pl.when(hp > 0)
            def _():
                kv_halo.settle(hp)

            cols = pl.ds(pl.multiple_of(hp * 128, 128), 128)

            def turn(i, _):
                at_rows = pl.ds(pl.multiple_of(i * 256, 256), 256)
                vt[:, at_rows] = kv[hp, at_rows, 128:256].T
                return 0

            lax.fori_loop(0, window // 256, turn, 0)

            def one(k, _):
                @pl.when((k == 1) & (hp == 1))
                def _():
                    ag(7)

                t, e = k // 2, k % 2
                base = pl.multiple_of(t * 256, 256)
                head = hp * 2 + e
                q = qv[pl.ds(base, 256), cols]
                q = jnp.where(lane == e, q, jnp.zeros_like(q))
                qa = jnp.concatenate([q, qx[pl.ds(base, 256), :]], 1)

                def score(b, m):
                    at_rows = pl.ds(pl.multiple_of(base + b * 256, 256), 256)
                    ka = jnp.concatenate([kv[hp, at_rows, 0:128], kx[at_rows, :]], 1)
                    s = nt(ka, qa)
                    low = pl.multiple_of(b * 256, 256)
                    plane = jnp.concatenate(
                        [bias[head, pl.ds(low + 128, 256), :], bias[head, pl.ds(low, 256), :]], 1
                    )
                    s = s + plane
                    S[pl.ds(low, 256), :] = s
                    return jnp.maximum(m, jnp.max(s.reshape(32, 8, 256), axis=0))

                m = lax.fori_loop(0, span // 256, score, jnp.full((8, 256), -3e38, F32), unroll=True)
                m = jnp.max(m, axis=0, keepdims=True)

                def weigh(b, total):
                    at_rows = pl.ds(pl.multiple_of(b * 256, 256), 256)
                    p = jnp.exp(S[at_rows, :] - m)
                    Pm[at_rows, :] = p.astype(BF)
                    return total + jnp.sum(p.reshape(32, 8, 256), axis=0)

                total = lax.fori_loop(0, span // 256, weigh, jnp.zeros((8, 256), F32), unroll=True)
                total = jnp.sum(total, axis=0, keepdims=True)
                out_rows = pl.ds(pl.multiple_of(head * 64, 64), 64)
                mixed = nn(vt[pl.ds(pl.multiple_of(e * 64, 64), 64), pl.ds(base, span)], Pm[...])
                at[out_rows, pl.ds(base, 256)] = mixed / total
                lse[pl.ds(head, 1), pl.ds(base, 256)] = m + jnp.log(total)
                return 0

            lax.fori_loop(0, 2 * tiles, one, 0)

            @pl.when(hp < heads // 2 - 1)
            def _():
                kv_halo.spread(hp + 1)

            return 0

        lax.fori_loop(0, heads // 2, pair, 0)
        kv_out = pltpu.make_async_copy(kv, o_kv, osem.at[2])
        kv_out.start()
        outs = [
            pltpu.make_async_copy(at, o_at, osem.at[5]),
            pltpu.make_async_copy(lse, o_lse, osem.at[6]),
        ]
        for o in outs:
            o.start()
        w_out = ga[3].reshape(inner, D)

        def after(i, _):
            at_rows = pl.ds(pl.multiple_of(i * 128, 128), 128)
            a = at[:, at_rows].T.astype(BF)
            v = hid[at_rows, :].astype(F32) + nn(a, w_out)
            x1[at_rows, :] = v
            n2f[pl.ds(pl.multiple_of(c * rows + i * 128, 128), 128), :] = (v * row_norm(v) * nf[...]).astype(BF)
            return 0

        lax.fori_loop(0, rows // 128, after, 0)
        n2_out = to_partner(n2f.at[mine], n2f.at[mine], 2)
        n2_out.start()
        x1_out = pltpu.make_async_copy(x1, o_x1, osem.at[7])
        x1_out.start()
        give.wait_send()
        n2_out.wait()
        dy_out.wait()
        kx_halo.close()
        for hp in range(heads // 2):
            kv_halo.close(hp)
        for o in outs + [ga_out, kv_out, kx_out, q_out, x1_out]:
            o.wait()

    pl.run_scoped(
        attention,
        pltpu.VMEM((rows, D), BF),
        pltpu.VMEM((heads, span + 128, 128), F32),
        pltpu.VMEM((128, window), BF),
        pltpu.VMEM((span, 256), F32),
        pltpu.VMEM((span, 256), BF),
    )

    def feed(acc_o, acc_n, ft, gt, ut, stage):
        acc_o[...] = jnp.zeros_like(acc_o)
        acc_n[...] = jnp.zeros_like(acc_n)

        def stage_out(j):
            return pltpu.make_async_copy(stage.at[j % 2], o_grads.at[j + 1], stsem.at[j % 2])

        def chunk(j, _):
            ag(j + 8)
            g = j + 1
            wg = G.at[g, :, :, :, pl.ds(0, 16), :]
            wu = G.at[g, :, :, :, pl.ds(16, 16), :]
            wd = G.at[g, :, :, :, pl.ds(32, 16), :]
            whole = lambda ref: ref[...].reshape(256, D)

            def tokens(i, _):
                at_rows = pl.ds(pl.multiple_of(i * 256, 256), 256)
                n2 = n2f[at_rows, :]
                gate = nt(whole(wg), n2)
                up = nt(whole(wu), n2)
                df = nt(whole(wd), dyf[at_rows, :])
                value, slope = gelu_parts(gate)
                f = (value * up).astype(BF)
                dg = (df * up * slope).astype(BF)
                du = (df * value).astype(BF)
                ft[:, at_rows] = f
                gt[:, at_rows] = dg
                ut[:, at_rows] = du
                acc_o[at_rows, :] += nn(f.T, whole(wd))
                acc_n[at_rows, :] += nn(dg.T, whole(wg)) + nn(du.T, whole(wu))
                return 0

            lax.fori_loop(0, 2 * rows // 256, tokens, 0, unroll=2)

            @pl.when(j >= 2)
            def _():
                stage_out(j - 2).wait()

            s = j % 2
            stage[s, :, :, :, 0:16, :] = nn(gt[...], n2f[...]).astype(BF).reshape(here.grid + (16, D))
            stage[s, :, :, :, 16:32, :] = nn(ut[...], n2f[...]).astype(BF).reshape(here.grid + (16, D))
            stage[s, :, :, :, 32:48, :] = nn(ft[...], dyf[...]).astype(BF).reshape(here.grid + (16, D))
            stage_out(j).start()
            return 0

        lax.fori_loop(0, GROUPS - 1, chunk, 0)
        outs = [
            pltpu.make_async_copy(acc_o, o_outp, osem.at[0]),
            pltpu.make_async_copy(acc_n, o_dn2p, osem.at[1]),
        ]
        for o in outs:
            o.start()
        gather_drain(parts, copy)
        for o in outs:
            o.wait()
        stage_out(GROUPS - 3).wait()
        stage_out(GROUPS - 2).wait()

    pl.run_scoped(
        feed,
        pltpu.VMEM((2 * rows, D), F32),
        pltpu.VMEM((2 * rows, D), F32),
        pltpu.VMEM((256, 2 * rows), BF),
        pltpu.VMEM((256, 2 * rows), BF),
        pltpu.VMEM((256, 2 * rows), BF),
        pltpu.VMEM((2,) + here.grid + (PIECE, D), BF),
    )


def forward_call(n, heads, slab, hid, dy, kx_own, qx, table, rel, na, nf):
    rows, D = hid.shape
    inner = heads * 64
    zs, ys, xs = GRIDS[n]
    window = 5 * rows
    span = window - rows + 256
    shape = jax.ShapeDtypeStruct
    any_, vm = pl.BlockSpec(memory_space=pl.ANY), pl.BlockSpec(memory_space=pltpu.VMEM)
    sm = pl.BlockSpec(memory_space=pltpu.SMEM)
    slots = 3 * 8
    dma = pltpu.SemaphoreType.DMA
    return pl.pallas_call(
        functools.partial(forward_kernel, n, heads),
        out_shape=(
            shape((GROUPS, zs, ys, xs, PIECE, D), BF),
            shape((2 * rows, D), F32),
            shape((2 * rows, D), F32),
            shape((rows, D), F32),
            shape((inner, rows), F32),
            shape((rows, inner), BF),
            shape((heads // 2, window, 256), BF),
            shape((window, 128), BF),
            shape((8, rows), F32),
            shape((zs, ys, xs, 2, PIECE, D), BF),
        ),
        in_specs=[any_, vm, any_, any_, vm, vm, sm, vm, vm],
        out_specs=(any_,) * 10,
        scratch_shapes=[
            pltpu.VMEM((GROUPS, zs, ys, xs, PIECE, D), BF),
            pltpu.VMEM((zs, ys, xs, 2, PIECE, D), BF),
            pltpu.VMEM((2 * rows, D), BF),
            pltpu.VMEM((2 * rows, D), BF),
            pltpu.VMEM((heads // 2, window, 256), BF),
            pltpu.VMEM((window, 128), BF),
            pltpu.VMEM((rows, inner), BF),
            pltpu.VMEM((rows, D), F32),
            pltpu.VMEM((inner, rows), F32),
            pltpu.VMEM((8, rows), F32),
            dma((GROUPS, slots)), dma((GROUPS, slots)),
            dma((GROUPS + 3,)),
            dma((heads // 2, 4)), dma((heads // 2, 4)), dma((1, 4)), dma((1, 4)),
            dma((3,)), dma((3,)),
            dma((8,)), dma((2,)),
        ],
        compiler_params=pltpu.CompilerParams(
            collective_id=1, has_side_effects=True, vmem_limit_bytes=63 * 2**20
        ),
        cost_estimate=pl.CostEstimate(flops=55 * 10**9, bytes_accessed=80 * 10**6, transcendentals=10**7),
        name="forward",
    )(slab, hid, dy, kx_own, qx, table, rel, na, nf)


def prepare(hidden, segments, delete_mask, bucket_table, attn_weight, gate_weight, up_weight, down_weight):
    D = hidden.shape[1]
    rows = hidden.shape[0]
    groups = GROUPS - 1
    ffn = jnp.stack([gate_weight.T, up_weight.T, down_weight]).reshape(3, groups, 16, D)
    ffn = jnp.transpose(ffn, (1, 0, 2, 3)).reshape(groups, PIECE, D)
    slab = jnp.concatenate([attn_weight.T[None], ffn], 0)
    lane = jnp.arange(128, dtype=jnp.int32)[None, :]
    seg = segments[:, None]
    digit = jnp.where(lane < 9, seg % 8, jnp.where(lane < 17, (seg // 8) % 8, seg // 64))
    hit = digit == (lane - 1) % 8
    coded = (lane >= 1) & (lane < 25)
    kx = jnp.where(lane == 0, delete_mask.astype(F32)[:, None], jnp.where(coded & ~hit, -BIG, 0.0)).astype(BF)
    qx = jnp.where((lane == 0) | (lane == 25) | (coded & hit), 1.0, 0.0).astype(BF)
    reach = bucket_table.shape[0]
    table = jnp.pad(jnp.flip(bucket_table), (257, 20 * 128 - 257 - reach), constant_values=-1).reshape(20, 128)
    table = jnp.pad(table, ((0, 4), (0, 0)), constant_values=-1)
    return slab, kx, qx, table


FIRST = (1, 2, 3, 4, 5, 6, 7, 0)
AT = 7
AFTER = 10
SLOTS = 4
ZSLOTS = 4
WORK = 8
LINES = 56


def group_of(pos):
    if isinstance(pos, int):
        return FIRST[pos]
    return (pos + 1) % GROUPS


def add_into(dst, src):
    dst[...] = (dst[...].astype(F32) + src[...].astype(F32)).astype(BF)


class Scatter:
    def __init__(self, here, source, work, land, landa, landz, result, send, recv, load, width):
        self.here, self.source, self.work, self.result = here, source, work, result
        self.land, self.landa, self.landz = land, landa, landz
        self.send, self.recv, self.load = send, recv, load
        self.parts = column_parts(width)

    def loading(self, part, pos):
        here = self.here
        zs, ys, xs = here.grid
        in_y = pl.ds(here.y, 1) if part == 1 else pl.ds(0, ys)
        in_x = pl.ds(here.x, 1) if part == 2 else pl.ds(0, xs)
        cols = pl.ds(*self.parts[part])
        return pltpu.make_async_copy(
            self.source.at[group_of(pos), :, in_y, in_x, :, cols],
            self.work.at[pos % WORK, :, in_y, in_x, :, cols],
            self.load.at[pos, part],
        )

    def start_load(self, pos):
        for part in range(3):
            self.loading(part, pos).start()

    def moves(self, part, k, pos):
        here = self.here
        zs, ys, xs = here.grid
        z, y, x = here.z, here.y, here.x
        cols = pl.ds(*self.parts[part])
        dim = (("z0", "z1", "z2", "y", "x"), ("y", "x", "z0", "z1", "z2"), ("x", "y", "z0", "z1", "z2"))[part][k]
        work, source, g = self.work, self.source, group_of(pos)
        w, slot, zslot = pos % WORK, pos % SLOTS, pos % ZSLOTS
        base = 8 * part

        def remote(src, dst, at, device):
            return pltpu.make_async_remote_copy(
                src, dst, self.send.at[pos, at], self.recv.at[pos, at], device_id=(device,), device_id_type=MESH
            )

        if dim[0] == "z":
            step = int(dim[1])
            out = []
            for turn, way in enumerate((1, -1)):
                target = z + way * (zs - 1 - step)
                got = z + way * (zs - 2 - step)
                sends = inside(z + way, zs) & inside(target, zs)
                gets = inside(z - way, zs) & inside(got, zs)
                spot = step if turn == 0 or step == 0 else step + 2
                device = here.dev(jnp.clip(z + way, 0, zs - 1), y, x)
                block, mine = jnp.clip(target, 0, zs - 1), jnp.clip(got, 0, zs - 1)
                if part == 0:
                    src, dst = work.at[w, block, :, :, :, cols], self.landa.at[zslot, spot]
                else:
                    src, dst = work.at[w, block, y, x, :, cols], self.landz.at[zslot, spot, :, cols]

                def consume(mine=mine, dst=dst):
                    if part == 0:
                        for b in range(ys):
                            add_into(work.at[w, mine, b, :, :, cols], dst.at[b])
                    elif step < zs - 2:
                        add_into(work.at[w, mine, y, x, :, cols], dst)

                out.append((sends, gets, remote(src, dst, base + 2 + 2 * step + turn, device), consume))
            return out
        at = base + (0 if dim == "y" else 1)
        device = here.dev(z, 1 - y, x) if dim == "y" else here.dev(z, y, 1 - x)
        if k == 0 and dim == "y":
            src = source.at[g, :, pl.ds(1 - y, 1), :, :, cols]
            dst = work.at[w, :, pl.ds(y, 1), :, :, cols]
            pairs = [(work.at[w, b, y, :, :, cols], work.at[w, b, 1 - y, :, :, cols]) for b in range(zs)]
        elif k == 0:
            src = source.at[g, :, :, pl.ds(1 - x, 1), :, cols]
            dst = work.at[w, :, :, pl.ds(x, 1), :, cols]
            pairs = [(work.at[w, b, :, x, :, cols], work.at[w, b, :, 1 - x, :, cols]) for b in range(zs)]
        elif part != 0:
            src = work.at[w, :, y, 1 - x, :, cols] if dim == "x" else work.at[w, :, 1 - y, x, :, cols]
            dst = self.land.at[slot, :, :, cols]
            pairs = [(work.at[w, b, y, x, :, cols], self.land.at[slot, b, :, cols]) for b in range(zs)]
        elif dim == "y":
            src = work.at[w, z, 1 - y, :, :, cols]
            dst = self.land.at[slot, pl.ds(0, xs), :, cols]
            pairs = [(work.at[w, z, y, b, :, cols], self.land.at[slot, b, :, cols]) for b in range(xs)]
        else:
            src = work.at[w, z, y, 1 - x, :, cols]
            dst = self.land.at[slot, xs, :, cols]
            pairs = []

        def consume():
            for to, frm in pairs:
                add_into(to, frm)

        return [(None, None, remote(src, dst, at, device), consume)]

    def finish(self, part, pos):
        here = self.here
        zs, ys, xs = here.grid
        z, y, x = here.z, here.y, here.x
        slot, g = pos % SLOTS, group_of(pos)
        first, wide = self.parts[part]
        cols = pl.ds(first, wide)
        own = self.work[pos % WORK, z, y, x, :, cols].astype(F32)
        if part == 0:
            self.result[g, :, cols] = own + self.land[slot, xs, :, cols].astype(F32)
            return
        up = self.landz[pos % ZSLOTS, zs - 2, :, cols].astype(F32)
        down = self.landz[pos % ZSLOTS, zs, :, cols].astype(F32)
        self.result[g, :, cols] = own + jnp.where(z > 0, up, 0.0) + jnp.where(z < zs - 1, down, 0.0)

    def round(self, r):
        for k in range(STAGES, -1, -1):
            for part in range(3):

                def step(pos, k=k, part=part):
                    if k == (0 if part == 0 else 1):
                        self.loading(part, pos).wait()
                    if k > 0:
                        for _, gets, copy, consume in self.moves(part, k - 1, pos):
                            def take(copy=copy, consume=consume):
                                copy.wait_recv()
                                consume()

                            when(gets, take)
                    if k < STAGES:
                        for sends, _, copy, _ in self.moves(part, k, pos):
                            when(sends, lambda copy=copy: copy.start())
                        return
                    self.finish(part, pos)
                    for stage in range(STAGES):
                        for sends, _, copy, _ in self.moves(part, stage, pos):
                            when(sends, lambda copy=copy: copy.wait_send())

                pos = r - SCATTER_DELAY[part][k]
                if not isinstance(r, int):
                    pl.when(inside(pos, GROUPS - 1))(functools.partial(step, pos))
                    continue
                if 0 <= pos < GROUPS - 1:
                    step(pos)
                if r - AFTER == k:
                    step(AT)


def norm_back(v, gain, d):
    r = row_norm(v)
    vr = v * r
    dg = d * gain
    return r * (dg - vr * jnp.mean(vr * dg, axis=-1, keepdims=True)), d * vr


def put_line(small, first, line):
    width = line.shape[1]
    for i in range(-(-width // 128)):
        wide = min(128, width - 128 * i)
        small[first + i : first + i + 1, 0:wide] = line[:, 128 * i : 128 * i + wide]


def backward_kernel(
    n, heads,
    grads, outp, dn2p, x1_in, at_in, q_in, kv_in, kx_in, lse, ga_in,
    hid, dy, qx, table, rel, na, nf,
    gr, o_out, o_dh, o_res, o_small, dn_land, op_land,
    work, land, landa, landz, res, dx1, kv, kx, qv, at, ga, dat, das, back, fold, small, sland,
    ss, rs, lds, cs, cr, hs, hr, ls, ps, pr, osem,
):
    here = Place(n)
    c = here.c
    rows, D = dx1.shape
    inner = qv.shape[1]
    window = kx.shape[0]
    zs, ys, xs = here.grid
    z, y, x = here.z, here.y, here.x
    span = window - rows + 256
    partner = here.me + 1 - 2 * c
    mine = pl.ds(pl.multiple_of(c * rows, rows), rows)
    theirs = pl.ds(pl.multiple_of((1 - c) * rows, rows), rows)

    def to_partner(src, dst, i):
        return pltpu.make_async_remote_copy(
            src, dst, cs.at[i], cr.at[i], device_id=(partner,), device_id_type=MESH
        )

    def local(src, dst, i):
        return pltpu.make_async_copy(src, dst, ls.at[i])

    sc = Scatter(here, gr, work, land, landa, landz, res, ss, rs, lds, D)
    for pos in range(WORK):
        if pos != AT:
            sc.start_load(pos)
    loads = [
        local(dn2p.at[mine], dx1, 0), local(kv_in, kv, 1), local(kx_in, kx, 2),
        local(q_in, qv, 3), local(at_in, at, 4), local(ga_in, ga, 5),
    ]
    for load in loads:
        load.start()
    here.barrier(REACH, True)
    dn_out = to_partner(dn2p.at[theirs], dn_land, 0)
    dn_out.start()
    sc.round(0)
    op_out = to_partner(outp.at[theirs], op_land, 1)
    op_out.start()
    small[...] = jnp.zeros_like(small)

    def after_ffn(x1, other, grad, low):
        first = [local(x1_in, x1, 6), local(dy, grad, 7)]
        for load in first:
            load.start()
        dn_out.wait_recv()
        second = local(dn_land, other, 8)
        second.start()
        sc.round(1)
        for load in loads + first + [second]:
            load.wait()
        w_out = ga[zs - 1].reshape(inner, D)

        def through(i, total):
            at_rows = pl.ds(pl.multiple_of(i * 128, 128), 128)
            d = dx1[at_rows, :] + other[at_rows, :]
            back_v, gain_d = norm_back(x1[at_rows, :], nf[...], d)
            v = grad[at_rows, :].astype(F32) + back_v
            dx1[at_rows, :] = v
            v = v.astype(BF)
            low[at_rows, :] = v
            da = nt(v, w_out).astype(BF)
            das[at_rows, :] = da
            dat[:, at_rows] = da.T
            return total + jnp.sum(gain_d.reshape(16, 8, D), axis=0)

        total = lax.fori_loop(0, rows // 128, through, jnp.zeros((8, D), F32))
        put_line(small, 44, jnp.sum(total, axis=0, keepdims=True))
        third = local(outp.at[mine], other, 9)
        third.start()
        sc.round(2)
        for h in range(2):
            part = nn(at[pl.ds(h * (inner // 2), inner // 2), :].astype(BF), low[...])
            ga[zs - 1, h] = part.astype(BF).reshape(xs, 2, PIECE, D)
        third.wait()
        op_out.wait_recv()

        def add(i, _):
            at_rows = pl.ds(pl.multiple_of(i * 64, 64), 64)
            x1[at_rows, :] = x1[at_rows, :] + other[at_rows, :]
            return 0

        lax.fori_loop(0, rows // 64, add, 0)
        fourth = local(op_land, other, 10)
        fourth.start()
        fourth.wait()

        def put(i, _):
            at_rows = pl.ds(pl.multiple_of(i * 64, 64), 64)
            low[at_rows, :] = (x1[at_rows, :] + other[at_rows, :]).astype(BF)
            return 0

        lax.fori_loop(0, rows // 64, put, 0)
        out = pltpu.make_async_copy(low, o_out, osem.at[0])
        out.start()
        out.wait()
        dn_out.wait_send()
        op_out.wait_send()

    pl.run_scoped(
        after_ffn, pltpu.VMEM((rows, D), F32), pltpu.VMEM((rows, D), F32), pltpu.VMEM((rows, D), BF),
        pltpu.VMEM((rows, D), BF),
    )

    way = Halo(here, kx, hs, hr)

    def home(dkv, hp, kind):
        src, device = (
            (jnp.where(c == 0, 1, 3), partner),
            (jnp.where(c == 0, 3, 1), partner),
            (way.far, jnp.clip(here.me - jnp.where(way.even, 4, -4), 0, n - 1)),
            (way.near, way.across),
        )[kind]
        return pltpu.make_async_remote_copy(
            dkv.at[hp, pl.ds(pl.multiple_of(src * rows, rows), rows)],
            back.at[hp, kind],
            hs.at[hp, kind],
            hr.at[hp, kind],
            device_id=(device,),
            device_id_type=MESH,
        )

    def add_back(dkv, hp, kind, slot):
        at_rows = pl.ds(pl.multiple_of(slot * rows, rows), rows)
        add_into(dkv.at[hp, at_rows], back.at[hp, kind])

    def home_begin(dkv, hp):
        when(way.under, lambda: home(dkv, hp, 0).start())
        home(dkv, hp, 1).start()

    def home_merge(dkv, hp):
        def merge():
            home(dkv, hp, 0).wait_recv()
            add_back(dkv, hp, 0, jnp.where(c == 0, 4, 0))

        when(way.over, merge)
        when(way.from_far, lambda: home(dkv, hp, 2).start())

    def home_cross(dkv, hp):
        def merge():
            home(dkv, hp, 2).wait_recv()
            add_back(dkv, hp, 2, way.near)

        when(way.to_far, merge)
        home(dkv, hp, 3).start()

    def home_close(dkv, hp):
        when(way.under, lambda: home(dkv, hp, 0).wait_send())
        home(dkv, hp, 1).wait_send()
        when(way.from_far, lambda: home(dkv, hp, 2).wait_send())
        home(dkv, hp, 3).wait_send()

    def pairs(dkv, dqt, acc_k, acc_v, skew, kt, bias):
        dqt[...] = jnp.zeros_like(dqt)
        lane = lax.broadcasted_iota(jnp.int32, (256, 128), 1) // 64
        lane_of = lax.broadcasted_iota(jnp.int32, (32, 128), 1)
        blocks = skew.shape[0] // 128

        def one_head(hp, e):
            head = hp * 2 + e
            pl.when(e == 0)(lambda: sc.round(3 + hp))
            cols = pl.ds(pl.multiple_of(hp * 128, 128), 128)
            out_rows = pl.ds(pl.multiple_of(head * 64, 64), 64)
            line = shift_line(table[...], rel, head)
            for b in range(blocks):
                both = jnp.concatenate([line[19 - b : 20 - b, :], line[18 - b : 19 - b, :]], 1)
                both = jnp.broadcast_to(both, (128, 256))
                bias[128 * b : 128 * b + 128, :] = pltpu.roll(both, 0, 1, stride=1, stride_axis=0)[:, :128]
            skew[...] = jnp.zeros_like(skew)

            def tile(t, _):
                base = pl.multiple_of(t * 256, 256)
                here_q = pl.ds(base, 256)
                q = qv[here_q, cols]
                q = jnp.where(lane == e, q, jnp.zeros_like(q))
                qa = jnp.concatenate([q, qx[here_q, :]], 1)
                da = das[here_q, cols]
                da = jnp.where(lane == e, da, jnp.zeros_like(da))
                logs = lse[pl.ds(head, 1), here_q]
                delta = jnp.sum(dat[out_rows, here_q].astype(F32) * at[out_rows, here_q], axis=0, keepdims=True)

                def block(b, dq):
                    low = pl.multiple_of(b * 256, 256)
                    at_rows = pl.ds(pl.multiple_of(base + b * 256, 256), 256)
                    ka = jnp.concatenate([kv[hp, at_rows, 0:128], kx[at_rows, :]], 1)
                    plane = jnp.concatenate([bias[pl.ds(low + 128, 256), :], bias[pl.ds(low, 256), :]], 1)
                    p = jnp.exp(nt(ka, qa) + plane - logs)
                    ds = p * (nt(kv[hp, at_rows, 128:256], da) - delta)
                    skew[pl.ds(low + 128, 256), :] += ds[:, 0:128]
                    skew[pl.ds(low, 256), :] += ds[:, 128:256]
                    dsr = ds.astype(BF)
                    acc_v[at_rows, :] += nn(p.astype(BF), da)
                    acc_k[at_rows, :] += nn(dsr, q)
                    return dq + nn(kt[pl.ds(pl.multiple_of(e * 64, 64), 64), at_rows], dsr)

                dqt[out_rows, here_q] = lax.fori_loop(0, span // 256, block, jnp.zeros((64, 256), F32), unroll=True)
                return 0

            lax.fori_loop(0, rows // 256, tile, 0)
            tail = [None] * (blocks + 1)
            for b in range(blocks):
                a = jnp.concatenate([skew[128 * b : 128 * b + 128, :], jnp.zeros((128, 128), F32)], 1)
                half = 64
                while half >= 1:
                    a = a[0:half] + pltpu.roll(a[half : 2 * half], 256 - half, 1)
                    half //= 2
                for at_line, part in ((19 - b, a[:, 0:128]), (18 - b, a[:, 128:256])):
                    tail[at_line] = part if tail[at_line] is None else tail[at_line] + part
            line_d = jnp.concatenate(tail + [jnp.zeros((4, 128), F32)], 0)
            sums = [
                jnp.sum(jnp.where(table[...] == b, line_d, 0.0), axis=0, keepdims=True) for b in range(rel.shape[0])
            ]
            sums = jnp.sum(jnp.concatenate(sums, 0), axis=1, keepdims=True)
            small[0:32, :] = jnp.where(lane_of == head, sums, small[0:32, :])

        def pair(hp, _):
            acc_k[...] = jnp.zeros_like(acc_k)
            acc_v[...] = jnp.zeros_like(acc_v)

            def turn(i, _):
                at_rows = pl.ds(pl.multiple_of(i * 256, 256), 256)
                kt[:, at_rows] = kv[hp, at_rows, 0:128].T
                return 0

            lax.fori_loop(0, window // 256, turn, 0)
            lax.fori_loop(0, 2, lambda e, _: (one_head(hp, e), 0)[1], 0)

            def pack(i, _):
                at_rows = pl.ds(pl.multiple_of(i * 128, 128), 128)
                dkv[hp, at_rows, 0:128] = acc_k[at_rows, :].astype(BF)
                dkv[hp, at_rows, 128:256] = acc_v[at_rows, :].astype(BF)
                return 0

            lax.fori_loop(0, window // 128, pack, 0)
            home_begin(dkv, hp)
            pl.when(hp >= 1)(lambda: home_merge(dkv, hp - 1))
            pl.when(hp >= 2)(lambda: home_cross(dkv, hp - 2))
            return 0

        lax.fori_loop(0, heads // 2, pair, 0)
        last = heads // 2 - 1
        home_cross(dkv, last - 1)
        home_merge(dkv, last)
        sc.round(6)

    def to_weights(dkv, dqt, n1, proj, proj_t, hid_v):
        hid_in = local(hid, hid_v, 11)
        hid_in.start()
        hid_in.wait()

        def norm_rows(i, _):
            at_rows = pl.ds(pl.multiple_of(i * 64, 64), 64)
            v = hid_v[at_rows, :].astype(F32)
            n1[at_rows, :] = (v * row_norm(v) * na[...]).astype(BF)
            return 0

        lax.fori_loop(0, rows // 64, norm_rows, 0)

        def gather_pair(hp, _):
            home(dkv, hp, 1).wait_recv()
            home(dkv, hp, 3).wait_recv()

            def sum_rows(j, _):
                at_rows = pl.ds(pl.multiple_of(j * 128, 128), 128)
                total = dkv[hp, pl.ds(pl.multiple_of(2 * rows + j * 128, 128), 128), :].astype(F32)
                for i in (1, 3):
                    total = total + back[hp, i, at_rows, :].astype(F32)
                total = total.astype(BF)
                for part in range(2):
                    piece = total[:, 128 * part : 128 * part + 128]
                    to = pl.ds(pl.multiple_of((1 + part) * inner + hp * 128, 128), 128)
                    proj[at_rows, to] = piece
                    proj_t[to, at_rows] = piece.T
                to = pl.ds(pl.multiple_of(hp * 128, 128), 128)
                piece = dqt[to, at_rows].astype(BF)
                proj_t[to, at_rows] = piece
                proj[at_rows, to] = piece.T
                return 0

            lax.fori_loop(0, rows // 128, sum_rows, 0)
            return 0

        last = heads // 2 - 1
        sc.round(7)
        lax.fori_loop(0, last, gather_pair, 0)
        home_cross(dkv, last)
        sc.round(8)
        gather_pair(last, 0)

        def to_hidden(i, total):
            at_rows = pl.ds(pl.multiple_of(i * 128, 128), 128)
            d = nn(proj[at_rows, 0:inner], ga[0].reshape(inner, D))
            d = d + nn(proj[at_rows, inner : 2 * inner], ga[1].reshape(inner, D))
            d = d + nn(proj[at_rows, 2 * inner : 3 * inner], ga[2].reshape(inner, D))
            back_v, gain_d = norm_back(hid_v[at_rows, :].astype(F32), na[...], d)
            dx1[at_rows, :] = dx1[at_rows, :] + back_v
            return total + jnp.sum(gain_d.reshape(16, 8, D), axis=0)

        total = lax.fori_loop(0, rows // 128, to_hidden, jnp.zeros((8, D), F32))
        put_line(small, 32, jnp.sum(total, axis=0, keepdims=True))
        dh_out = pltpu.make_async_copy(dx1, o_dh, osem.at[1])
        dh_out.start()
        sc.round(9)

        for part in range(3):
            for h in range(2):
                take = pl.ds(part * inner + h * (inner // 2), inner // 2)
                ga[part, h] = nn(proj_t[take, :], n1[...]).astype(BF).reshape(xs, 2, PIECE, D)
        for hp in range(heads // 2):
            home_close(dkv, hp)
        dh_out.wait()

    def attention(dkv, dqt):
        pl.run_scoped(
            functools.partial(pairs, dkv, dqt),
            pltpu.VMEM((window, 128), F32), pltpu.VMEM((window, 128), F32), pltpu.VMEM((span + 128, 128), F32),
            pltpu.VMEM((128, window), BF), pltpu.VMEM((span + 128, 128), F32),
        )
        pl.run_scoped(
            functools.partial(to_weights, dkv, dqt),
            pltpu.VMEM((rows, D), BF), pltpu.VMEM((rows, 3 * inner), BF), pltpu.VMEM((3 * inner, rows), BF),
            pltpu.VMEM((rows, D), BF),
        )

    pl.run_scoped(attention, pltpu.VMEM((heads // 2, window, 256), BF), pltpu.VMEM((inner, rows), F32))

    fold_out = to_partner(ga.at[:, :, :, 1 - c], fold, 2)
    fold_out.start()
    def small_to(src, slot, device, i):
        return pltpu.make_async_remote_copy(
            src, sland.at[slot], ps.at[i], pr.at[i], device_id=(device,), device_id_type=MESH
        )

    swap = small_to(small, 0, partner, 0)
    swap.start()
    fold_out.wait()
    for a in range(zs):
        for b in range(ys):
            add_into(fold.at[a, b], ga.at[a, b, :, c])
    fold_in = pltpu.make_async_copy(fold, gr.at[0], osem.at[2])
    fold_in.start()
    fold_in.wait()
    sc.start_load(AT)
    sc.round(10)
    swap.wait()
    small[...] = small[...] + sland[0]
    swap = small_to(small, 1, here.dev(z, y, 1 - x), 1)
    swap.start()
    sc.round(11)
    swap.wait()
    small[...] = small[...] + sland[1]
    swap = small_to(small, 2, here.dev(z, 1 - y, x), 2)
    swap.start()
    sc.round(12)
    swap.wait()
    small[...] = small[...] + sland[2]
    swaps = []
    for far in range(1, zs):
        swaps.append(small_to(small, 3 + far, here.dev((z + far) % zs, y, x), 2 + far))
        swaps[-1].start()
    sc.round(13)
    for swap in swaps:
        swap.wait()
    sland[3] = small[...]
    ordered = jnp.zeros(small.shape, F32)
    for plane in range(zs):
        ordered = ordered + sland[3 + (z - plane + zs) % zs]
    small[...] = ordered
    small_out = pltpu.make_async_copy(small, o_small, osem.at[3])
    small_out.start()
    for r in range(14, AFTER + STAGES + 1):
        sc.round(r)
    res_out = pltpu.make_async_copy(res, o_res, osem.at[4])
    res_out.start()
    res_out.wait()
    small_out.wait()


def backward_call(n, heads, kept, hid, dy, qx, table, rel, na, nf):
    grads, outp, dn2p, x1, at, q, kv, kx, lse, ga = kept
    rows, D = hid.shape
    inner = heads * 64
    zs, ys, xs = GRIDS[n]
    window = 5 * rows
    shape = jax.ShapeDtypeStruct
    any_, vm = pl.BlockSpec(memory_space=pl.ANY), pl.BlockSpec(memory_space=pltpu.VMEM)
    sm = pl.BlockSpec(memory_space=pltpu.SMEM)
    dma = pltpu.SemaphoreType.DMA
    return pl.pallas_call(
        functools.partial(backward_kernel, n, heads),
        out_shape=(
            shape(grads.shape, BF),
            shape((rows, D), BF),
            shape((rows, D), F32),
            shape((GROUPS, PIECE, D), F32),
            shape((LINES, 128), F32),
            shape((rows, D), F32),
            shape((rows, D), F32),
        ),
        in_specs=[any_] * 8 + [vm] + [any_] * 3 + [vm, vm, sm, vm, vm],
        out_specs=(any_,) * 7,
        input_output_aliases={0: 0},
        scratch_shapes=[
            pltpu.VMEM((WORK, zs, ys, xs, PIECE, D), BF),
            pltpu.VMEM((SLOTS, zs, PIECE, D), BF),
            pltpu.VMEM((ZSLOTS, 5, ys, xs, PIECE, 384), BF),
            pltpu.VMEM((ZSLOTS, 5, PIECE, D), BF),
            pltpu.VMEM((GROUPS, PIECE, D), F32),
            pltpu.VMEM((rows, D), F32),
            pltpu.VMEM((heads // 2, window, 256), BF),
            pltpu.VMEM((window, 128), BF),
            pltpu.VMEM((rows, inner), BF),
            pltpu.VMEM((inner, rows), F32),
            pltpu.VMEM((zs, ys, xs, 2, PIECE, D), BF),
            pltpu.VMEM((inner, rows), BF),
            pltpu.VMEM((rows, inner), BF),
            pltpu.VMEM((heads // 2, 4, rows, 256), BF),
            pltpu.VMEM((zs, ys, xs, PIECE, D), BF),
            pltpu.VMEM((LINES, 128), F32),
            pltpu.VMEM((3 + zs, LINES, 128), F32),
            dma((GROUPS, 24)), dma((GROUPS, 24)), dma((GROUPS, 3)),
            dma((3,)), dma((3,)),
            dma((heads // 2, 4)), dma((heads // 2, 4)),
            dma((12,)),
            dma((3 + zs,)), dma((3 + zs,)),
            dma((5,)),
        ],
        compiler_params=pltpu.CompilerParams(
            collective_id=2, has_side_effects=True, vmem_limit_bytes=63 * 2**20
        ),
        cost_estimate=pl.CostEstimate(flops=12 * 10**9, bytes_accessed=60 * 10**6, transcendentals=10**7),
        name="backward",
    )(grads, outp, dn2p, x1, at, q, kv, kx, lse, ga, hid, dy, qx, table, rel, na, nf)


def shards(
    n, hidden, segments, delete_mask, bucket_table, attn_weight, gate_weight, up_weight, down_weight,
    norm_attn, norm_ffn, rel_bias, out_grad,
):
    heads = rel_bias.shape[1]
    D = hidden.shape[1]
    slab, kx, qx, table = prepare(
        hidden, segments, delete_mask, bucket_table, attn_weight, gate_weight, up_weight, down_weight
    )
    na, nf = norm_attn[None], norm_ffn[None]
    kept = forward_call(n, heads, slab, hidden, out_grad, kx, qx, table, rel_bias, na, nf)
    _, output, d_hidden, res, small, _, _ = backward_call(
        n, heads, kept, hidden, out_grad, qx, table, rel_bias, na, nf
    )
    ffn = res[1:].reshape(GROUPS - 1, 3, 16, D)
    mats = [ffn[:, i].reshape(-1, D) for i in range(3)]
    line = lambda first: small[first : first + 12].reshape(-1)[:D]
    return (
        output, d_hidden, res[0].T, mats[0].T, mats[1].T, mats[2], line(32), line(44), small[:32, :heads],
    )


def shifted(x, axis, by):
    count = lax.axis_size(axis)
    pairs = [(i, i + by) for i in range(count) if 0 <= i + by < count]
    return lax.ppermute(x, axis, pairs)


def shortened(x):

    def short(part):
        return part.astype(jnp.bfloat16) if part.dtype == jnp.float32 else part

    return jax.tree.map(short, x)


def rms_norm(value, gain):
    return value * lax.rsqrt(jnp.mean(value * value, axis=-1, keepdims=True) + 1e-06) * gain


def matmul(left, right):
    return jnp.dot(left, right, preferred_element_type=jnp.float32)


def matmul_tn(left, right):
    return lax.dot_general(
        left, right, (((0,), (0,)), ((), ())), preferred_element_type=jnp.float32
    )


def matmul_nt(left, right):
    return lax.dot_general(
        left, right, (((1,), (1,)), ((), ())), preferred_element_type=jnp.float32
    )


def gated_unit(gate_in, up_in):
    return jax.nn.gelu(gate_in) * up_in


def toeplitz(line, row_count, window):
    span_len = line.shape[0]
    tiled = jnp.tile(line, row_count)[: row_count * (span_len - 1)].reshape(row_count, span_len - 1)
    return tiled[:, :window]


def diagonal_sums(plane, span_len):
    row_count, window = plane.shape
    padded = jnp.pad(plane, ((0, 0), (0, span_len - 1 - window))).reshape(-1)
    padded = jnp.pad(padded, (0, row_count)).reshape(row_count, span_len)
    return jnp.sum(padded, axis=0)


def head_scores(q_head, k_head, mask_win, same_doc, bias_plane):
    raw = matmul_nt(q_head, k_head)
    scores = raw + bias_plane + mask_win[None, :]
    return jnp.where(same_doc, scores, -1e30)


def plain_shards(
    hidden,
    segments,
    delete_mask,
    bucket_table,
    attn_weight,
    gate_weight,
    up_weight,
    down_weight,
    norm_attn,
    norm_ffn,
    rel_bias,
    out_grad,
):
    row_count = hidden.shape[0]
    head_count = rel_bias.shape[1]
    bucket_count = rel_bias.shape[0]
    inner_width = attn_weight.shape[1] * lax.axis_size("seq") // 4
    head_width = inner_width // head_count
    table_len = bucket_table.shape[0]
    longest = (table_len + 1) // 2
    reach_blocks = (longest + row_count - 2) // row_count
    margin = reach_blocks * row_count
    window = (2 * reach_blocks + 1) * row_count
    span_len = row_count + window - 1
    w_attn, w_gate, w_up, w_down = (
        lax.all_gather(attn_weight, "seq", axis=1, tiled=True),
        lax.all_gather(gate_weight, "seq", axis=1, tiled=True),
        lax.all_gather(up_weight, "seq", axis=1, tiled=True),
        lax.all_gather(down_weight, "seq", axis=0, tiled=True),
    )
    residual = hidden.astype(jnp.float32)
    normed = rms_norm(residual, norm_attn).astype(jnp.bfloat16)
    projected = matmul(normed, w_attn[:, : 3 * inner_width]).astype(jnp.bfloat16)
    queries = projected[:, :inner_width]
    key_rows = projected[:, inner_width : 2 * inner_width]
    value_rows = projected[:, 2 * inner_width :]
    own_block = (key_rows, value_rows, segments + 1, delete_mask)
    both_sides = []
    for direction in (1, -1):
        current = own_block
        received = []
        for distance in range(reach_blocks):
            current = shifted((current[0], current[1], current[2], current[3]), "seq", direction)
            received.append(current)
        both_sides.append(received)
    ordered = both_sides[0][::-1] + [own_block] + both_sides[1]
    k_win = jnp.concatenate([portion[0] for portion in ordered], 0)
    v_win = jnp.concatenate([portion[1] for portion in ordered], 0)
    seg_win = jnp.concatenate([portion[2] for portion in ordered], 0)
    mask_win = jnp.concatenate([portion[3] for portion in ordered], 0).astype(jnp.float32)
    line_index = (jnp.arange(span_len, dtype=jnp.int32) + row_count - 1) % span_len
    line_offset = line_index - margin - (row_count - 1)
    line_bucket = jnp.take(
        bucket_table, jnp.clip(line_offset, 1 - longest, longest - 1) + longest - 1
    )
    line_onehot = (
        line_bucket[:, None] == jnp.arange(bucket_count, dtype=jnp.int32)[None, :]
    ).astype(jnp.float32)
    line_bias = jnp.dot(line_onehot, rel_bias, precision=lax.Precision.HIGHEST)
    same_doc = segments[:, None] + 1 == seg_win[None, :]
    mixed_parts = []
    log_parts = []
    for head in range(head_count):
        cols = slice(head * head_width, (head + 1) * head_width)
        bias_plane = toeplitz(line_bias[:, head], row_count, window)
        scores = head_scores(queries[:, cols], k_win[:, cols], mask_win, same_doc, bias_plane)
        row_max = jnp.max(scores, axis=-1, keepdims=True)
        exp_scores = jnp.exp(scores - row_max)
        row_total = jnp.sum(exp_scores, axis=-1, keepdims=True)
        log_parts.append(row_max + jnp.log(row_total))
        softmax_weights = (exp_scores / row_total).astype(jnp.bfloat16)
        mixed_parts.append(matmul(softmax_weights, v_win[:, cols]))
    attended = jnp.concatenate(mixed_parts, 1).astype(jnp.bfloat16)
    w_out = w_attn[:, 3 * inner_width :]
    after = residual + matmul_nt(attended, w_out)
    normed_ffn = rms_norm(after, norm_ffn).astype(jnp.bfloat16)
    gate_act = matmul(normed_ffn, w_gate)
    up_act = matmul(normed_ffn, w_up)
    activated = gated_unit(gate_act, up_act).astype(jnp.bfloat16)
    output = (after + matmul(activated, w_down)).astype(jnp.bfloat16)
    d_activated = matmul_nt(out_grad, w_down)
    d_down = matmul_tn(activated, out_grad)
    unit_out, unit_pull = jax.vjp(gated_unit, gate_act, up_act)
    d_gate_act, d_up_act = unit_pull(d_activated)
    d_gate_act = d_gate_act.astype(jnp.bfloat16)
    d_up_act = d_up_act.astype(jnp.bfloat16)
    d_normed_ffn = matmul_nt(d_gate_act, w_gate) + matmul_nt(d_up_act, w_up)
    d_w_gate = matmul_tn(normed_ffn, d_gate_act)
    d_w_up = matmul_tn(normed_ffn, d_up_act)
    norm_out, second_pull = jax.vjp(rms_norm, after, norm_ffn)
    d_after_part, d_norm_ffn = second_pull(d_normed_ffn)
    d_after = out_grad.astype(jnp.float32) + d_after_part
    d_after_low = d_after.astype(jnp.bfloat16)
    d_w_out = matmul_tn(d_after_low, attended)
    d_mixed = matmul(d_after_low, w_out).astype(jnp.bfloat16)
    dq_parts = []
    dk_parts = []
    dv_parts = []
    line_grads = []
    for head in range(head_count):
        cols = slice(head * head_width, (head + 1) * head_width)
        bias_plane = toeplitz(line_bias[:, head], row_count, window)
        scores = head_scores(queries[:, cols], k_win[:, cols], mask_win, same_doc, bias_plane)
        recomputed = jnp.exp(scores - log_parts[head])
        d_mix_head = d_mixed[:, cols]
        d_weights = matmul_nt(d_mix_head, v_win[:, cols])
        dv_parts.append(matmul_tn(recomputed.astype(jnp.bfloat16), d_mix_head))
        row_delta = jnp.sum(recomputed * d_weights, axis=-1, keepdims=True)
        d_scores = recomputed * (d_weights - row_delta)
        line_grads.append(diagonal_sums(d_scores, span_len))
        d_scores_low = d_scores.astype(jnp.bfloat16)
        dq_parts.append(matmul(d_scores_low, k_win[:, cols]))
        dk_parts.append(matmul_tn(d_scores_low, queries[:, cols]))
    d_queries = jnp.concatenate(dq_parts, 1)
    d_k_win = jnp.concatenate(dk_parts, 1)
    d_v_win = jnp.concatenate(dv_parts, 1)
    d_rel = lax.dot_general(
        line_onehot,
        jnp.stack(line_grads, 1),
        (((0,), (0,)), ((), ())),
        precision=lax.Precision.HIGHEST,
    )
    returned = [
        (
            d_k_win[slot * row_count : (slot + 1) * row_count],
            d_v_win[slot * row_count : (slot + 1) * row_count],
        )
        for slot in range(2 * reach_blocks + 1)
    ]
    d_keys = returned[reach_blocks][0]
    d_values = returned[reach_blocks][1]
    for direction in (1, -1):
        carried = (jnp.zeros_like(d_keys), jnp.zeros_like(d_values))
        for distance in range(reach_blocks, 0, -1):
            portion = returned[reach_blocks - direction * distance]
            carried = shifted(
                (shortened(carried[0] + portion[0]), shortened(carried[1] + portion[1])),
                "seq",
                -direction,
            )
        d_keys = d_keys + carried[0]
        d_values = d_values + carried[1]
    d_projected = jnp.concatenate([d_queries, d_keys, d_values], 1).astype(jnp.bfloat16)
    d_normed = matmul_nt(d_projected, w_attn[:, : 3 * inner_width])
    d_w_proj = matmul_tn(normed, d_projected)
    first_out, first_pull = jax.vjp(rms_norm, residual, norm_attn)
    d_resid_part, d_norm_attn = first_pull(d_normed)
    d_hidden = d_after + d_resid_part
    d_attn_full = jnp.concatenate([d_w_proj, d_w_out], 1)
    g_attn, g_gate, g_up, g_down = (
        lax.psum_scatter(d_attn_full, "seq", scatter_dimension=1, tiled=True),
        lax.psum_scatter(d_w_gate, "seq", scatter_dimension=1, tiled=True),
        lax.psum_scatter(d_w_up, "seq", scatter_dimension=1, tiled=True),
        lax.psum_scatter(d_down, "seq", scatter_dimension=0, tiled=True),
    )
    s_attn, s_ffn, s_rel = lax.psum((d_norm_attn, d_norm_ffn, d_rel), "seq")
    return (output, d_hidden, g_attn, g_gate, g_up, g_down, s_attn, s_ffn, s_rel)


def solution(mesh):
    placed = (
        P("seq", None), P("seq"), P("seq"), P(), P(None, "seq"), P(None, "seq"), P(None, "seq"), P("seq", None),
        P(), P(), P(), P("seq", None),
    )
    n = mesh.shape["seq"]
    body = functools.partial(shards, n) if n in GRIDS else plain_shards
    return jax.shard_map(
        body,
        mesh=mesh,
        in_specs=placed,
        out_specs=(
            P("seq", None), P("seq", None), P(None, "seq"), P(None, "seq"), P(None, "seq"), P("seq", None),
            P(), P(), P(),
        ),
        check_vma=False,
    )
```

```python
import functools
import math
import jax
import jax.numpy as jnp
from jax import lax
from jax.experimental import pallas as pl
from jax.experimental.pallas import tpu as pltpu
from jax.sharding import PartitionSpec as P

MESH = pl.DeviceIdType.MESH
BF = jnp.bfloat16
F32 = jnp.float32
BIG = 1e30
GRIDS = {32: (4, 2, 2)}
ORDERS = ("xyz", "zxy", "zyx")
GROUPS = 8
STAGES = 5
GATHER_DELAY = ((0, 2, 4, 5, 6, 7), (0, 1, 2, 3, 5, 7), (0, 1, 2, 3, 5, 7))
SCATTER_DELAY = ((0, 1, 2, 3, 5, 7), (0, 2, 4, 5, 6, 7), (0, 2, 4, 5, 6, 7))
PIECE = 48
EPS = 1e-06


def nt(a, b):
    return lax.dot_general(a, b, (((1,), (1,)), ((), ())), preferred_element_type=F32)


def nn(a, b):
    return jnp.dot(a, b, preferred_element_type=F32)


def column_parts(width):
    return ((0, 384), (384, 512), (896, width - 896))


def when(cond, body):
    if cond is None:
        body()
    else:
        pl.when(cond)(body)


def inside(value, count):
    return (value >= 0) & (value < count)


class Place:
    def __init__(self, n):
        self.n = n
        self.grid = GRIDS[n]
        zs, ys, xs = self.grid
        self.me = lax.axis_index("seq")
        self.c = self.me % 2
        chip = self.me // 2
        self.x = chip % xs
        self.y = (chip // xs) % ys
        self.z = chip // (xs * ys)

    def dev(self, z, y, x):
        _, ys, xs = self.grid
        return ((z * ys + y) * xs + x) * 2 + self.c

    def around(self):
        zs = self.grid[0]
        z, y, x = self.z, self.y, self.x
        out = [
            (None, self.me + 1 - 2 * self.c),
            (None, self.dev(z, y, 1 - x)),
            (None, self.dev(z, 1 - y, x)),
            (z < zs - 1, self.dev(jnp.minimum(z + 1, zs - 1), y, x)),
            (z > 0, self.dev(jnp.maximum(z - 1, 0), y, x)),
        ]
        return out

    def barrier(self, reach, far=False):
        sem = pltpu.get_barrier_semaphore()
        pairs = self.around()
        if far:
            zs = self.grid[0]
            pairs = pairs[:3] + [(None, self.dev((self.z + i) % zs, self.y, self.x)) for i in range(1, zs)]
        for by in reach:
            target = self.me + by
            pairs.append((inside(target, self.n), jnp.clip(target, 0, self.n - 1)))
        count = 0
        for cond, device in pairs:
            when(
                cond,
                lambda device=device: pl.semaphore_signal(
                    sem, inc=1, device_id=(device,), device_id_type=MESH
                ),
            )
            count = count + (1 if cond is None else cond.astype(jnp.int32))
        pl.semaphore_wait(sem, count)


def gather_stages(here, blocks, send, recv, width):
    zs, ys, xs = here.grid
    z, y, x = here.z, here.y, here.x
    parts = []
    slot = 0
    for order, (first, wide) in zip(ORDERS, column_parts(width)):
        cols = pl.ds(first, wide)
        have = set()
        stages = []
        for dim in order:
            in_y = pl.ds(0, ys) if "y" in have else pl.ds(y, 1)
            in_x = pl.ds(0, xs) if "x" in have else pl.ds(x, 1)
            if dim == "z":
                for step in range(zs - 1):
                    moves = []
                    for way in (1, -1):
                        source = z - way * step
                        sends = inside(source, zs) & inside(z + way, zs)
                        gets = inside(z - way - way * step, zs) & inside(z - way, zs)
                        in_z = pl.ds(jnp.clip(source, 0, zs - 1), 1)
                        device = here.dev(jnp.clip(z + way, 0, zs - 1), y, x)
                        moves.append((sends, gets, in_z, in_y, in_x, cols, device, slot))
                        slot += 1
                    stages.append(moves)
            else:
                in_z = pl.ds(0, zs) if "z" in have else pl.ds(z, 1)
                device = here.dev(z, y, 1 - x) if dim == "x" else here.dev(z, 1 - y, x)
                stages.append([(None, None, in_z, in_y, in_x, cols, device, slot)])
                slot += 1
            have.add(dim)
        parts.append(stages)

    def copy(move, g):
        _, _, in_z, in_y, in_x, cols, device, at = move
        ref = blocks.at[g, in_z, in_y, in_x, :, cols]
        return pltpu.make_async_remote_copy(
            ref, ref, send.at[g, at], recv.at[g, at], device_id=(device,), device_id_type=MESH
        )

    return parts, copy, slot


def gather_visit(parts, copy, v):
    for k in range(STAGES, -1, -1):
        for part, stages in enumerate(parts):

            def step(g, k=k, stages=stages):
                if k > 0:
                    for move in stages[k - 1]:
                        when(move[1], lambda move=move: copy(move, g).wait_recv())
                if k < STAGES:
                    for move in stages[k]:
                        when(move[0], lambda move=move: copy(move, g).start())

            g = v - GATHER_DELAY[part][k]
            if not isinstance(v, int):
                pl.when((g > 0) & (g < GROUPS))(functools.partial(step, g))
                continue
            if v == k:
                step(0)
            if 0 < g < GROUPS:
                step(g)


def gather_drain(parts, copy):
    def body(g, _):
        for stages in parts:
            for moves in stages:
                for move in moves:
                    when(move[0], lambda move=move: copy(move, g).wait_send())
        return 0

    lax.fori_loop(0, GROUPS, body, 0)


def shift_line(table, rel, head):
    line = jnp.zeros(table.shape, F32)
    for bucket in range(rel.shape[0]):
        line = jnp.where(table == bucket, rel[bucket, head], line)
    return line


def gelu_parts(v):
    root = math.sqrt(2.0 / math.pi)
    sq = v * v
    t = jnp.tanh(root * (v + 0.044715 * (sq * v)))
    half = 0.5 * (1.0 + t)
    value = v * half
    slope = half + 0.5 * v * (1.0 - t * t) * (root * (1.0 + 3 * 0.044715 * sq))
    return value, slope


def row_norm(v):
    return lax.rsqrt(jnp.mean(v * v, axis=-1, keepdims=True) + EPS)


REACH = (4, -4)


class Halo:
    def __init__(self, here, ref, send, recv):
        self.here, self.ref, self.send, self.recv = here, ref, send, recv
        self.rows = ref.shape[-2] // 5
        even = here.x == 0
        self.even = even
        self.partner = here.me + 1 - 2 * here.c
        self.across = here.me + jnp.where(even, 2, -2)
        self.near = jnp.where(even, 4, 0)
        self.far = 4 - self.near
        step = jnp.where(even, 4, -4)
        self.to_far = inside(here.me + step, here.n)
        self.from_far = inside(here.me - step, here.n)
        self.far_device = jnp.clip(here.me + step, 0, here.n - 1)
        core0 = here.c == 0
        self.has_prev, self.has_next = here.me >= 2, here.me < here.n - 2
        self.over = jnp.where(core0, self.has_next, self.has_prev)
        self.under = jnp.where(core0, self.has_prev, self.has_next)

    def part(self, slot, piece):
        at = pl.ds(pl.multiple_of(slot * self.rows, self.rows), self.rows)
        return self.ref.at[at] if piece is None else self.ref.at[piece, at]

    def move(self, kind, piece):
        c, j = self.here.c, 0 if piece is None else piece
        src, dst, device = (
            (2, self.far, self.across),
            (self.near, self.far, self.far_device),
            (2, jnp.where(c == 0, 1, 3), self.partner),
            (jnp.where(c == 0, 4, 0), jnp.where(c == 0, 3, 1), self.partner),
        )[kind]
        return pltpu.make_async_remote_copy(
            self.part(src, piece), self.part(dst, piece), self.send.at[j, kind], self.recv.at[j, kind],
            device_id=(device,), device_id_type=MESH,
        )

    def begin(self, piece=None):
        self.move(0, piece).start()
        self.move(2, piece).start()

    def forward(self, piece=None):
        self.move(0, piece).wait_recv()
        when(self.to_far, lambda: self.move(1, piece).start())

    def spread(self, piece=None):
        when(self.from_far, lambda: self.move(1, piece).wait_recv())
        when(self.over, lambda: self.move(3, piece).start())

    def settle(self, piece=None):
        self.move(2, piece).wait_recv()
        when(self.under, lambda: self.move(3, piece).wait_recv())

    def close(self, piece=None):
        self.move(0, piece).wait_send()
        self.move(2, piece).wait_send()
        when(self.to_far, lambda: self.move(1, piece).wait_send())
        when(self.over, lambda: self.move(3, piece).wait_send())

    def absent(self):
        core0 = self.here.c == 0
        no_prev, no_next = jnp.logical_not(self.has_prev), jnp.logical_not(self.has_next)
        return ((no_prev, 0), (no_next, 4), (no_prev & core0, 1), (no_next & jnp.logical_not(core0), 3))


def forward_kernel(
    n, heads,
    slab, hid, dy, qx, table, rel, gains,
    o_grads, o_outp, o_dn2p, o_x1, o_at, o_q, o_kv, o_kx, o_lse, o_ga,
    G, ga, n2f, dyf, kv, kx, qv, x1, at, lse,
    gs, gr, lsem, hs, hr, ks, kr, cs, cr, osem, stsem,
):
    here = Place(n)
    c = here.c
    rows, D = hid.shape
    inner = qv.shape[1]
    nz = here.grid[0]
    partner = here.me + 1 - 2 * c
    window = kx.shape[0]
    tiles = rows // 256
    span = (window - rows) + 256
    mine = pl.ds(pl.multiple_of(c * rows, rows), rows)
    centre = pl.ds(2 * rows, rows)

    def to_partner(src, dst, i):
        return pltpu.make_async_remote_copy(
            src, dst, cs.at[i], cr.at[i], device_id=(partner,), device_id_type=MESH
        )

    kv_halo, kx_halo = Halo(here, kv, hs, hr), Halo(here, kx, ks, kr)

    own = [
        pltpu.make_async_copy(slab.at[g], G.at[g, here.z, here.y, here.x], lsem.at[g])
        for g in range(GROUPS)
    ]
    for copy in own:
        copy.start()
    kx_in = pltpu.make_async_copy(qx.at[:, 0:128], kx.at[centre], lsem.at[GROUPS])
    kx_in.start()
    dy_in = pltpu.make_async_copy(dy, dyf.at[mine], lsem.at[GROUPS + 1])
    dy_in.start()
    here.barrier(REACH)
    for copy in own:
        copy.wait()
    parts, copy, _ = gather_stages(here, G, gs, gr, D)
    ag = lambda v: gather_visit(parts, copy, v)
    ag(0)
    kx_in.wait()
    kx_halo.begin()
    dy_in.wait()
    dy_out = to_partner(dyf.at[mine], dyf.at[mine], 0)
    dy_out.start()
    edge = jnp.where(lax.broadcasted_iota(jnp.int32, (rows, 128), 1) == 25, -BIG, 0.0).astype(BF)
    for cond, slot in kv_halo.absent():
        def absent(slot=slot):
            at_rows = pl.ds(slot * rows, rows)
            kx[at_rows, :] = edge
            for hp in range(heads // 2):
                kv[hp, at_rows, :] = jnp.zeros((rows, 256), BF)

        pl.when(cond)(absent)

    def attention(n1, bias, vt, S, Pm):
        ag(1)

        def norm_rows(i, _):
            at_rows = pl.ds(i * 64, 64)
            v = hid[at_rows, :].astype(F32)
            n1[at_rows, :] = (v * row_norm(v) * gains[0:1, :]).astype(BF)
            return 0

        lax.fori_loop(0, rows // 64, norm_rows, 0)
        ag(2)
        kx_halo.forward()
        for head in range(heads):
            line = shift_line(table[...], rel, head)
            for b in range(bias.shape[1] // 128):
                lo = line[19 - b : 20 - b, :]
                hi = line[18 - b : 19 - b, :]
                both = jnp.broadcast_to(jnp.concatenate([lo, hi], 1), (128, 256))
                bias[head, 128 * b : 128 * b + 128, :] = pltpu.roll(both, 0, 1, stride=1, stride_axis=0)[:, :128]
            if head == 1:
                ag(3)
                kx_halo.spread()
            if head == 3:
                ag(4)
                kx_halo.settle()
        ag(5)
        keep = pltpu.make_async_copy(G.at[0], ga.at[:, :, :, c], lsem.at[GROUPS + 2])
        keep.start()
        give = to_partner(G.at[0], ga.at[:, :, :, c], 1)
        give.start()
        keep.wait()
        give.wait_recv()
        ga_out = pltpu.make_async_copy(ga, o_ga, osem.at[1])
        ga_out.start()

        for part in (1, 2, 0):
            weight = ga[part].reshape(inner, D)
            for half in range(rows // 256):
                at_rows = pl.ds(256 * half, 256)
                got = nt(n1[at_rows, :], weight).astype(BF)
                if part == 0:
                    qv[at_rows, :] = got
                    continue
                for hp in range(heads // 2):
                    kv[hp, pl.ds(2 * rows + 256 * half, 256), 128 * (part - 1) : 128 * part] = got[
                        :, 128 * hp : 128 * hp + 128
                    ]
            if part == 2:
                for hp in range(heads // 2):
                    kv_halo.begin(hp)
        kx_out = pltpu.make_async_copy(kx, o_kx, osem.at[3])
        kx_out.start()
        q_out = pltpu.make_async_copy(qv, o_q, osem.at[4])
        q_out.start()
        ag(6)
        kv_halo.forward(0)
        kv_halo.forward(1)
        kv_halo.spread(0)
        kv_halo.forward(2)
        kv_halo.settle(0)
        lane = lax.broadcasted_iota(jnp.int32, (256, 128), 1) // 64

        def pair(hp, _):
            @pl.when(hp > 0)
            def _():
                kv_halo.settle(hp)

            cols = pl.ds(pl.multiple_of(hp * 128, 128), 128)

            def turn(i, _):
                at_rows = pl.ds(pl.multiple_of(i * 256, 256), 256)
                vt[:, at_rows] = kv[hp, at_rows, 128:256].T
                return 0

            lax.fori_loop(0, window // 256, turn, 0)

            def one(k, _):
                @pl.when((k == 1) & (hp == 1))
                def _():
                    ag(7)

                t, e = k // 2, k % 2
                base = pl.multiple_of(t * 256, 256)
                head = hp * 2 + e
                q = qv[pl.ds(base, 256), cols]
                q = jnp.where(lane == e, q, jnp.zeros_like(q))
                qa = jnp.concatenate([q, qx[pl.ds(base, 256), 128:256]], 1)

                def score(b, m):
                    at_rows = pl.ds(pl.multiple_of(base + b * 256, 256), 256)
                    ka = jnp.concatenate([kv[hp, at_rows, 0:128], kx[at_rows, :]], 1)
                    s = nt(ka, qa)
                    low = pl.multiple_of(b * 256, 256)
                    plane = jnp.concatenate(
                        [bias[head, pl.ds(low + 128, 256), :], bias[head, pl.ds(low, 256), :]], 1
                    )
                    s = s + plane
                    S[pl.ds(low, 256), :] = s
                    return jnp.maximum(m, jnp.max(s.reshape(32, 8, 256), axis=0))

                m = lax.fori_loop(0, span // 256, score, jnp.full((8, 256), -3e38, F32), unroll=True)
                m = jnp.max(m, axis=0, keepdims=True)

                def weigh(b, total):
                    at_rows = pl.ds(pl.multiple_of(b * 256, 256), 256)
                    p = jnp.exp(S[at_rows, :] - m)
                    Pm[at_rows, :] = p.astype(BF)
                    return total + jnp.sum(p.reshape(32, 8, 256), axis=0)

                total = lax.fori_loop(0, span // 256, weigh, jnp.zeros((8, 256), F32), unroll=True)
                total = jnp.sum(total, axis=0, keepdims=True)
                out_rows = pl.ds(pl.multiple_of(head * 64, 64), 64)
                mixed = nn(vt[pl.ds(pl.multiple_of(e * 64, 64), 64), pl.ds(base, span)], Pm[...])
                at[out_rows, pl.ds(base, 256)] = mixed / total
                lse[pl.ds(head, 1), pl.ds(base, 256)] = m + jnp.log(total)
                return 0

            lax.fori_loop(0, 2 * tiles, one, 0)

            @pl.when(hp < heads // 2 - 1)
            def _():
                kv_halo.spread(hp + 1)

            return 0

        lax.fori_loop(0, heads // 2, pair, 0)
        kv_out = pltpu.make_async_copy(kv, o_kv, osem.at[2])
        kv_out.start()
        outs = [
            pltpu.make_async_copy(at, o_at, osem.at[5]),
            pltpu.make_async_copy(lse, o_lse, osem.at[6]),
        ]
        for o in outs:
            o.start()
        w_out = ga[3].reshape(inner, D)

        def after(i, _):
            at_rows = pl.ds(pl.multiple_of(i * 128, 128), 128)
            a = at[:, at_rows].T.astype(BF)
            v = hid[at_rows, :].astype(F32) + nn(a, w_out)
            x1[at_rows, :] = v
            n2f[pl.ds(pl.multiple_of(c * rows + i * 128, 128), 128), :] = (v * row_norm(v) * gains[1:2, :]).astype(BF)
            return 0

        lax.fori_loop(0, rows // 128, after, 0)
        n2_out = to_partner(n2f.at[mine], n2f.at[mine], 2)
        n2_out.start()
        x1_out = pltpu.make_async_copy(x1, o_x1, osem.at[7])
        x1_out.start()
        give.wait_send()
        n2_out.wait()
        dy_out.wait()
        kx_halo.close()
        for hp in range(heads // 2):
            kv_halo.close(hp)
        for o in outs + [ga_out, kv_out, kx_out, q_out, x1_out]:
            o.wait()

    pl.run_scoped(
        attention,
        pltpu.VMEM((rows, D), BF),
        pltpu.VMEM((heads, span + 128, 128), F32),
        pltpu.VMEM((128, window), BF),
        pltpu.VMEM((span, 256), F32),
        pltpu.VMEM((span, 256), BF),
    )

    def feed(acc_o, acc_n, ft, gt, ut, stage):
        acc_o[...] = jnp.zeros_like(acc_o)
        acc_n[...] = jnp.zeros_like(acc_n)

        def acc_out(i):
            at_rows = pl.ds(pl.multiple_of(i * 256, 256), 256)
            return (
                pltpu.make_async_copy(acc_o.at[at_rows], o_outp.at[at_rows], osem.at[i]),
                pltpu.make_async_copy(acc_n.at[at_rows], o_dn2p.at[at_rows], osem.at[4 + i]),
            )

        def stage_out(j):
            return pltpu.make_async_copy(stage.at[j % 2], o_grads.at[j + 1], stsem.at[j % 2])

        def chunk(j, _):
            ag(j + 8)
            g = j + 1
            wg = G.at[g, :, :, :, pl.ds(0, 16), :]
            wu = G.at[g, :, :, :, pl.ds(16, 16), :]
            wd = G.at[g, :, :, :, pl.ds(32, 16), :]
            whole = lambda ref: ref[...].reshape(256, D)

            def tokens(i, _):
                at_rows = pl.ds(pl.multiple_of(i * 256, 256), 256)
                n2 = n2f[at_rows, :]
                gate = nt(whole(wg), n2)
                up = nt(whole(wu), n2)
                df = nt(whole(wd), dyf[at_rows, :])
                value, slope = gelu_parts(gate)
                f = (value * up).astype(BF)
                dg = (df * up * slope).astype(BF)
                du = (df * value).astype(BF)
                ft[:, at_rows] = f
                gt[:, at_rows] = dg
                ut[:, at_rows] = du
                acc_o[at_rows, :] += nn(f.T, whole(wd))
                acc_n[at_rows, :] += nn(dg.T, whole(wg)) + nn(du.T, whole(wu))

                @pl.when(j == GROUPS - 2)
                def _():
                    for o in acc_out(i):
                        o.start()

                return 0

            lax.fori_loop(0, 2 * rows // 256, tokens, 0, unroll=2)

            @pl.when(j >= 2)
            def _():
                stage_out(j - 2).wait()

            s = j % 2
            stage[s, :, :, :, 0:16, :] = nn(gt[...], n2f[...]).astype(BF).reshape(here.grid + (16, D))
            stage[s, :, :, :, 16:32, :] = nn(ut[...], n2f[...]).astype(BF).reshape(here.grid + (16, D))
            stage[s, :, :, :, 32:48, :] = nn(ft[...], dyf[...]).astype(BF).reshape(here.grid + (16, D))
            stage_out(j).start()
            return 0

        lax.fori_loop(0, GROUPS - 1, chunk, 0)
        gather_drain(parts, copy)
        for i in range(2 * rows // 256):
            for o in acc_out(i):
                o.wait()
        stage_out(GROUPS - 3).wait()
        stage_out(GROUPS - 2).wait()

    pl.run_scoped(
        feed,
        pltpu.VMEM((2 * rows, D), F32),
        pltpu.VMEM((2 * rows, D), F32),
        pltpu.VMEM((256, 2 * rows), BF),
        pltpu.VMEM((256, 2 * rows), BF),
        pltpu.VMEM((256, 2 * rows), BF),
        pltpu.VMEM((2,) + here.grid + (PIECE, D), BF),
    )


def forward_call(n, heads, slab, hid, dy, qx, table, rel, gains):
    rows, D = hid.shape
    inner = heads * 64
    zs, ys, xs = GRIDS[n]
    window = 5 * rows
    span = window - rows + 256
    shape = jax.ShapeDtypeStruct
    any_, vm = pl.BlockSpec(memory_space=pl.ANY), pl.BlockSpec(memory_space=pltpu.VMEM)
    sm = pl.BlockSpec(memory_space=pltpu.SMEM)
    slots = 3 * 8
    dma = pltpu.SemaphoreType.DMA
    return pl.pallas_call(
        functools.partial(forward_kernel, n, heads),
        out_shape=(
            shape((GROUPS, zs, ys, xs, PIECE, D), BF),
            shape((2 * rows, D), F32),
            shape((2 * rows, D), F32),
            shape((rows, D), F32),
            shape((inner, rows), F32),
            shape((rows, inner), BF),
            shape((heads // 2, window, 256), BF),
            shape((window, 128), BF),
            shape((8, rows), F32),
            shape((zs, ys, xs, 2, PIECE, D), BF),
        ),
        in_specs=[any_, vm, any_, vm, vm, sm, vm],
        out_specs=(any_,) * 10,
        scratch_shapes=[
            pltpu.VMEM((GROUPS, zs, ys, xs, PIECE, D), BF),
            pltpu.VMEM((zs, ys, xs, 2, PIECE, D), BF),
            pltpu.VMEM((2 * rows, D), BF),
            pltpu.VMEM((2 * rows, D), BF),
            pltpu.VMEM((heads // 2, window, 256), BF),
            pltpu.VMEM((window, 128), BF),
            pltpu.VMEM((rows, inner), BF),
            pltpu.VMEM((rows, D), F32),
            pltpu.VMEM((inner, rows), F32),
            pltpu.VMEM((8, rows), F32),
            dma((GROUPS, slots)), dma((GROUPS, slots)),
            dma((GROUPS + 3,)),
            dma((heads // 2, 4)), dma((heads // 2, 4)), dma((1, 4)), dma((1, 4)),
            dma((3,)), dma((3,)),
            dma((8,)), dma((2,)),
        ],
        compiler_params=pltpu.CompilerParams(
            collective_id=1, has_side_effects=True, vmem_limit_bytes=63 * 2**20
        ),
        cost_estimate=pl.CostEstimate(flops=55 * 10**9, bytes_accessed=80 * 10**6, transcendentals=10**7),
        name="forward",
    )(slab, hid, dy, qx, table, rel, gains)


def prepare(hidden, segments, delete_mask, bucket_table, attn_weight, gate_weight, up_weight, down_weight):
    D = hidden.shape[1]
    rows = hidden.shape[0]
    groups = GROUPS - 1
    ffn = jnp.stack([gate_weight.T, up_weight.T, down_weight]).reshape(3, groups, 16, D)
    ffn = jnp.transpose(ffn, (1, 0, 2, 3)).reshape(groups, PIECE, D)
    slab = jnp.concatenate([attn_weight.T[None], ffn], 0)
    wide = jnp.arange(256, dtype=jnp.int32)[None, :]
    lane = wide % 128
    seg = segments[:, None]
    digit = jnp.where(lane < 9, seg % 8, jnp.where(lane < 17, (seg // 8) % 8, seg // 64))
    hit = digit == (lane - 1) % 8
    coded = (lane >= 1) & (lane < 25)
    key = jnp.where(lane == 0, delete_mask.astype(F32)[:, None], jnp.where(coded & ~hit, -BIG, 0.0))
    query = jnp.where((lane == 0) | (lane == 25) | (coded & hit), 1.0, 0.0)
    codes = jnp.where(wide < 128, key, query).astype(BF)
    reach = bucket_table.shape[0]
    table = jnp.pad(jnp.flip(bucket_table), (257, 20 * 128 - 257 - reach), constant_values=-1).reshape(20, 128)
    table = jnp.pad(table, ((0, 4), (0, 0)), constant_values=-1)
    return slab, codes, table


FIRST = (1, 2, 3, 4, 5, 6, 7, 0)
AT = 7
AFTER = 10
SLOTS = 4
ZSLOTS = 4
WORK = 8
LINES = 56


def group_of(pos):
    if isinstance(pos, int):
        return FIRST[pos]
    return (pos + 1) % GROUPS


def add_into(dst, src):
    dst[...] = (dst[...].astype(F32) + src[...].astype(F32)).astype(BF)


class Scatter:
    def __init__(self, here, source, work, land, landa, landz, result, send, recv, load, width):
        self.here, self.source, self.work, self.result = here, source, work, result
        self.land, self.landa, self.landz = land, landa, landz
        self.send, self.recv, self.load = send, recv, load
        self.parts = column_parts(width)

    def loading(self, part, pos):
        here = self.here
        zs, ys, xs = here.grid
        in_y = pl.ds(here.y, 1) if part == 1 else pl.ds(0, ys)
        in_x = pl.ds(here.x, 1) if part == 2 else pl.ds(0, xs)
        cols = pl.ds(*self.parts[part])
        return pltpu.make_async_copy(
            self.source.at[group_of(pos), :, in_y, in_x, :, cols],
            self.work.at[pos % WORK, :, in_y, in_x, :, cols],
            self.load.at[pos, part],
        )

    def start_load(self, pos):
        for part in range(3):
            self.loading(part, pos).start()

    def moves(self, part, k, pos):
        here = self.here
        zs, ys, xs = here.grid
        z, y, x = here.z, here.y, here.x
        cols = pl.ds(*self.parts[part])
        dim = (("z0", "z1", "z2", "y", "x"), ("y", "x", "z0", "z1", "z2"), ("x", "y", "z0", "z1", "z2"))[part][k]
        work, source, g = self.work, self.source, group_of(pos)
        w, slot, zslot = pos % WORK, pos % SLOTS, pos % ZSLOTS
        base = 8 * part

        def remote(src, dst, at, device):
            return pltpu.make_async_remote_copy(
                src, dst, self.send.at[pos, at], self.recv.at[pos, at], device_id=(device,), device_id_type=MESH
            )

        if dim[0] == "z":
            step = int(dim[1])
            out = []
            for turn, way in enumerate((1, -1)):
                target = z + way * (zs - 1 - step)
                got = z + way * (zs - 2 - step)
                sends = inside(z + way, zs) & inside(target, zs)
                gets = inside(z - way, zs) & inside(got, zs)
                spot = step if turn == 0 or step == 0 else step + 2
                device = here.dev(jnp.clip(z + way, 0, zs - 1), y, x)
                block, mine = jnp.clip(target, 0, zs - 1), jnp.clip(got, 0, zs - 1)
                if part == 0:
                    src, dst = work.at[w, block, :, :, :, cols], self.landa.at[zslot, spot]
                else:
                    src, dst = work.at[w, block, y, x, :, cols], self.landz.at[zslot, spot, :, cols]

                def consume(mine=mine, dst=dst):
                    if part == 0:
                        for b in range(ys):
                            add_into(work.at[w, mine, b, :, :, cols], dst.at[b])
                    elif step < zs - 2:
                        add_into(work.at[w, mine, y, x, :, cols], dst)

                out.append((sends, gets, remote(src, dst, base + 2 + 2 * step + turn, device), consume))
            return out
        at = base + (0 if dim == "y" else 1)
        device = here.dev(z, 1 - y, x) if dim == "y" else here.dev(z, y, 1 - x)
        if k == 0 and dim == "y":
            src = source.at[g, :, pl.ds(1 - y, 1), :, :, cols]
            dst = work.at[w, :, pl.ds(y, 1), :, :, cols]
            pairs = [(work.at[w, b, y, :, :, cols], work.at[w, b, 1 - y, :, :, cols]) for b in range(zs)]
        elif k == 0:
            src = source.at[g, :, :, pl.ds(1 - x, 1), :, cols]
            dst = work.at[w, :, :, pl.ds(x, 1), :, cols]
            pairs = [(work.at[w, b, :, x, :, cols], work.at[w, b, :, 1 - x, :, cols]) for b in range(zs)]
        elif part != 0:
            src = work.at[w, :, y, 1 - x, :, cols] if dim == "x" else work.at[w, :, 1 - y, x, :, cols]
            dst = self.land.at[slot, :, :, cols]
            pairs = [(work.at[w, b, y, x, :, cols], self.land.at[slot, b, :, cols]) for b in range(zs)]
        elif dim == "y":
            src = work.at[w, z, 1 - y, :, :, cols]
            dst = self.land.at[slot, pl.ds(0, xs), :, cols]
            pairs = [(work.at[w, z, y, b, :, cols], self.land.at[slot, b, :, cols]) for b in range(xs)]
        else:
            src = work.at[w, z, y, 1 - x, :, cols]
            dst = self.land.at[slot, xs, :, cols]
            pairs = []

        def consume():
            for to, frm in pairs:
                add_into(to, frm)

        return [(None, None, remote(src, dst, at, device), consume)]

    def finish(self, part, pos):
        here = self.here
        zs, ys, xs = here.grid
        z, y, x = here.z, here.y, here.x
        slot, g = pos % SLOTS, group_of(pos)
        first, wide = self.parts[part]
        cols = pl.ds(first, wide)
        own = self.work[pos % WORK, z, y, x, :, cols].astype(F32)
        if part == 0:
            self.result[g, :, cols] = own + self.land[slot, xs, :, cols].astype(F32)
            return
        up = self.landz[pos % ZSLOTS, zs - 2, :, cols].astype(F32)
        down = self.landz[pos % ZSLOTS, zs, :, cols].astype(F32)
        self.result[g, :, cols] = own + jnp.where(z > 0, up, 0.0) + jnp.where(z < zs - 1, down, 0.0)

    def round(self, r):
        for k in range(STAGES, -1, -1):
            for part in range(3):

                def step(pos, k=k, part=part):
                    if k == (0 if part == 0 else 1):
                        self.loading(part, pos).wait()
                    if k > 0:
                        for _, gets, copy, consume in self.moves(part, k - 1, pos):
                            def take(copy=copy, consume=consume):
                                copy.wait_recv()
                                consume()

                            when(gets, take)
                    if k < STAGES:
                        for sends, _, copy, _ in self.moves(part, k, pos):
                            when(sends, lambda copy=copy: copy.start())
                        return
                    self.finish(part, pos)
                    for stage in range(STAGES):
                        for sends, _, copy, _ in self.moves(part, stage, pos):
                            when(sends, lambda copy=copy: copy.wait_send())

                pos = r - SCATTER_DELAY[part][k]
                if not isinstance(r, int):
                    pl.when(inside(pos, GROUPS - 1))(functools.partial(step, pos))
                    continue
                if 0 <= pos < GROUPS - 1:
                    step(pos)
                if r - AFTER == k:
                    step(AT)


def norm_back(v, gain, d):
    r = row_norm(v)
    vr = v * r
    dg = d * gain
    return r * (dg - vr * jnp.mean(vr * dg, axis=-1, keepdims=True)), d * vr


def put_line(small, first, line):
    width = line.shape[1]
    for i in range(-(-width // 128)):
        wide = min(128, width - 128 * i)
        small[first + i : first + i + 1, 0:wide] = line[:, 128 * i : 128 * i + wide]


def backward_kernel(
    n, heads,
    grads, outp, dn2p, x1_in, at_in, q_in, kv_in, kx_in, lse, ga_in,
    hid, dy, qx, table, rel, gains,
    gr, o_out, o_dh, o_res, o_small, dn_land, op_land,
    work, land, landa, landz, res, dx1, kv, kx, qv, at, ga, dat, das, back, fold, small, sland,
    ss, rs, lds, cs, cr, hs, hr, ls, ps, pr, osem,
):
    here = Place(n)
    c = here.c
    rows, D = dx1.shape
    inner = qv.shape[1]
    window = kx.shape[0]
    zs, ys, xs = here.grid
    z, y, x = here.z, here.y, here.x
    span = window - rows + 256
    partner = here.me + 1 - 2 * c
    mine = pl.ds(pl.multiple_of(c * rows, rows), rows)
    theirs = pl.ds(pl.multiple_of((1 - c) * rows, rows), rows)

    def to_partner(src, dst, i):
        return pltpu.make_async_remote_copy(
            src, dst, cs.at[i], cr.at[i], device_id=(partner,), device_id_type=MESH
        )

    def local(src, dst, i):
        return pltpu.make_async_copy(src, dst, ls.at[i])

    sc = Scatter(here, gr, work, land, landa, landz, res, ss, rs, lds, D)
    for pos in range(WORK):
        if pos != AT:
            sc.start_load(pos)
    loads = [
        local(dn2p.at[mine], dx1, 0), local(kv_in, kv, 1), local(kx_in, kx, 2),
        local(q_in, qv, 3), local(at_in, at, 4), local(ga_in, ga, 5),
    ]
    for load in loads:
        load.start()
    here.barrier(REACH, True)
    dn_out = to_partner(dn2p.at[theirs], dn_land, 0)
    dn_out.start()
    sc.round(0)
    op_out = to_partner(outp.at[theirs], op_land, 1)
    op_out.start()
    small[...] = jnp.zeros_like(small)

    def after_ffn(x1, other, grad, low):
        first = [local(x1_in, x1, 6), local(dy, grad, 7)]
        for load in first:
            load.start()
        dn_out.wait_recv()
        second = local(dn_land, other, 8)
        second.start()
        sc.round(1)
        for load in loads + first + [second]:
            load.wait()
        w_out = ga[zs - 1].reshape(inner, D)

        def through(i, total):
            at_rows = pl.ds(pl.multiple_of(i * 128, 128), 128)
            d = dx1[at_rows, :] + other[at_rows, :]
            back_v, gain_d = norm_back(x1[at_rows, :], gains[1:2, :], d)
            v = grad[at_rows, :].astype(F32) + back_v
            dx1[at_rows, :] = v
            v = v.astype(BF)
            low[at_rows, :] = v
            da = nt(v, w_out).astype(BF)
            das[at_rows, :] = da
            dat[:, at_rows] = da.T
            return total + jnp.sum(gain_d.reshape(16, 8, D), axis=0)

        total = lax.fori_loop(0, rows // 128, through, jnp.zeros((8, D), F32))
        put_line(small, 44, jnp.sum(total, axis=0, keepdims=True))
        third = local(outp.at[mine], other, 9)
        third.start()
        sc.round(2)
        for h in range(2):
            part = nn(at[pl.ds(h * (inner // 2), inner // 2), :].astype(BF), low[...])
            ga[zs - 1, h] = part.astype(BF).reshape(xs, 2, PIECE, D)
        third.wait()
        op_out.wait_recv()

        def add(i, _):
            at_rows = pl.ds(pl.multiple_of(i * 64, 64), 64)
            x1[at_rows, :] = x1[at_rows, :] + other[at_rows, :]
            return 0

        lax.fori_loop(0, rows // 64, add, 0)
        fourth = local(op_land, other, 10)
        fourth.start()
        fourth.wait()

        def put(i, _):
            at_rows = pl.ds(pl.multiple_of(i * 64, 64), 64)
            low[at_rows, :] = (x1[at_rows, :] + other[at_rows, :]).astype(BF)
            return 0

        lax.fori_loop(0, rows // 64, put, 0)
        out = pltpu.make_async_copy(low, o_out, osem.at[0])
        out.start()
        out.wait()
        dn_out.wait_send()
        op_out.wait_send()

    pl.run_scoped(
        after_ffn, pltpu.VMEM((rows, D), F32), pltpu.VMEM((rows, D), F32), pltpu.VMEM((rows, D), BF),
        pltpu.VMEM((rows, D), BF),
    )

    way = Halo(here, kx, hs, hr)

    def home(dkv, hp, kind):
        src, device = (
            (jnp.where(c == 0, 1, 3), partner),
            (jnp.where(c == 0, 3, 1), partner),
            (way.far, jnp.clip(here.me - jnp.where(way.even, 4, -4), 0, n - 1)),
            (way.near, way.across),
        )[kind]
        return pltpu.make_async_remote_copy(
            dkv.at[hp, pl.ds(pl.multiple_of(src * rows, rows), rows)],
            back.at[hp, kind],
            hs.at[hp, kind],
            hr.at[hp, kind],
            device_id=(device,),
            device_id_type=MESH,
        )

    def add_back(dkv, hp, kind, slot):
        at_rows = pl.ds(pl.multiple_of(slot * rows, rows), rows)
        add_into(dkv.at[hp, at_rows], back.at[hp, kind])

    def home_begin(dkv, hp):
        when(way.under, lambda: home(dkv, hp, 0).start())
        home(dkv, hp, 1).start()

    def home_merge(dkv, hp):
        def merge():
            home(dkv, hp, 0).wait_recv()
            add_back(dkv, hp, 0, jnp.where(c == 0, 4, 0))

        when(way.over, merge)
        when(way.from_far, lambda: home(dkv, hp, 2).start())

    def home_cross(dkv, hp):
        def merge():
            home(dkv, hp, 2).wait_recv()
            add_back(dkv, hp, 2, way.near)

        when(way.to_far, merge)
        home(dkv, hp, 3).start()

    def home_close(dkv, hp):
        when(way.under, lambda: home(dkv, hp, 0).wait_send())
        home(dkv, hp, 1).wait_send()
        when(way.from_far, lambda: home(dkv, hp, 2).wait_send())
        home(dkv, hp, 3).wait_send()

    def pairs(dkv, dqt, acc_k, acc_v, skew, kt, bias):
        dqt[...] = jnp.zeros_like(dqt)
        lane = lax.broadcasted_iota(jnp.int32, (256, 128), 1) // 64
        lane_of = lax.broadcasted_iota(jnp.int32, (32, 128), 1)
        blocks = skew.shape[0] // 128

        def one_head(hp, e):
            head = hp * 2 + e
            pl.when(e == 0)(lambda: sc.round(3 + hp))
            cols = pl.ds(pl.multiple_of(hp * 128, 128), 128)
            out_rows = pl.ds(pl.multiple_of(head * 64, 64), 64)
            line = shift_line(table[...], rel, head)
            for b in range(blocks):
                both = jnp.concatenate([line[19 - b : 20 - b, :], line[18 - b : 19 - b, :]], 1)
                both = jnp.broadcast_to(both, (128, 256))
                bias[128 * b : 128 * b + 128, :] = pltpu.roll(both, 0, 1, stride=1, stride_axis=0)[:, :128]
            skew[...] = jnp.zeros_like(skew)

            def tile(t, _):
                base = pl.multiple_of(t * 256, 256)
                here_q = pl.ds(base, 256)
                q = qv[here_q, cols]
                q = jnp.where(lane == e, q, jnp.zeros_like(q))
                qa = jnp.concatenate([q, qx[here_q, 128:256]], 1)
                da = das[here_q, cols]
                da = jnp.where(lane == e, da, jnp.zeros_like(da))
                logs = lse[pl.ds(head, 1), here_q]
                delta = jnp.sum(dat[out_rows, here_q].astype(F32) * at[out_rows, here_q], axis=0, keepdims=True)

                def block(b, dq):
                    low = pl.multiple_of(b * 256, 256)
                    at_rows = pl.ds(pl.multiple_of(base + b * 256, 256), 256)
                    ka = jnp.concatenate([kv[hp, at_rows, 0:128], kx[at_rows, :]], 1)
                    plane = jnp.concatenate([bias[pl.ds(low + 128, 256), :], bias[pl.ds(low, 256), :]], 1)
                    p = jnp.exp(nt(ka, qa) + plane - logs)
                    ds = p * (nt(kv[hp, at_rows, 128:256], da) - delta)
                    skew[pl.ds(low + 128, 256), :] += ds[:, 0:128]
                    skew[pl.ds(low, 256), :] += ds[:, 128:256]
                    dsr = ds.astype(BF)
                    acc_v[at_rows, :] += nn(p.astype(BF), da)
                    acc_k[at_rows, :] += nn(dsr, q)
                    return dq + nn(kt[pl.ds(pl.multiple_of(e * 64, 64), 64), at_rows], dsr)

                dqt[out_rows, here_q] = lax.fori_loop(0, span // 256, block, jnp.zeros((64, 256), F32), unroll=True)
                return 0

            lax.fori_loop(0, rows // 256, tile, 0)
            tail = [None] * (blocks + 1)
            for b in range(blocks):
                a = jnp.concatenate([skew[128 * b : 128 * b + 128, :], jnp.zeros((128, 128), F32)], 1)
                half = 64
                while half >= 1:
                    a = a[0:half] + pltpu.roll(a[half : 2 * half], 256 - half, 1)
                    half //= 2
                for at_line, part in ((19 - b, a[:, 0:128]), (18 - b, a[:, 128:256])):
                    tail[at_line] = part if tail[at_line] is None else tail[at_line] + part
            line_d = jnp.concatenate(tail + [jnp.zeros((4, 128), F32)], 0)
            sums = [
                jnp.sum(jnp.where(table[...] == b, line_d, 0.0), axis=0, keepdims=True) for b in range(rel.shape[0])
            ]
            sums = jnp.sum(jnp.concatenate(sums, 0), axis=1, keepdims=True)
            small[0:32, :] = jnp.where(lane_of == head, sums, small[0:32, :])

        def pair(hp, _):
            acc_k[...] = jnp.zeros_like(acc_k)
            acc_v[...] = jnp.zeros_like(acc_v)

            def turn(i, _):
                at_rows = pl.ds(pl.multiple_of(i * 256, 256), 256)
                kt[:, at_rows] = kv[hp, at_rows, 0:128].T
                return 0

            lax.fori_loop(0, window // 256, turn, 0)
            lax.fori_loop(0, 2, lambda e, _: (one_head(hp, e), 0)[1], 0)

            def pack(i, _):
                at_rows = pl.ds(pl.multiple_of(i * 128, 128), 128)
                dkv[hp, at_rows, 0:128] = acc_k[at_rows, :].astype(BF)
                dkv[hp, at_rows, 128:256] = acc_v[at_rows, :].astype(BF)
                return 0

            lax.fori_loop(0, window // 128, pack, 0)
            home_begin(dkv, hp)
            pl.when(hp >= 1)(lambda: home_merge(dkv, hp - 1))
            pl.when(hp >= 2)(lambda: home_cross(dkv, hp - 2))
            return 0

        lax.fori_loop(0, heads // 2, pair, 0)
        last = heads // 2 - 1
        home_cross(dkv, last - 1)
        home_merge(dkv, last)
        sc.round(6)

    def to_weights(dkv, dqt, n1, proj, proj_t, hid_v):
        hid_in = local(hid, hid_v, 11)
        hid_in.start()
        hid_in.wait()

        def norm_rows(i, _):
            at_rows = pl.ds(pl.multiple_of(i * 64, 64), 64)
            v = hid_v[at_rows, :].astype(F32)
            n1[at_rows, :] = (v * row_norm(v) * gains[0:1, :]).astype(BF)
            return 0

        lax.fori_loop(0, rows // 64, norm_rows, 0)

        def gather_pair(hp, _):
            home(dkv, hp, 1).wait_recv()
            home(dkv, hp, 3).wait_recv()

            def sum_rows(j, _):
                at_rows = pl.ds(pl.multiple_of(j * 128, 128), 128)
                total = dkv[hp, pl.ds(pl.multiple_of(2 * rows + j * 128, 128), 128), :].astype(F32)
                for i in (1, 3):
                    total = total + back[hp, i, at_rows, :].astype(F32)
                total = total.astype(BF)
                for part in range(2):
                    piece = total[:, 128 * part : 128 * part + 128]
                    to = pl.ds(pl.multiple_of((1 + part) * inner + hp * 128, 128), 128)
                    proj[at_rows, to] = piece
                    proj_t[to, at_rows] = piece.T
                to = pl.ds(pl.multiple_of(hp * 128, 128), 128)
                piece = dqt[to, at_rows].astype(BF)
                proj_t[to, at_rows] = piece
                proj[at_rows, to] = piece.T
                return 0

            lax.fori_loop(0, rows // 128, sum_rows, 0)
            return 0

        last = heads // 2 - 1
        sc.round(7)
        lax.fori_loop(0, last, gather_pair, 0)
        home_cross(dkv, last)
        sc.round(8)
        gather_pair(last, 0)

        def to_hidden(i, total):
            at_rows = pl.ds(pl.multiple_of(i * 128, 128), 128)
            d = nn(proj[at_rows, 0:inner], ga[0].reshape(inner, D))
            d = d + nn(proj[at_rows, inner : 2 * inner], ga[1].reshape(inner, D))
            d = d + nn(proj[at_rows, 2 * inner : 3 * inner], ga[2].reshape(inner, D))
            back_v, gain_d = norm_back(hid_v[at_rows, :].astype(F32), gains[0:1, :], d)
            dx1[at_rows, :] = dx1[at_rows, :] + back_v
            return total + jnp.sum(gain_d.reshape(16, 8, D), axis=0)

        total = lax.fori_loop(0, rows // 128, to_hidden, jnp.zeros((8, D), F32))
        put_line(small, 32, jnp.sum(total, axis=0, keepdims=True))
        dh_out = pltpu.make_async_copy(dx1, o_dh, osem.at[1])
        dh_out.start()
        sc.round(9)

        for part in range(3):
            for h in range(2):
                take = pl.ds(part * inner + h * (inner // 2), inner // 2)
                ga[part, h] = nn(proj_t[take, :], n1[...]).astype(BF).reshape(xs, 2, PIECE, D)
        for hp in range(heads // 2):
            home_close(dkv, hp)
        dh_out.wait()

    def attention(dkv, dqt):
        pl.run_scoped(
            functools.partial(pairs, dkv, dqt),
            pltpu.VMEM((window, 128), F32), pltpu.VMEM((window, 128), F32), pltpu.VMEM((span + 128, 128), F32),
            pltpu.VMEM((128, window), BF), pltpu.VMEM((span + 128, 128), F32),
        )
        pl.run_scoped(
            functools.partial(to_weights, dkv, dqt),
            pltpu.VMEM((rows, D), BF), pltpu.VMEM((rows, 3 * inner), BF), pltpu.VMEM((3 * inner, rows), BF),
            pltpu.VMEM((rows, D), BF),
        )

    pl.run_scoped(attention, pltpu.VMEM((heads // 2, window, 256), BF), pltpu.VMEM((inner, rows), F32))

    fold_out = to_partner(ga.at[:, :, :, 1 - c], fold, 2)
    fold_out.start()
    def small_to(src, slot, device, i):
        return pltpu.make_async_remote_copy(
            src, sland.at[slot], ps.at[i], pr.at[i], device_id=(device,), device_id_type=MESH
        )

    swap = small_to(small, 0, partner, 0)
    swap.start()
    fold_out.wait()
    for a in range(zs):
        for b in range(ys):
            add_into(fold.at[a, b], ga.at[a, b, :, c])
    fold_in = pltpu.make_async_copy(fold, gr.at[0], osem.at[2])
    fold_in.start()
    fold_in.wait()
    sc.start_load(AT)
    sc.round(10)
    swap.wait()
    small[...] = small[...] + sland[0]
    swap = small_to(small, 1, here.dev(z, y, 1 - x), 1)
    swap.start()
    sc.round(11)
    swap.wait()
    small[...] = small[...] + sland[1]
    swap = small_to(small, 2, here.dev(z, 1 - y, x), 2)
    swap.start()
    sc.round(12)
    swap.wait()
    small[...] = small[...] + sland[2]
    swaps = []
    for far in range(1, zs):
        swaps.append(small_to(small, 3 + far, here.dev((z + far) % zs, y, x), 2 + far))
        swaps[-1].start()
    sc.round(13)
    for swap in swaps:
        swap.wait()
    sland[3] = small[...]
    ordered = jnp.zeros(small.shape, F32)
    for plane in range(zs):
        ordered = ordered + sland[3 + (z - plane + zs) % zs]
    small[...] = ordered
    small_out = pltpu.make_async_copy(small, o_small, osem.at[3])
    small_out.start()
    for r in range(14, AFTER + STAGES + 1):
        sc.round(r)
    res_out = pltpu.make_async_copy(res, o_res, osem.at[4])
    res_out.start()
    res_out.wait()
    small_out.wait()


def backward_call(n, heads, kept, hid, dy, qx, table, rel, gains):
    grads, outp, dn2p, x1, at, q, kv, kx, lse, ga = kept
    rows, D = hid.shape
    inner = heads * 64
    zs, ys, xs = GRIDS[n]
    window = 5 * rows
    shape = jax.ShapeDtypeStruct
    any_, vm = pl.BlockSpec(memory_space=pl.ANY), pl.BlockSpec(memory_space=pltpu.VMEM)
    sm = pl.BlockSpec(memory_space=pltpu.SMEM)
    dma = pltpu.SemaphoreType.DMA
    return pl.pallas_call(
        functools.partial(backward_kernel, n, heads),
        out_shape=(
            shape(grads.shape, BF),
            shape((rows, D), BF),
            shape((rows, D), F32),
            shape((GROUPS, PIECE, D), F32),
            shape((LINES, 128), F32),
            shape((rows, D), F32),
            shape((rows, D), F32),
        ),
        in_specs=[any_] * 8 + [vm] + [any_] * 3 + [vm, vm, sm, vm],
        out_specs=(any_,) * 7,
        input_output_aliases={0: 0},
        scratch_shapes=[
            pltpu.VMEM((WORK, zs, ys, xs, PIECE, D), BF),
            pltpu.VMEM((SLOTS, zs, PIECE, D), BF),
            pltpu.VMEM((ZSLOTS, 5, ys, xs, PIECE, 384), BF),
            pltpu.VMEM((ZSLOTS, 5, PIECE, D), BF),
            pltpu.VMEM((GROUPS, PIECE, D), F32),
            pltpu.VMEM((rows, D), F32),
            pltpu.VMEM((heads // 2, window, 256), BF),
            pltpu.VMEM((window, 128), BF),
            pltpu.VMEM((rows, inner), BF),
            pltpu.VMEM((inner, rows), F32),
            pltpu.VMEM((zs, ys, xs, 2, PIECE, D), BF),
            pltpu.VMEM((inner, rows), BF),
            pltpu.VMEM((rows, inner), BF),
            pltpu.VMEM((heads // 2, 4, rows, 256), BF),
            pltpu.VMEM((zs, ys, xs, PIECE, D), BF),
            pltpu.VMEM((LINES, 128), F32),
            pltpu.VMEM((3 + zs, LINES, 128), F32),
            dma((GROUPS, 24)), dma((GROUPS, 24)), dma((GROUPS, 3)),
            dma((3,)), dma((3,)),
            dma((heads // 2, 4)), dma((heads // 2, 4)),
            dma((12,)),
            dma((3 + zs,)), dma((3 + zs,)),
            dma((5,)),
        ],
        compiler_params=pltpu.CompilerParams(
            collective_id=2, has_side_effects=True, vmem_limit_bytes=63 * 2**20
        ),
        cost_estimate=pl.CostEstimate(flops=12 * 10**9, bytes_accessed=60 * 10**6, transcendentals=10**7),
        name="backward",
    )(grads, outp, dn2p, x1, at, q, kv, kx, lse, ga, hid, dy, qx, table, rel, gains)


def shards(
    n, hidden, segments, delete_mask, bucket_table, attn_weight, gate_weight, up_weight, down_weight,
    norm_attn, norm_ffn, rel_bias, out_grad,
):
    heads = rel_bias.shape[1]
    D = hidden.shape[1]
    slab, qx, table = prepare(
        hidden, segments, delete_mask, bucket_table, attn_weight, gate_weight, up_weight, down_weight
    )
    gains = jnp.stack([norm_attn, norm_ffn])
    kept = forward_call(n, heads, slab, hidden, out_grad, qx, table, rel_bias, gains)
    _, output, d_hidden, res, small, _, _ = backward_call(
        n, heads, kept, hidden, out_grad, qx, table, rel_bias, gains
    )
    ffn = res[1:].reshape(GROUPS - 1, 3, 16, D)
    mats = [ffn[:, i].reshape(-1, D) for i in range(3)]
    line = lambda first: small[first : first + 12].reshape(-1)[:D]
    return (
        output, d_hidden, res[0].T, mats[0].T, mats[1].T, mats[2], line(32), line(44), small[:32, :heads],
    )


def shifted(x, axis, by):
    count = lax.axis_size(axis)
    pairs = [(i, i + by) for i in range(count) if 0 <= i + by < count]
    return lax.ppermute(x, axis, pairs)


def shortened(x):

    def short(part):
        return part.astype(jnp.bfloat16) if part.dtype == jnp.float32 else part

    return jax.tree.map(short, x)


def rms_norm(value, gain):
    return value * lax.rsqrt(jnp.mean(value * value, axis=-1, keepdims=True) + 1e-06) * gain


def matmul(left, right):
    return jnp.dot(left, right, preferred_element_type=jnp.float32)


def matmul_tn(left, right):
    return lax.dot_general(
        left, right, (((0,), (0,)), ((), ())), preferred_element_type=jnp.float32
    )


def matmul_nt(left, right):
    return lax.dot_general(
        left, right, (((1,), (1,)), ((), ())), preferred_element_type=jnp.float32
    )


def gated_unit(gate_in, up_in):
    return jax.nn.gelu(gate_in) * up_in


def toeplitz(line, row_count, window):
    span_len = line.shape[0]
    tiled = jnp.tile(line, row_count)[: row_count * (span_len - 1)].reshape(row_count, span_len - 1)
    return tiled[:, :window]


def diagonal_sums(plane, span_len):
    row_count, window = plane.shape
    padded = jnp.pad(plane, ((0, 0), (0, span_len - 1 - window))).reshape(-1)
    padded = jnp.pad(padded, (0, row_count)).reshape(row_count, span_len)
    return jnp.sum(padded, axis=0)


def head_scores(q_head, k_head, mask_win, same_doc, bias_plane):
    raw = matmul_nt(q_head, k_head)
    scores = raw + bias_plane + mask_win[None, :]
    return jnp.where(same_doc, scores, -1e30)


def plain_shards(
    hidden,
    segments,
    delete_mask,
    bucket_table,
    attn_weight,
    gate_weight,
    up_weight,
    down_weight,
    norm_attn,
    norm_ffn,
    rel_bias,
    out_grad,
):
    row_count = hidden.shape[0]
    head_count = rel_bias.shape[1]
    bucket_count = rel_bias.shape[0]
    inner_width = attn_weight.shape[1] * lax.axis_size("seq") // 4
    head_width = inner_width // head_count
    table_len = bucket_table.shape[0]
    longest = (table_len + 1) // 2
    reach_blocks = (longest + row_count - 2) // row_count
    margin = reach_blocks * row_count
    window = (2 * reach_blocks + 1) * row_count
    span_len = row_count + window - 1
    w_attn, w_gate, w_up, w_down = (
        lax.all_gather(attn_weight, "seq", axis=1, tiled=True),
        lax.all_gather(gate_weight, "seq", axis=1, tiled=True),
        lax.all_gather(up_weight, "seq", axis=1, tiled=True),
        lax.all_gather(down_weight, "seq", axis=0, tiled=True),
    )
    residual = hidden.astype(jnp.float32)
    normed = rms_norm(residual, norm_attn).astype(jnp.bfloat16)
    projected = matmul(normed, w_attn[:, : 3 * inner_width]).astype(jnp.bfloat16)
    queries = projected[:, :inner_width]
    key_rows = projected[:, inner_width : 2 * inner_width]
    value_rows = projected[:, 2 * inner_width :]
    own_block = (key_rows, value_rows, segments + 1, delete_mask)
    both_sides = []
    for direction in (1, -1):
        current = own_block
        received = []
        for distance in range(reach_blocks):
            current = shifted((current[0], current[1], current[2], current[3]), "seq", direction)
            received.append(current)
        both_sides.append(received)
    ordered = both_sides[0][::-1] + [own_block] + both_sides[1]
    k_win = jnp.concatenate([portion[0] for portion in ordered], 0)
    v_win = jnp.concatenate([portion[1] for portion in ordered], 0)
    seg_win = jnp.concatenate([portion[2] for portion in ordered], 0)
    mask_win = jnp.concatenate([portion[3] for portion in ordered], 0).astype(jnp.float32)
    line_index = (jnp.arange(span_len, dtype=jnp.int32) + row_count - 1) % span_len
    line_offset = line_index - margin - (row_count - 1)
    line_bucket = jnp.take(
        bucket_table, jnp.clip(line_offset, 1 - longest, longest - 1) + longest - 1
    )
    line_onehot = (
        line_bucket[:, None] == jnp.arange(bucket_count, dtype=jnp.int32)[None, :]
    ).astype(jnp.float32)
    line_bias = jnp.dot(line_onehot, rel_bias, precision=lax.Precision.HIGHEST)
    same_doc = segments[:, None] + 1 == seg_win[None, :]
    mixed_parts = []
    log_parts = []
    for head in range(head_count):
        cols = slice(head * head_width, (head + 1) * head_width)
        bias_plane = toeplitz(line_bias[:, head], row_count, window)
        scores = head_scores(queries[:, cols], k_win[:, cols], mask_win, same_doc, bias_plane)
        row_max = jnp.max(scores, axis=-1, keepdims=True)
        exp_scores = jnp.exp(scores - row_max)
        row_total = jnp.sum(exp_scores, axis=-1, keepdims=True)
        log_parts.append(row_max + jnp.log(row_total))
        softmax_weights = (exp_scores / row_total).astype(jnp.bfloat16)
        mixed_parts.append(matmul(softmax_weights, v_win[:, cols]))
    attended = jnp.concatenate(mixed_parts, 1).astype(jnp.bfloat16)
    w_out = w_attn[:, 3 * inner_width :]
    after = residual + matmul_nt(attended, w_out)
    normed_ffn = rms_norm(after, norm_ffn).astype(jnp.bfloat16)
    gate_act = matmul(normed_ffn, w_gate)
    up_act = matmul(normed_ffn, w_up)
    activated = gated_unit(gate_act, up_act).astype(jnp.bfloat16)
    output = (after + matmul(activated, w_down)).astype(jnp.bfloat16)
    d_activated = matmul_nt(out_grad, w_down)
    d_down = matmul_tn(activated, out_grad)
    unit_out, unit_pull = jax.vjp(gated_unit, gate_act, up_act)
    d_gate_act, d_up_act = unit_pull(d_activated)
    d_gate_act = d_gate_act.astype(jnp.bfloat16)
    d_up_act = d_up_act.astype(jnp.bfloat16)
    d_normed_ffn = matmul_nt(d_gate_act, w_gate) + matmul_nt(d_up_act, w_up)
    d_w_gate = matmul_tn(normed_ffn, d_gate_act)
    d_w_up = matmul_tn(normed_ffn, d_up_act)
    norm_out, second_pull = jax.vjp(rms_norm, after, norm_ffn)
    d_after_part, d_norm_ffn = second_pull(d_normed_ffn)
    d_after = out_grad.astype(jnp.float32) + d_after_part
    d_after_low = d_after.astype(jnp.bfloat16)
    d_w_out = matmul_tn(d_after_low, attended)
    d_mixed = matmul(d_after_low, w_out).astype(jnp.bfloat16)
    dq_parts = []
    dk_parts = []
    dv_parts = []
    line_grads = []
    for head in range(head_count):
        cols = slice(head * head_width, (head + 1) * head_width)
        bias_plane = toeplitz(line_bias[:, head], row_count, window)
        scores = head_scores(queries[:, cols], k_win[:, cols], mask_win, same_doc, bias_plane)
        recomputed = jnp.exp(scores - log_parts[head])
        d_mix_head = d_mixed[:, cols]
        d_weights = matmul_nt(d_mix_head, v_win[:, cols])
        dv_parts.append(matmul_tn(recomputed.astype(jnp.bfloat16), d_mix_head))
        row_delta = jnp.sum(recomputed * d_weights, axis=-1, keepdims=True)
        d_scores = recomputed * (d_weights - row_delta)
        line_grads.append(diagonal_sums(d_scores, span_len))
        d_scores_low = d_scores.astype(jnp.bfloat16)
        dq_parts.append(matmul(d_scores_low, k_win[:, cols]))
        dk_parts.append(matmul_tn(d_scores_low, queries[:, cols]))
    d_queries = jnp.concatenate(dq_parts, 1)
    d_k_win = jnp.concatenate(dk_parts, 1)
    d_v_win = jnp.concatenate(dv_parts, 1)
    d_rel = lax.dot_general(
        line_onehot,
        jnp.stack(line_grads, 1),
        (((0,), (0,)), ((), ())),
        precision=lax.Precision.HIGHEST,
    )
    returned = [
        (
            d_k_win[slot * row_count : (slot + 1) * row_count],
            d_v_win[slot * row_count : (slot + 1) * row_count],
        )
        for slot in range(2 * reach_blocks + 1)
    ]
    d_keys = returned[reach_blocks][0]
    d_values = returned[reach_blocks][1]
    for direction in (1, -1):
        carried = (jnp.zeros_like(d_keys), jnp.zeros_like(d_values))
        for distance in range(reach_blocks, 0, -1):
            portion = returned[reach_blocks - direction * distance]
            carried = shifted(
                (shortened(carried[0] + portion[0]), shortened(carried[1] + portion[1])),
                "seq",
                -direction,
            )
        d_keys = d_keys + carried[0]
        d_values = d_values + carried[1]
    d_projected = jnp.concatenate([d_queries, d_keys, d_values], 1).astype(jnp.bfloat16)
    d_normed = matmul_nt(d_projected, w_attn[:, : 3 * inner_width])
    d_w_proj = matmul_tn(normed, d_projected)
    first_out, first_pull = jax.vjp(rms_norm, residual, norm_attn)
    d_resid_part, d_norm_attn = first_pull(d_normed)
    d_hidden = d_after + d_resid_part
    d_attn_full = jnp.concatenate([d_w_proj, d_w_out], 1)
    g_attn, g_gate, g_up, g_down = (
        lax.psum_scatter(d_attn_full, "seq", scatter_dimension=1, tiled=True),
        lax.psum_scatter(d_w_gate, "seq", scatter_dimension=1, tiled=True),
        lax.psum_scatter(d_w_up, "seq", scatter_dimension=1, tiled=True),
        lax.psum_scatter(d_down, "seq", scatter_dimension=0, tiled=True),
    )
    s_attn, s_ffn, s_rel = lax.psum((d_norm_attn, d_norm_ffn, d_rel), "seq")
    return (output, d_hidden, g_attn, g_gate, g_up, g_down, s_attn, s_ffn, s_rel)


def solution(mesh):
    placed = (
        P("seq", None), P("seq"), P("seq"), P(), P(None, "seq"), P(None, "seq"), P(None, "seq"), P("seq", None),
        P(), P(), P(), P("seq", None),
    )
    n = mesh.shape["seq"]
    body = functools.partial(shards, n) if n in GRIDS else plain_shards
    return jax.shard_map(
        body,
        mesh=mesh,
        in_specs=placed,
        out_specs=(
            P("seq", None), P("seq", None), P(None, "seq"), P(None, "seq"), P(None, "seq"), P("seq", None),
            P(), P(), P(),
        ),
        check_vma=False,
    )
```
